128 devices in a mesh: src: 16 (over x_lo, y, core), tgt: 8 (over x_hi, z).
Axes of the slice: x: 4 (x_hi: 2, x_lo: 2; x = x_hi * 2 + x_lo), y: 4, z: 4, core: 2. Of those that a mesh axis runs over, the one named last changes fastest.
Arguments:
- h_src: bfloat16 [8192, 768], P(('src', 'tgt')), may hold values from -6 to 6
- rel_table: bfloat16 [1387, 768], replicated, may hold values from -6 to 6
- cotangent: bfloat16 [4096, 768], P(('tgt', 'src')), may hold values from -6 to 6
- h_tgt: bfloat16 [4096, 768], P(('tgt', 'src')), may hold values from -6 to 6
- loop_rel: bfloat16 [768], replicated, may hold values from -6 to 6
- weights: bfloat16 [3, 768, 768], replicated, may hold values from -0.21875 to 0.21875
- src_index: int32 [16, 8, 16, 128], P('src', 'tgt'), may hold values from 0 to 511
- tgt_index: int32 [16, 8, 16, 128], P('src', 'tgt'), may hold values from 0 to 511
- rel_ids: int32 [16, 8, 16, 128], P('src', 'tgt'), may hold values from 0 to 1386
- direction: int32 [16, 8, 16, 128], P('src', 'tgt'), may hold values from 0 to 1
- counts: int32 [16, 8], P('src', 'tgt'), may hold values from 2 to 16, as said below
Outputs:
- grad_src: float32 [8192, 768], P(('src', 'tgt'))
- grad_tgt: float32 [4096, 768], P(('tgt', 'src'))
- grad_weights: float32 [3, 768, 768], replicated
- grad_rel: float32 [1387, 768], replicated
- grad_loop: float32 [768], replicated
The draws below stay inside these ranges and needn't reach their ends.
Inputs may be any that keep to these rules, and one draw needn't show every extreme that they name: `counts`: each device has 16, 8, 4 or 2 live tiles; some device has all 16.
All inputs are finite; a program needn't handle non-finite values.
Results may differ from the reference program's by a relative error of at most 0.0031.
Values may be sent and summed in bfloat16 or wider, within the bound.
A program may use at most 128 MiB of HBM per device.

```python
import jax
import jax.numpy as jnp
from jax import lax

D = 768
RELS = 1387
EDGE = 128
TILES = 16
SOURCES = 8192
TARGETS = 4096
SRC_PANEL = 512
TGT_PANEL = 512
EDGES_ALL = 262144
N_SRC = 16
N_TGT = 8


def draw_counts(key, part):
    key = jax.random.fold_in(key, 7)
    first, second = jax.random.split(key)
    shifts = jax.random.randint(first, (N_SRC * N_TGT,), 0, 4)
    levels = jnp.right_shift(jnp.full((N_SRC * N_TGT,), TILES, jnp.int32), shifts)
    chosen = jax.random.randint(second, (), 0, N_SRC * N_TGT)
    levels = jnp.where(jnp.arange(N_SRC * N_TGT) == chosen, TILES, levels)
    return levels.reshape(N_SRC, N_TGT).astype(jnp.int32)


def with_ends(values, rng, smallest, top_value):
    longest = values.shape.index(max(values.shape))
    spots = []
    for shift in (0, 1):
        where = [jax.random.randint(jax.random.fold_in(rng, axis), (), 0, length) for axis, length in enumerate(values.shape)]
        where[longest] = (where[longest] + shift) % values.shape[longest]
        spots.append(tuple(where))
    return values.at[spots[0]].set(smallest).at[spots[1]].set(top_value)


def shard_levels(key, shape, pieces, smallest, largest):
    def one(axis_at, blocks):
        heights = jax.random.uniform(jax.random.fold_in(jax.random.fold_in(key, 6), axis_at), (blocks,), jnp.float32, smallest / len(pieces), largest / len(pieces))
        return jnp.repeat(jnp.exp(heights), shape[axis_at] // blocks).reshape((-1,) + (1,) * (len(shape) - axis_at - 1))

    gain = one(*pieces[0])
    for cut in pieces[1:]:
        gain = gain * one(*cut)
    return gain


def centred(own_key, dims, spread, reach, cuts=(), kind=jnp.bfloat16):
    entries = spread * jax.random.normal(own_key, dims, jnp.float32)
    if cuts:
        entries = entries * shard_levels(own_key, dims, cuts, -0.22, 0.18)
    return jnp.clip(entries, -reach, reach).astype(kind)


def setup_inputs(seed: int = 0) -> dict:
    keys = jax.random.split(jax.random.key(seed), 12)
    return {
        "h_src": centred(keys[0], (SOURCES, D), 1.0, 6.0, ((0, 128),)),
        "rel_table": centred(keys[1], (RELS, D), 1.0, 6.0),
        "cotangent": centred(keys[2], (TARGETS, D), 1.0, 6.0, ((0, 128),)),
        "h_tgt": centred(keys[3], (TARGETS, D), 1.0, 6.0, ((0, 128),)),
        "loop_rel": centred(keys[4], (D,), 1.0, 6.0),
        "weights": centred(keys[5], (3, D, D), D ** -0.5, 0.21875),
        "src_index": with_ends(jax.random.randint(keys[6], (N_SRC, N_TGT, TILES, EDGE), 0, SRC_PANEL), jax.random.fold_in(keys[6], 1), 0, SRC_PANEL - 1).astype(jnp.int32),
        "tgt_index": with_ends(jax.random.randint(keys[7], (N_SRC, N_TGT, TILES, EDGE), 0, TGT_PANEL), jax.random.fold_in(keys[7], 1), 0, TGT_PANEL - 1).astype(jnp.int32),
        "rel_ids": with_ends(jax.random.randint(keys[8], (N_SRC, N_TGT, TILES, EDGE), 0, RELS), jax.random.fold_in(keys[8], 1), 0, RELS - 1).astype(jnp.int32),
        "direction": with_ends(jax.random.randint(keys[9], (N_SRC, N_TGT, TILES, EDGE), 0, 2), jax.random.fold_in(keys[9], 1), 0, 1).astype(jnp.int32),
        "counts": draw_counts(jax.random.fold_in(keys[11], 71), 0),
    }


def reference(h_src, rel_table, cotangent, h_tgt, loop_rel, weights, src_index, tgt_index, rel_ids, direction, counts):
    w_cat = jnp.concatenate([weights[0], weights[1]], axis=1)
    rel_wide = rel_table.astype(jnp.float32)
    slots = TILES * EDGE
    zero_rows = jnp.zeros((slots, D), jnp.bfloat16)

    def device(carry, index):
        acc_src, acc_w, acc_rel = carry
        first = index // N_TGT
        second = index % N_TGT
        source = src_index[first, second].reshape(slots).astype(jnp.int32) + first * SRC_PANEL
        target = tgt_index[first, second].reshape(slots).astype(jnp.int32) + second * TGT_PANEL
        relation = rel_ids[first, second].reshape(slots).astype(jnp.int32)
        flags = direction[first, second].reshape(slots)
        live = (jnp.arange(slots) // EDGE) < counts[first, second]
        h_rows = jnp.take(h_src, source, axis=0).astype(jnp.float32)
        z_rows = jnp.take(rel_wide, relation, axis=0)
        comp = (h_rows * z_rows).astype(jnp.bfloat16)
        g_rows = jnp.take(cotangent, target, axis=0)
        g_in = jnp.where((live & (flags == 0))[:, None], g_rows, zero_rows)
        g_out = jnp.where((live & (flags == 1))[:, None], g_rows, zero_rows)
        g_cat = jnp.concatenate([g_in, g_out], axis=1)
        dcomp = lax.dot_general(g_cat, w_cat, (((1,), (1,)), ((), ())), preferred_element_type=jnp.float32)
        acc_w = acc_w + lax.dot_general(comp, g_cat, (((0,), (0,)), ((), ())), preferred_element_type=jnp.float32)
        acc_src = acc_src.at[source].add(dcomp * z_rows)
        acc_rel = acc_rel.at[relation].add(dcomp * h_rows)
        return (acc_src, acc_w, acc_rel), None

    init = (jnp.zeros((SOURCES, D), jnp.float32), jnp.zeros((D, 2 * D), jnp.float32), jnp.zeros((RELS, D), jnp.float32))
    (grad_src, wsum, rsum), _ = lax.scan(device, init, jnp.arange(N_SRC * N_TGT, dtype=jnp.int32))
    loop_wide = loop_rel.astype(jnp.float32)
    back = lax.dot_general(cotangent, weights[2], (((1,), (1,)), ((), ())), preferred_element_type=jnp.float32)
    grad_tgt = back * loop_wide[None, :]
    self_comp = (h_tgt.astype(jnp.float32) * loop_wide[None, :]).astype(jnp.bfloat16)
    wself = lax.dot_general(self_comp, cotangent, (((0,), (0,)), ((), ())), preferred_element_type=jnp.float32)
    lsum = jnp.sum(back * h_tgt.astype(jnp.float32), axis=0)
    edge_scale = float(EDGES_ALL) ** -0.5
    self_scale = float(TARGETS) ** -0.5
    grad_weights = jnp.stack([wsum[:, :D] * edge_scale, wsum[:, D:] * edge_scale, wself * self_scale])
    grad_rel = rsum * (float(RELS) / float(EDGES_ALL)) ** 0.5
    grad_loop = lsum * self_scale
    return grad_src, grad_tgt, grad_weights, grad_rel, grad_loop
```

```python
import functools

import jax
import jax.numpy as jnp
from jax import lax
from jax.experimental import pallas as pl
from jax.experimental.pallas import tpu as pltpu
from jax.sharding import PartitionSpec as P

F32 = jnp.float32
BF16 = jnp.bfloat16
MESH = pl.DeviceIdType.MESH
ANY = pl.BlockSpec(memory_space=pl.ANY)
VMEM = pl.BlockSpec(memory_space=pltpu.VMEM)
SMEM = pl.BlockSpec(memory_space=pltpu.SMEM)
DMA = pltpu.SemaphoreType.DMA

HALF_BLOCKS = 116
HALF_ROWS = 11264
W_BLOCKS = 144
PARTS = ((("x", "y", "z"), 64), (("y", "z", "x"), 64), (("z", "x", "y"), 48))
BASES = (0, 4096, 8192)
UNROLL = 8


class Place:
    def __init__(self):
        s, t = lax.axis_index("src"), lax.axis_index("tgt")
        self.x_lo, self.core = s // 8, s % 2
        self.x_hi = t // 4
        self.at = {"x": self.x_hi * 2 + self.x_lo, "y": (s // 2) % 4, "z": t % 4}

    def device(self, at, core):
        return ((at["x"] % 2) * 8 + at["y"] * 2 + core, (at["x"] // 2) * 4 + at["z"])

    def along(self, axis, offset):
        at = dict(self.at)
        at[axis] = (at[axis] + offset) % 4
        return self.device(at, self.core)

    def sibling(self):
        return self.device(self.at, 1 - self.core)

    def x_lo_partner(self):
        at = dict(self.at)
        at["x"] = self.x_hi * 2 + (1 - self.x_lo)
        return self.device(at, self.core)


def greet(partners):
    barrier = pltpu.get_barrier_semaphore()
    for partner in partners:
        pl.semaphore_signal(barrier, inc=1, device_id=partner, device_id_type=MESH)
    pl.semaphore_wait(barrier, len(partners))


def push(src, dst, send, recv, device):
    return pltpu.make_async_remote_copy(
        src_ref=src, dst_ref=dst, send_sem=send, recv_sem=recv, device_id=device, device_id_type=MESH
    )


def gather_kernel(
    h_ref, c_ref, h_all, c_all, local, hx_s, hx_r, hz_s, hz_r, cy_s, cy_r, cx_s, cx_r, cs_s, cs_r
):
    me = Place()
    x_lo, x_hi, core, y, z = me.x_lo, me.x_hi, me.core, me.at["y"], me.at["z"]
    sibling, across = me.sibling(), me.x_lo_partner()
    own_h = pltpu.make_async_copy(h_ref, h_all.at[x_hi, z], local.at[0])
    own_c = pltpu.make_async_copy(c_ref, c_all.at[x_lo, y, core], local.at[1])
    own_h.start()
    own_c.start()
    greet(
        [me.along("x", 2), across, sibling]
        + [me.along("y", k) for k in (1, 2, 3)]
        + [me.along("z", k) for k in (1, 2, 3)]
    )
    hx = push(h_ref, h_all.at[x_hi, z], hx_s, hx_r, me.along("x", 2))
    hx.start()
    cy = []
    for k in (1, 2, 3):
        copy = push(c_ref, c_all.at[x_lo, y, core], cy_s.at[k - 1], cy_r.at[k - 1], me.along("y", k))
        copy.start()
        cy.append(copy)
    own_h.wait()
    own_c.wait()
    hx.wait()
    hz = []
    for k in (1, 2, 3):
        copy = push(h_all.at[:, z], h_all.at[:, z], hz_s.at[k - 1], hz_r.at[k - 1], me.along("z", k))
        copy.start()
        hz.append(copy)
    for copy in cy:
        copy.wait()
    mine = c_all.at[x_lo, :, core]
    theirs = c_all.at[1 - x_lo, :, core]
    cx = push(mine, mine, cx_s, cx_r, across)
    cx.start()
    first = push(mine, mine, cs_s.at[0], cs_r.at[0], sibling)
    first.start()
    cx.wait()
    second = push(theirs, theirs, cs_s.at[1], cs_r.at[1], sibling)
    second.start()
    first.wait()
    second.wait()
    for copy in hz:
        copy.wait()


def gather(h_src, cotangent):
    rows, width = h_src.shape
    trows = cotangent.shape[0]
    h_all, c_all = pl.pallas_call(
        gather_kernel,
        out_shape=(
            jax.ShapeDtypeStruct((2, 4, rows, width), BF16),
            jax.ShapeDtypeStruct((2, 4, 2, trows, width), BF16),
        ),
        in_specs=[ANY] * 2,
        out_specs=[ANY] * 2,
        scratch_shapes=[
            DMA((2,)), DMA, DMA, DMA((3,)), DMA((3,)), DMA((3,)), DMA((3,)), DMA, DMA, DMA((2,)), DMA((2,)),
        ],
        compiler_params=pltpu.CompilerParams(collective_id=0, has_side_effects=True),
        name="gather_panels",
    )(h_src, cotangent)
    return h_all.reshape(8 * rows, width), c_all.reshape(16 * trows, width)


def edge_kernel(
    live_ref, src_ref, tgt_ref, rel_ref, h_ref, c_ref, w_ref, z_ref, own_c, own_h, loop_ref,
    g_out, t_out, keep, give, hx, px, zx, gs, aa, rr, hi, lo,
):
    core = lax.axis_index("src") % 2
    rows = h_ref.shape[0]
    trows = c_ref.shape[0]
    rels, width = z_ref.shape
    chunks = width // 128

    def spread(dst, row, value):
        for c in range(chunks):
            dst[pl.ds(row * 8 + c, value.shape[0], stride=8), :] = value[:, c * 128 : (c + 1) * 128]

    def put(half, row, tile):
        @pl.when(core == half)
        def _():
            keep[pl.ds(row, 16), :] = tile

        @pl.when(core != half)
        def _():
            give[pl.ds(row, 16), :] = tile.astype(BF16)

    def put_blocks(block, value):
        for half in range(2):
            first = max(block, half * HALF_BLOCKS)
            last = min(block + value.shape[0] // 16, (half + 1) * HALF_BLOCKS)
            if first >= last:
                continue

            def store(ref, half=half, first=first, last=last):
                for b in range(first, last):
                    for c in range(chunks):
                        row = ((b - half * HALF_BLOCKS) * chunks + c) * 16
                        part = value[(b - block) * 16 : (b - block + 1) * 16, c * 128 : (c + 1) * 128]
                        ref[row : row + 16, :] = part.astype(ref.dtype)

            @pl.when(core == half)
            def _(store=store):
                store(keep)

            @pl.when(core != half)
            def _(store=store):
                store(give)

    @pl.loop(0, rows // 16)
    def _(i):
        r = pl.multiple_of(i * 16, 16)
        spread(hx, r, h_ref[pl.ds(r, 16), :].astype(F32))

    @pl.loop(0, rels // 16)
    def _(i):
        r = pl.multiple_of(i * 16, 16)
        spread(zx, r, z_ref[pl.ds(r, 16), :].astype(F32))

    tail = rels // 16 * 16
    if tail < rels:
        spread(zx, tail, z_ref[tail:rels, :].astype(F32))
    for d in range(2):
        for k in range(width // 256):
            p = lax.dot_general(
                c_ref[...], w_ref[d, k * 256 : (k + 1) * 256, :], (((1,), (1,)), ((), ())),
                preferred_element_type=F32,
            )
            for h in range(2):
                px[pl.ds(d * trows * 8 + 2 * k + h, trows, stride=8), :] = p[:, h * 128 : (h + 1) * 128]
    zero = jnp.zeros((64, 128), F32)
    for ref in (gs, aa, rr):

        @pl.loop(0, ref.shape[0] // 64)
        def _(i, ref=ref):
            ref[pl.ds(pl.multiple_of(i * 64, 64), 64), :] = zero

    @pl.loop(0, live_ref[0])
    def _(i):
        for u in range(UNROLL):
            e = i * UNROLL + u
            s = pl.ds(pl.multiple_of(src_ref[e], 8), 8)
            t = pl.ds(pl.multiple_of(tgt_ref[e], 8), 8)
            r = pl.ds(pl.multiple_of(rel_ref[e], 8), 8)
            h = hx[s, :]
            p = px[t, :]
            z = zx[r, :]
            gs[s, :] += p * z
            aa[t, :] += (h * z).astype(BF16).astype(F32)
            rr[r, :] += p * h

    loop_wide = loop_ref[...].astype(F32)
    h_wide = own_h[...].astype(F32)
    back = lax.dot_general(
        own_c[...], w_ref[2], (((1,), (1,)), ((), ())), preferred_element_type=F32
    )
    t_out[...] = back * loop_wide
    lsum = jnp.sum(back * h_wide, axis=0, keepdims=True)
    for c in range(chunks):
        rr[rels * 8 + c : rels * 8 + c + 1, :] = lsum[:, c * 128 : (c + 1) * 128]
    self_comp = (h_wide * loop_wide).astype(BF16)
    for k in range(width // 256):
        wself = lax.dot_general(
            self_comp[:, k * 256 : (k + 1) * 256], own_c[...], (((0,), (0,)), ((), ())),
            preferred_element_type=F32,
        )
        put_blocks(96 + k * 16, wself)

    @pl.loop(0, rows // 16)
    def _(i):
        r = pl.multiple_of(i * 16, 16)
        for c in range(chunks):
            g_out[pl.ds(r, 16), c * 128 : (c + 1) * 128] = gs[pl.ds(r * 8 + c, 16, stride=8), :].astype(BF16)

    @pl.loop(0, 2 * trows // 16)
    def _(i):
        r = pl.multiple_of(i * 16, 16)
        for c in range(chunks):
            a = aa[pl.ds(r * 8 + c, 16, stride=8), :]
            top = a.astype(BF16)
            hi[pl.ds(r, 16), c * 128 : (c + 1) * 128] = top
            lo[pl.ds(r, 16), c * 128 : (c + 1) * 128] = (a - top.astype(F32)).astype(BF16)

    for d in range(2):
        at = slice(d * trows, (d + 1) * trows)
        for k in range(width // 256):
            cols = slice(k * 256, (k + 1) * 256)
            w = lax.dot_general(
                hi[at, cols], c_ref[...], (((0,), (0,)), ((), ())), preferred_element_type=F32
            ) + lax.dot_general(
                lo[at, cols], c_ref[...], (((0,), (0,)), ((), ())), preferred_element_type=F32
            )
            put_blocks(d * 48 + k * 16, w)

    rel_base = (W_BLOCKS - HALF_BLOCKS) * chunks * 16

    @pl.loop(0, rr.shape[0] // 128)
    def _(i):
        for c in range(chunks):
            put(
                1,
                pl.multiple_of(rel_base + (i * chunks + c) * 16, 16),
                rr[pl.ds(i * 128 + c, 16, stride=8), :],
            )

    low = rel_base + rr.shape[0] // 128 * chunks * 16
    high = HALF_BLOCKS * chunks * 16
    for half, end in ((0, high), (1, low)):

        @pl.when(core == half)
        def _(end=end):
            keep[end:, :] = jnp.zeros((HALF_ROWS - end, 128), F32)

        @pl.when(core != half)
        def _(end=end):
            give[end:, :] = jnp.zeros((HALF_ROWS - end, 128), BF16)


def edges(live, s8, t8, r8, h, c, w, z, own_c, own_h, loop):
    rows, width = h.shape
    trows = c.shape[0]
    rpad = (z.shape[0] + 16) // 16 * 16
    return pl.pallas_call(
        edge_kernel,
        out_shape=(
            jax.ShapeDtypeStruct((rows, width), BF16),
            jax.ShapeDtypeStruct((own_c.shape[0], width), F32),
            jax.ShapeDtypeStruct((HALF_ROWS, 128), F32),
            jax.ShapeDtypeStruct((HALF_ROWS, 128), BF16),
        ),
        in_specs=[SMEM] * 4 + [VMEM] * 7,
        out_specs=[VMEM] * 4,
        scratch_shapes=[
            pltpu.VMEM((rows * 8, 128), F32),
            pltpu.VMEM((2 * trows * 8, 128), F32),
            pltpu.VMEM((rpad * 8, 128), F32),
            pltpu.VMEM((rows * 8, 128), F32),
            pltpu.VMEM((2 * trows * 8, 128), F32),
            pltpu.VMEM((rpad * 8, 128), F32),
            pltpu.VMEM((2 * trows, width), BF16),
            pltpu.VMEM((2 * trows, width), BF16),
        ],
        compiler_params=pltpu.CompilerParams(vmem_limit_bytes=58 * 2**20),
        name="edges",
    )(live, s8, t8, r8, h, c, w, z, own_c, own_h, loop)


def reduce_kernel(
    keep, give, g_ref, full, g_out,
    pair, out1, in1, acc1, in2, acc2, in3, unit, g_in, g_acc, g_side,
    pair_s, pair_r, s1, r1, s2, r2, s3, r3, s4, r4, s5, r5, s6, r6, sib_s, sib_r, gz_s, gz_r, gx_s, gx_r,
    local,
):
    me = Place()
    core = me.core
    sibling = me.sibling()
    x_hi, z = me.x_hi, me.at["z"]
    greet([me.along(axis, k) for axis in ("x", "y", "z") for k in (1, 2, 3)] + [sibling])

    sent = []
    gz = []
    for k in (1, 2, 3):
        copy = push(
            g_ref.at[:, (z + k) % 4], g_in.at[k - 1], gz_s.at[k - 1], gz_r.at[k - 1], me.along("z", k)
        )
        copy.start()
        gz.append(copy)

    def rows_of(p, a):
        size = PARTS[p][1] * 16
        return pl.ds(pl.multiple_of(BASES[p] + a * size, 16), size)

    def first(p):
        return me.at[PARTS[p][0][0]]

    def second(p):
        return me.at[PARTS[p][0][1]]

    def third(p):
        return me.at[PARTS[p][0][2]]

    pairs = {}
    for j in (1, 2, 3, 0):
        for p in range(3):
            where = rows_of(p, (first(p) + j) % 4)
            copy = push(give.at[where], pair.at[where], pair_s.at[p * 4 + j], pair_r.at[p * 4 + j], sibling)
            copy.start()
            pairs[p, j] = copy

    step1 = {}
    for j in (1, 2, 3):
        for p in range(3):
            axis, unit_rows = PARTS[p][0][0], PARTS[p][1]
            base = BASES[p] + ((first(p) + j) % 4) * (unit_rows * 16)
            pairs[p, j].wait_recv()

            @pl.loop(0, unit_rows * 16 // 128)
            def _(i, base=base):
                r = pl.ds(pl.multiple_of(base + i * 128, 16), 128)
                out1[r, :] = (keep[r, :] + pair[r, :].astype(F32)).astype(BF16)

            where = rows_of(p, (first(p) + j) % 4)
            copy = push(
                out1.at[where],
                in1.at[j - 1, pl.ds(BASES[p] // 4, unit_rows * 16)],
                s1.at[p * 3 + j - 1],
                r1.at[p * 3 + j - 1],
                me.along(axis, j),
            )
            copy.start()
            step1[p, j] = copy

    for copy in gz:
        copy.wait_recv()
    for half in range(2):
        g_acc[half] = (
            g_ref[half, z].astype(F32)
            + g_in[0, half].astype(F32)
            + g_in[1, half].astype(F32)
            + g_in[2, half].astype(F32)
        )
    gx = push(g_acc.at[1 - x_hi], g_side, gx_s, gx_r, me.along("x", 2))
    gx.start()

    step2 = {}
    for p in range(3):
        axis, unit_rows = PARTS[p][0][1], PARTS[p][1]
        base = BASES[p] + first(p) * (unit_rows * 16)
        low = BASES[p] // 4
        pairs[p, 0].wait_recv()
        for j in (1, 2, 3):
            step1[p, j].wait_recv()

        @pl.loop(0, unit_rows * 16 // 128)
        def _(i, base=base, low=low):
            r = pl.ds(pl.multiple_of(base + i * 128, 16), 128)
            q = pl.ds(pl.multiple_of(low + i * 128, 16), 128)
            acc1[q, :] = (
                keep[r, :]
                + pair[r, :].astype(F32)
                + in1[0, q, :].astype(F32)
                + in1[1, q, :].astype(F32)
                + in1[2, q, :].astype(F32)
            )

        for j in (1, 2, 3):
            where = pl.ds(pl.multiple_of(low + ((second(p) + j) % 4) * (unit_rows * 4), 16), unit_rows * 4)
            copy = push(
                acc1.at[where],
                in2.at[j - 1, pl.ds(BASES[p] // 16, unit_rows * 4)],
                s2.at[p * 3 + j - 1],
                r2.at[p * 3 + j - 1],
                me.along(axis, j),
            )
            copy.start()
            step2[p, j] = copy

    step3 = {}
    for p in range(3):
        axis, unit_rows = PARTS[p][0][2], PARTS[p][1]
        for j in (1, 2, 3):
            step2[p, j].wait_recv()
        size = unit_rows * 4
        q = pl.ds(BASES[p] // 16, size)
        mine = pl.ds(pl.multiple_of(BASES[p] // 4 + second(p) * size, 16), size)
        acc2[q, :] = acc1[mine, :] + in2[0, q, :] + in2[1, q, :] + in2[2, q, :]
        for j in (1, 2, 3):
            where = pl.ds(
                pl.multiple_of(BASES[p] // 16 + ((third(p) + j) % 4) * unit_rows, 16), unit_rows
            )
            copy = push(
                acc2.at[where],
                in3.at[j - 1, pl.ds(BASES[p] // 64, unit_rows)],
                s3.at[p * 3 + j - 1],
                r3.at[p * 3 + j - 1],
                me.along(axis, j),
            )
            copy.start()
            step3[p, j] = copy

    def place(p, depth):
        unit_rows = PARTS[p][1]
        row = core * HALF_ROWS + BASES[p] + first(p) * (unit_rows * 16)
        if depth > 1:
            row = row + second(p) * (unit_rows * 4)
        if depth > 2:
            row = row + third(p) * unit_rows
        size = (unit_rows * 16, unit_rows * 4, unit_rows)[depth - 1]
        return pl.ds(pl.multiple_of(row, 16), size)

    step4, own = {}, {}
    for p in range(3):
        axis, unit_rows = PARTS[p][0][2], PARTS[p][1]
        for j in (1, 2, 3):
            step3[p, j].wait_recv()
        q = pl.ds(BASES[p] // 64, unit_rows)
        mine = pl.ds(pl.multiple_of(BASES[p] // 16 + third(p) * unit_rows, 16), unit_rows)
        unit[q, :] = (acc2[mine, :] + in3[0, q, :] + in3[1, q, :] + in3[2, q, :]).astype(BF16)
        own[p] = pltpu.make_async_copy(unit.at[q], full.at[place(p, 3)], local.at[p])
        own[p].start()
        for j in (1, 2, 3):
            copy = push(
                unit.at[q], full.at[place(p, 3)], s4.at[p * 3 + j - 1], r4.at[p * 3 + j - 1], me.along(axis, j)
            )
            copy.start()
            step4[p, j] = copy

    step5 = {}
    for p in range(3):
        own[p].wait()
        for j in (1, 2, 3):
            step4[p, j].wait_recv()
        for j in (1, 2, 3):
            block = full.at[place(p, 2)]
            copy = push(block, block, s5.at[p * 3 + j - 1], r5.at[p * 3 + j - 1], me.along(PARTS[p][0][1], j))
            copy.start()
            step5[p, j] = copy

    step6, side = {}, {}
    for p in range(3):
        for j in (1, 2, 3):
            step5[p, j].wait_recv()
        block = full.at[place(p, 1)]
        for j in (1, 2, 3):
            copy = push(block, block, s6.at[p * 3 + j - 1], r6.at[p * 3 + j - 1], me.along(PARTS[p][0][0], j))
            copy.start()
            step6[p, j] = copy
        side[p, 0] = push(block, block, sib_s.at[p * 4], sib_r.at[p * 4], sibling)
        side[p, 0].start()

    gx.wait_recv()
    g_out[...] = g_acc[x_hi] + g_side[...]

    for j in (1, 3, 2):
        for p in range(3):
            size = PARTS[p][1] * 16
            step6[p, j].wait_recv()
            row = core * HALF_ROWS + BASES[p] + ((first(p) + 4 - j) % 4) * size
            block = full.at[pl.ds(pl.multiple_of(row, 16), size)]
            side[p, j] = push(block, block, sib_s.at[p * 4 + j], sib_r.at[p * 4 + j], sibling)
            side[p, j].start()

    for copy in side.values():
        copy.wait_recv()
    gx.wait_send()
    for group in (gz, pairs.values(), step1.values(), step2.values(), step3.values(), step4.values()):
        for copy in group:
            copy.wait_send()
    for group in (step5.values(), step6.values(), side.values()):
        for copy in group:
            copy.wait_send()


def reduce_all(keep, give, g):
    rows, width = g.shape
    g = g.reshape(2, 4, rows // 8, width)
    return pl.pallas_call(
        reduce_kernel,
        out_shape=(
            jax.ShapeDtypeStruct((2 * HALF_ROWS, 128), BF16),
            jax.ShapeDtypeStruct((rows // 8, width), F32),
        ),
        in_specs=[VMEM, ANY, VMEM],
        out_specs=[ANY, VMEM],
        scratch_shapes=[
            pltpu.VMEM((HALF_ROWS, 128), BF16),
            pltpu.VMEM((HALF_ROWS, 128), BF16),
            pltpu.VMEM((3, HALF_ROWS // 4, 128), BF16),
            pltpu.VMEM((HALF_ROWS // 4, 128), F32),
            pltpu.VMEM((3, HALF_ROWS // 16, 128), F32),
            pltpu.VMEM((HALF_ROWS // 16, 128), F32),
            pltpu.VMEM((3, HALF_ROWS // 64, 128), F32),
            pltpu.VMEM((HALF_ROWS // 64, 128), BF16),
            pltpu.VMEM((3, 2, rows // 8, width), BF16),
            pltpu.VMEM((2, rows // 8, width), F32),
            pltpu.VMEM((rows // 8, width), F32),
            DMA((12,)), DMA((12,)),
            *[DMA((9,)) for _ in range(12)],
            DMA((12,)), DMA((12,)), DMA((3,)), DMA((3,)), DMA, DMA, DMA((3,)),
        ],
        compiler_params=pltpu.CompilerParams(
            collective_id=1, has_side_effects=True, vmem_limit_bytes=48 * 2**20
        ),
        name="reduce_all",
    )(keep, give, g)


def unpack_kernel(full, w_out, r_out, l_out, *, edge_scale, self_scale, rel_scale):
    rels, width = r_out.shape
    chunks = width // 128
    per = width // 16

    def tile(block, c):
        half = block // HALF_BLOCKS
        row = half * HALF_ROWS + ((block - half * HALF_BLOCKS) * chunks + c) * 16
        return full[pl.ds(pl.multiple_of(row, 16), 16), :].astype(F32)

    for d, scale in enumerate((edge_scale, edge_scale, self_scale)):

        @pl.loop(0, per)
        def _(i, d=d, scale=scale):
            for c in range(chunks):
                w_out[d, pl.ds(pl.multiple_of(i * 16, 16), 16), c * 128 : (c + 1) * 128] = (
                    tile(d * per + i, c) * scale
                )

    whole = rels // 16

    @pl.loop(0, whole)
    def _(i):
        for c in range(chunks):
            r_out[pl.ds(pl.multiple_of(i * 16, 16), 16), c * 128 : (c + 1) * 128] = (
                tile(W_BLOCKS + i, c) * rel_scale
            )

    rest = rels - whole * 16
    for c in range(chunks):
        last = tile(W_BLOCKS + whole, c)
        cols = slice(c * 128, (c + 1) * 128)
        if rest:
            r_out[whole * 16 : rels, cols] = last[:rest] * rel_scale
        l_out[:, cols] = last[rest : rest + 1] * self_scale


def unpack(full, rels, width, **scales):
    return pl.pallas_call(
        functools.partial(unpack_kernel, **scales),
        out_shape=(
            jax.ShapeDtypeStruct((3, width, width), F32),
            jax.ShapeDtypeStruct((rels, width), F32),
            jax.ShapeDtypeStruct((1, width), F32),
        ),
        in_specs=[VMEM],
        out_specs=[VMEM] * 3,
        compiler_params=pltpu.CompilerParams(vmem_limit_bytes=48 * 2**20),
        name="unpack",
    )(full)


def body(
    h_src, rel_table, cotangent, h_tgt, loop_rel, weights, src_index, tgt_index, rel_ids, direction, counts
):
    width = weights.shape[1]
    tiles, edge = src_index.shape[2:]
    rels = rel_table.shape[0]
    h_all, c_all = gather(h_src, cotangent)
    trows = c_all.shape[0]
    live = (counts * (edge // UNROLL)).reshape(1)
    s8 = (src_index * 8).reshape(tiles * edge)
    t8 = ((tgt_index + direction * trows) * 8).reshape(tiles * edge)
    r8 = (rel_ids * 8).reshape(tiles * edge)
    g, grad_tgt, keep, give = edges(
        live, s8, t8, r8, h_all, c_all, weights, rel_table, cotangent, h_tgt, loop_rel.reshape(1, width)
    )
    full, grad_src = reduce_all(keep, give, g)
    devices = lax.axis_size("src") * lax.axis_size("tgt")
    edges_all = float(devices * tiles * edge)
    targets_all = float(devices * cotangent.shape[0])
    grad_weights, grad_rel, grad_loop = unpack(
        full,
        rels,
        width,
        edge_scale=edges_all**-0.5,
        self_scale=targets_all**-0.5,
        rel_scale=(float(rels) / edges_all) ** 0.5,
    )
    return grad_src, grad_tgt, grad_weights, grad_rel, grad_loop.reshape(width)


def solution(mesh):
    return jax.shard_map(
        body,
        mesh=mesh,
        in_specs=(
            P(("src", "tgt"), None),
            P(),
            P(("tgt", "src"), None),
            P(("tgt", "src"), None),
            P(),
            P(),
            P("src", "tgt", None, None),
            P("src", "tgt", None, None),
            P("src", "tgt", None, None),
            P("src", "tgt", None, None),
            P("src", "tgt"),
        ),
        out_specs=(P(("src", "tgt"), None), P(("tgt", "src"), None), P(), P(), P()),
        check_vma=False,
    )
```

```python
import functools

import jax
import jax.numpy as jnp
from jax import lax
from jax.experimental import pallas as pl
from jax.experimental.pallas import tpu as pltpu
from jax.sharding import PartitionSpec as P

F32 = jnp.float32
BF16 = jnp.bfloat16
MESH = pl.DeviceIdType.MESH
ANY = pl.BlockSpec(memory_space=pl.ANY)
VMEM = pl.BlockSpec(memory_space=pltpu.VMEM)
SMEM = pl.BlockSpec(memory_space=pltpu.SMEM)
DMA = pltpu.SemaphoreType.DMA

HALF_BLOCKS = 116
HALF_ROWS = 11264
W_BLOCKS = 144
PARTS = ((("x", "y", "z"), 64), (("y", "z", "x"), 64), (("z", "x", "y"), 48))
BASES = (0, 4096, 8192)
UNROLL = 16
VMEM_BYTES = 63 * 2**20


class Place:
    def __init__(self):
        s, t = lax.axis_index("src"), lax.axis_index("tgt")
        self.x_lo, self.core = s // 8, s % 2
        self.x_hi = t // 4
        self.at = {"x": self.x_hi * 2 + self.x_lo, "y": (s // 2) % 4, "z": t % 4}

    def device(self, at, core):
        return ((at["x"] % 2) * 8 + at["y"] * 2 + core, (at["x"] // 2) * 4 + at["z"])

    def along(self, axis, offset):
        at = dict(self.at)
        at[axis] = (at[axis] + offset) % 4
        return self.device(at, self.core)

    def sibling(self):
        return self.device(self.at, 1 - self.core)

    def x_lo_partner(self):
        at = dict(self.at)
        at["x"] = self.x_hi * 2 + (1 - self.x_lo)
        return self.device(at, self.core)


def greet(partners):
    barrier = pltpu.get_barrier_semaphore()
    for partner in partners:
        pl.semaphore_signal(barrier, inc=1, device_id=partner, device_id_type=MESH)
    pl.semaphore_wait(barrier, len(partners))


def push(src, dst, send, recv, device):
    return pltpu.make_async_remote_copy(
        src_ref=src, dst_ref=dst, send_sem=send, recv_sem=recv, device_id=device, device_id_type=MESH
    )


def gather_kernel(
    h_ref, c_ref, src_ref, tgt_ref, rel_ref, dir_ref, h_all, c_all, s8, t8, r8, local, hx_s, hx_r, hz_s, hz_r, cy_s, cy_r, cx_s, cx_r, cs_s, cs_r
):
    me = Place()
    x_lo, x_hi, core, y, z = me.x_lo, me.x_hi, me.core, me.at["y"], me.at["z"]
    sibling, across = me.sibling(), me.x_lo_partner()
    own_h = pltpu.make_async_copy(h_ref, h_all.at[x_hi, z], local.at[0])
    own_c = pltpu.make_async_copy(c_ref, c_all.at[x_lo, y, core], local.at[1])
    own_h.start()
    own_c.start()
    s8[...] = src_ref[...] * 8
    t8[...] = (tgt_ref[...] + dir_ref[...] * (16 * c_ref.shape[0])) * 8
    r8[...] = rel_ref[...] * 8
    greet(
        [me.along("x", 2), across, sibling]
        + [me.along("y", k) for k in (1, 2, 3)]
        + [me.along("z", k) for k in (1, 2, 3)]
    )
    hx = push(h_ref, h_all.at[x_hi, z], hx_s, hx_r, me.along("x", 2))
    hx.start()
    cy = []
    for k in (1, 2, 3):
        copy = push(c_ref, c_all.at[x_lo, y, core], cy_s.at[k - 1], cy_r.at[k - 1], me.along("y", k))
        copy.start()
        cy.append(copy)
    own_h.wait()
    own_c.wait()
    hx.wait()
    hz = []
    for k in (1, 2, 3):
        copy = push(h_all.at[:, z], h_all.at[:, z], hz_s.at[k - 1], hz_r.at[k - 1], me.along("z", k))
        copy.start()
        hz.append(copy)
    for copy in cy:
        copy.wait()
    mine = c_all.at[x_lo, :, core]
    theirs = c_all.at[1 - x_lo, :, core]
    cx = push(mine, mine, cx_s, cx_r, across)
    cx.start()
    first = push(mine, mine, cs_s.at[0], cs_r.at[0], sibling)
    first.start()
    cx.wait()
    second = push(theirs, theirs, cs_s.at[1], cs_r.at[1], sibling)
    second.start()
    first.wait()
    second.wait()
    for copy in hz:
        copy.wait()


def gather(h_src, cotangent, *indices):
    rows, width = h_src.shape
    trows = cotangent.shape[0]
    h_all, c_all, s8, t8, r8 = pl.pallas_call(
        gather_kernel,
        out_shape=(
            jax.ShapeDtypeStruct((2, 4, rows, width), BF16),
            jax.ShapeDtypeStruct((2, 4, 2, trows, width), BF16),
            *[jax.ShapeDtypeStruct(indices[0].shape, jnp.int32)] * 3,
        ),
        in_specs=[ANY] * 2 + [VMEM] * 4,
        out_specs=[ANY] * 2 + [VMEM] * 3,
        scratch_shapes=[
            DMA((2,)), DMA, DMA, DMA((3,)), DMA((3,)), DMA((3,)), DMA((3,)), DMA, DMA, DMA((2,)), DMA((2,)),
        ],
        compiler_params=pltpu.CompilerParams(collective_id=0, has_side_effects=True, vmem_limit_bytes=VMEM_BYTES),
        name="gather_panels",
    )(h_src, cotangent, *indices)
    return h_all.reshape(8 * rows, width), c_all.reshape(16 * trows, width), s8, t8, r8


def edge_kernel(
    live_ref, src_ref, tgt_ref, rel_ref, h_hbm, c_hbm, w_hbm, z_hbm, own_c, own_h, loop_ref,
    g_out, t_out, keep_out, give_out,
    h_ref, c_ref, w_ref, z_ref, g_ref, keep, give, hx, px, zx, gs, aa, rr, hi, lo, in_sem, out_sem,
):
    loads = [
        pltpu.make_async_copy(a, b, in_sem.at[i])
        for i, (a, b) in enumerate(((h_hbm, h_ref), (z_hbm, z_ref), (c_hbm, c_ref), (w_hbm, w_ref)))
    ]
    for load in loads:
        load.start()
    core = lax.axis_index("src") % 2
    rows = h_ref.shape[0]
    trows = c_ref.shape[0]
    rels, width = z_ref.shape
    chunks = width // 128

    def spread(dst, row, value):
        for c in range(chunks):
            dst[pl.ds(row * 8 + c, value.shape[0], stride=8), :] = value[:, c * 128 : (c + 1) * 128]

    def put(half, row, tile):
        @pl.when(core == half)
        def _():
            keep[pl.ds(row, 16), :] = tile

        @pl.when(core != half)
        def _():
            give[pl.ds(row, 16), :] = tile.astype(BF16)

    def put_blocks(block, value):
        for half in range(2):
            first = max(block, half * HALF_BLOCKS)
            last = min(block + value.shape[0] // 16, (half + 1) * HALF_BLOCKS)
            if first >= last:
                continue

            def store(ref, half=half, first=first, last=last):
                for b in range(first, last):
                    for c in range(chunks):
                        row = ((b - half * HALF_BLOCKS) * chunks + c) * 16
                        part = value[(b - block) * 16 : (b - block + 1) * 16, c * 128 : (c + 1) * 128]
                        ref[row : row + 16, :] = part.astype(ref.dtype)

            @pl.when(core == half)
            def _(store=store):
                store(keep)

            @pl.when(core != half)
            def _(store=store):
                store(give)

    flushed = []

    def flush(half, first, last):
        n = len(flushed)
        where = pl.ds(first, last - first)
        kept = pltpu.make_async_copy(keep.at[where], keep_out.at[where], out_sem.at[2 * n])
        given = pltpu.make_async_copy(give.at[where], give_out.at[where], out_sem.at[2 * n + 1])
        flushed.append((half, kept, given))
        pl.when(core == half)(kept.start)
        pl.when(core != half)(given.start)

    zero = jnp.zeros((64, 128), F32)
    for ref in (gs, aa, rr):

        @pl.loop(0, ref.shape[0] // 64)
        def _(i, ref=ref):
            ref[pl.ds(pl.multiple_of(i * 64, 64), 64), :] = zero

    loads[0].wait()

    @pl.loop(0, rows // 16)
    def _(i):
        r = pl.multiple_of(i * 16, 16)
        spread(hx, r, h_ref[pl.ds(r, 16), :].astype(F32))

    loads[1].wait()

    @pl.loop(0, rels // 16)
    def _(i):
        r = pl.multiple_of(i * 16, 16)
        spread(zx, r, z_ref[pl.ds(r, 16), :].astype(F32))

    tail = rels // 16 * 16
    if tail < rels:
        spread(zx, tail, z_ref[tail:rels, :].astype(F32))
    loads[2].wait()
    loads[3].wait()
    for d in range(2):
        for k in range(width // 256):
            p = lax.dot_general(
                c_ref[...], w_ref[d, k * 256 : (k + 1) * 256, :], (((1,), (1,)), ((), ())),
                preferred_element_type=F32,
            )
            for h in range(2):
                px[pl.ds(d * trows * 8 + 2 * k + h, trows, stride=8), :] = p[:, h * 128 : (h + 1) * 128]
    def row(at):
        return pl.ds(pl.multiple_of(at, 8), 8)

    edge = src_ref.shape[1]

    @pl.loop(0, live_ref[0] * (edge // UNROLL))
    def _(i):
        tile = i // (edge // UNROLL)
        start = (i % (edge // UNROLL)) * UNROLL
        for u in range(0, UNROLL, 2):
            s0, s1 = src_ref[tile, start + u], src_ref[tile, start + u + 1]
            t0, t1 = tgt_ref[tile, start + u], tgt_ref[tile, start + u + 1]
            r0, r1 = rel_ref[tile, start + u], rel_ref[tile, start + u + 1]
            h0, h1 = hx[row(s0), :], hx[row(s1), :]
            p0, p1 = px[row(t0), :], px[row(t1), :]
            z0, z1 = zx[row(r0), :], zx[row(r1), :]
            for ref, at0, at1, v0, v1 in (
                (gs, s0, s1, p0 * z0, p1 * z1),
                (aa, t0, t1, (h0 * z0).astype(BF16).astype(F32), (h1 * z1).astype(BF16).astype(F32)),
                (rr, r0, r1, p0 * h0, p1 * h1),
            ):
                sum0 = ref[row(at0), :] + v0
                sum1 = ref[row(at1), :] + v1 + jnp.where(at0 == at1, v0, jnp.zeros_like(v0))
                ref[row(at0), :] = sum0
                ref[row(at1), :] = sum1

    loop_wide = loop_ref[...].astype(F32).reshape(1, width)
    h_wide = own_h[...].astype(F32)
    back = lax.dot_general(
        own_c[...], w_ref[2], (((1,), (1,)), ((), ())), preferred_element_type=F32
    )
    t_out[...] = back * loop_wide
    lsum = jnp.sum(back * h_wide, axis=0, keepdims=True)
    for c in range(chunks):
        rr[rels * 8 + c : rels * 8 + c + 1, :] = lsum[:, c * 128 : (c + 1) * 128]
    rel_base = (W_BLOCKS - HALF_BLOCKS) * chunks * 16

    @pl.loop(0, rr.shape[0] // 128)
    def _(i):
        for c in range(chunks):
            put(
                1,
                pl.multiple_of(rel_base + (i * chunks + c) * 16, 16),
                rr[pl.ds(i * 128 + c, 16, stride=8), :],
            )

    low = rel_base + rr.shape[0] // 128 * chunks * 16
    high = HALF_BLOCKS * chunks * 16
    for half, end in ((0, high), (1, low)):

        @pl.when(core == half)
        def _(end=end):
            keep[end:, :] = jnp.zeros((HALF_ROWS - end, 128), F32)

        @pl.when(core != half)
        def _(end=end):
            give[end:, :] = jnp.zeros((HALF_ROWS - end, 128), BF16)

    flush(1, rel_base, HALF_ROWS)
    self_comp = (h_wide * loop_wide).astype(BF16)
    for k in range(width // 256):
        wself = lax.dot_general(
            self_comp[:, k * 256 : (k + 1) * 256], own_c[...], (((0,), (0,)), ((), ())),
            preferred_element_type=F32,
        )
        put_blocks(96 + k * 16, wself)
    flush(0, 96 * chunks * 16, HALF_ROWS)
    flush(1, 0, rel_base)

    @pl.loop(0, rows // 16)
    def _(i):
        r = pl.multiple_of(i * 16, 16)
        for c in range(chunks):
            g_ref[pl.ds(r, 16), c * 128 : (c + 1) * 128] = gs[pl.ds(r * 8 + c, 16, stride=8), :].astype(BF16)

    g_copy = pltpu.make_async_copy(g_ref, g_out, in_sem.at[4])
    g_copy.start()

    @pl.loop(0, 2 * trows // 16)
    def _(i):
        r = pl.multiple_of(i * 16, 16)
        for c in range(chunks):
            a = aa[pl.ds(r * 8 + c, 16, stride=8), :]
            top = a.astype(BF16)
            hi[pl.ds(r, 16), c * 128 : (c + 1) * 128] = top
            lo[pl.ds(r, 16), c * 128 : (c + 1) * 128] = (a - top.astype(F32)).astype(BF16)

    for d in range(2):
        at = slice(d * trows, (d + 1) * trows)
        for k in range(width // 256):
            cols = slice(k * 256, (k + 1) * 256)
            w = lax.dot_general(
                hi[at, cols], c_ref[...], (((0,), (0,)), ((), ())), preferred_element_type=F32
            ) + lax.dot_general(
                lo[at, cols], c_ref[...], (((0,), (0,)), ((), ())), preferred_element_type=F32
            )
            put_blocks(d * 48 + k * 16, w)
        flush(0, d * 48 * chunks * 16, (d + 1) * 48 * chunks * 16)

    g_copy.wait()
    for half, kept, given in flushed:
        pl.when(core == half)(kept.wait)
        pl.when(core != half)(given.wait)


def edges(live, s8, t8, r8, h, c, w, z, own_c, own_h, loop):
    rows, width = h.shape
    trows = c.shape[0]
    rpad = (z.shape[0] + 16) // 16 * 16
    return pl.pallas_call(
        edge_kernel,
        out_shape=(
            jax.ShapeDtypeStruct((rows, width), BF16),
            jax.ShapeDtypeStruct((own_c.shape[0], width), F32),
            jax.ShapeDtypeStruct((HALF_ROWS, 128), F32),
            jax.ShapeDtypeStruct((HALF_ROWS, 128), BF16),
        ),
        in_specs=[SMEM] * 4 + [ANY] * 4 + [VMEM] * 3,
        out_specs=[ANY, VMEM, ANY, ANY],
        scratch_shapes=[
            pltpu.VMEM(h.shape, BF16),
            pltpu.VMEM(c.shape, BF16),
            pltpu.VMEM(w.shape, BF16),
            pltpu.VMEM(z.shape, BF16),
            pltpu.VMEM((rows, width), BF16),
            pltpu.VMEM((HALF_ROWS, 128), F32),
            pltpu.VMEM((HALF_ROWS, 128), BF16),
            pltpu.VMEM((rows * 8, 128), F32),
            pltpu.VMEM((2 * trows * 8, 128), F32),
            pltpu.VMEM((rpad * 8, 128), F32),
            pltpu.VMEM((rows * 8, 128), F32),
            pltpu.VMEM((2 * trows * 8, 128), F32),
            pltpu.VMEM((rpad * 8, 128), F32),
            pltpu.VMEM((2 * trows, width), BF16),
            pltpu.VMEM((2 * trows, width), BF16),
            DMA((5,)),
            DMA((10,)),
        ],
        compiler_params=pltpu.CompilerParams(vmem_limit_bytes=VMEM_BYTES),
        name="edges",
    )(live, s8, t8, r8, h, c, w, z, own_c, own_h, loop)


def reduce_kernel(
    keep_hbm, give, g_ref, full, g_out,
    keep, g_own, pair, out1, in1, acc1, in2, acc2, in3, unit, g_in, g_acc, g_side,
    pair_s, pair_r, s1, r1, s2, r2, s3, r3, s4, r4, s5, r5, s6, r6, sib_s, sib_r, gz_s, gz_r, gx_s, gx_r,
    local, kept,
):
    me = Place()
    core = me.core
    sibling = me.sibling()
    x_hi, z = me.x_hi, me.at["z"]

    def rows_of(p, a):
        size = PARTS[p][1] * 16
        return pl.ds(pl.multiple_of(BASES[p] + a * size, 16), size)

    def first(p):
        return me.at[PARTS[p][0][0]]

    def second(p):
        return me.at[PARTS[p][0][1]]

    def third(p):
        return me.at[PARTS[p][0][2]]

    order = [(p, j) for j in (1, 2, 3, 0) for p in range(3)]
    keeps = {}
    for p, j in order:
        where = rows_of(p, (first(p) + j) % 4)
        keeps[p, j] = pltpu.make_async_copy(keep_hbm.at[where], keep.at[where], kept.at[p * 4 + j])
        keeps[p, j].start()
    own_g = pltpu.make_async_copy(g_ref.at[:, z], g_own, kept.at[12])
    own_g.start()
    greet([me.along(axis, k) for axis in ("x", "y", "z") for k in (1, 2, 3)] + [sibling])

    gz = []
    for k in (1, 2, 3):
        copy = push(
            g_ref.at[:, (z + k) % 4], g_in.at[k - 1], gz_s.at[k - 1], gz_r.at[k - 1], me.along("z", k)
        )
        copy.start()
        gz.append(copy)

    pairs = {}
    for p, j in order:
        where = rows_of(p, (first(p) + j) % 4)
        copy = push(give.at[where], pair.at[where], pair_s.at[p * 4 + j], pair_r.at[p * 4 + j], sibling)
        copy.start()
        pairs[p, j] = copy

    step1 = {}
    for j in (1, 2, 3):
        for p in range(3):
            axis, unit_rows = PARTS[p][0][0], PARTS[p][1]
            base = BASES[p] + ((first(p) + j) % 4) * (unit_rows * 16)
            keeps[p, j].wait()
            pairs[p, j].wait_recv()

            @pl.loop(0, unit_rows * 16 // 128)
            def _(i, base=base):
                r = pl.ds(pl.multiple_of(base + i * 128, 16), 128)
                out1[r, :] = (keep[r, :] + pair[r, :].astype(F32)).astype(BF16)

            where = rows_of(p, (first(p) + j) % 4)
            copy = push(
                out1.at[where],
                in1.at[j - 1, pl.ds(BASES[p] // 4, unit_rows * 16)],
                s1.at[p * 3 + j - 1],
                r1.at[p * 3 + j - 1],
                me.along(axis, j),
            )
            copy.start()
            step1[p, j] = copy

    own_g.wait()
    for copy in gz:
        copy.wait_recv()
    for half in range(2):
        g_acc[half] = (
            g_own[half].astype(F32)
            + g_in[0, half].astype(F32)
            + g_in[1, half].astype(F32)
            + g_in[2, half].astype(F32)
        )
    gx = push(g_acc.at[1 - x_hi], g_side, gx_s, gx_r, me.along("x", 2))
    gx.start()

    step2 = {}
    for p in range(3):
        axis, unit_rows = PARTS[p][0][1], PARTS[p][1]
        base = BASES[p] + first(p) * (unit_rows * 16)
        low = BASES[p] // 4
        keeps[p, 0].wait()
        pairs[p, 0].wait_recv()
        for j in (1, 2, 3):
            step1[p, j].wait_recv()

        @pl.loop(0, unit_rows * 16 // 128)
        def _(i, base=base, low=low):
            r = pl.ds(pl.multiple_of(base + i * 128, 16), 128)
            q = pl.ds(pl.multiple_of(low + i * 128, 16), 128)
            acc1[q, :] = (
                keep[r, :]
                + pair[r, :].astype(F32)
                + in1[0, q, :].astype(F32)
                + in1[1, q, :].astype(F32)
                + in1[2, q, :].astype(F32)
            )

        for j in (1, 2, 3):
            where = pl.ds(pl.multiple_of(low + ((second(p) + j) % 4) * (unit_rows * 4), 16), unit_rows * 4)
            copy = push(
                acc1.at[where],
                in2.at[j - 1, pl.ds(BASES[p] // 16, unit_rows * 4)],
                s2.at[p * 3 + j - 1],
                r2.at[p * 3 + j - 1],
                me.along(axis, j),
            )
            copy.start()
            step2[p, j] = copy

    step3 = {}
    for p in range(3):
        axis, unit_rows = PARTS[p][0][2], PARTS[p][1]
        for j in (1, 2, 3):
            step2[p, j].wait_recv()
        size = unit_rows * 4
        q = pl.ds(BASES[p] // 16, size)
        mine = pl.ds(pl.multiple_of(BASES[p] // 4 + second(p) * size, 16), size)
        acc2[q, :] = acc1[mine, :] + in2[0, q, :] + in2[1, q, :] + in2[2, q, :]
        for j in (1, 2, 3):
            where = pl.ds(
                pl.multiple_of(BASES[p] // 16 + ((third(p) + j) % 4) * unit_rows, 16), unit_rows
            )
            copy = push(
                acc2.at[where],
                in3.at[j - 1, pl.ds(BASES[p] // 64, unit_rows)],
                s3.at[p * 3 + j - 1],
                r3.at[p * 3 + j - 1],
                me.along(axis, j),
            )
            copy.start()
            step3[p, j] = copy

    def place(p, depth):
        unit_rows = PARTS[p][1]
        row = core * HALF_ROWS + BASES[p] + first(p) * (unit_rows * 16)
        if depth > 1:
            row = row + second(p) * (unit_rows * 4)
        if depth > 2:
            row = row + third(p) * unit_rows
        size = (unit_rows * 16, unit_rows * 4, unit_rows)[depth - 1]
        return pl.ds(pl.multiple_of(row, 16), size)

    step4, own = {}, {}
    for p in range(3):
        axis, unit_rows = PARTS[p][0][2], PARTS[p][1]
        for j in (1, 2, 3):
            step3[p, j].wait_recv()
        q = pl.ds(BASES[p] // 64, unit_rows)
        mine = pl.ds(pl.multiple_of(BASES[p] // 16 + third(p) * unit_rows, 16), unit_rows)
        unit[q, :] = (acc2[mine, :] + in3[0, q, :] + in3[1, q, :] + in3[2, q, :]).astype(BF16)
        own[p] = pltpu.make_async_copy(unit.at[q], full.at[place(p, 3)], local.at[p])
        own[p].start()
        for j in (1, 2, 3):
            copy = push(
                unit.at[q], full.at[place(p, 3)], s4.at[p * 3 + j - 1], r4.at[p * 3 + j - 1], me.along(axis, j)
            )
            copy.start()
            step4[p, j] = copy

    step5 = {}
    for p in range(3):
        own[p].wait()
        for j in (1, 2, 3):
            step4[p, j].wait_recv()
        for j in (1, 2, 3):
            block = full.at[place(p, 2)]
            copy = push(block, block, s5.at[p * 3 + j - 1], r5.at[p * 3 + j - 1], me.along(PARTS[p][0][1], j))
            copy.start()
            step5[p, j] = copy

    step6, side = {}, {}
    for p in range(3):
        for j in (1, 2, 3):
            step5[p, j].wait_recv()
        block = full.at[place(p, 1)]
        for j in (1, 2, 3):
            copy = push(block, block, s6.at[p * 3 + j - 1], r6.at[p * 3 + j - 1], me.along(PARTS[p][0][0], j))
            copy.start()
            step6[p, j] = copy
        side[p, 0] = push(block, block, sib_s.at[p * 4], sib_r.at[p * 4], sibling)
        side[p, 0].start()

    gx.wait_recv()
    g_out[...] = g_acc[x_hi] + g_side[...]

    for j in (1, 3, 2):
        for p in range(3):
            size = PARTS[p][1] * 16
            step6[p, j].wait_recv()
            row = core * HALF_ROWS + BASES[p] + ((first(p) + 4 - j) % 4) * size
            block = full.at[pl.ds(pl.multiple_of(row, 16), size)]
            side[p, j] = push(block, block, sib_s.at[p * 4 + j], sib_r.at[p * 4 + j], sibling)
            side[p, j].start()

    for copy in side.values():
        copy.wait_recv()
    gx.wait_send()
    for group in (gz, pairs.values(), step1.values(), step2.values(), step3.values(), step4.values()):
        for copy in group:
            copy.wait_send()
    for group in (step5.values(), step6.values(), side.values()):
        for copy in group:
            copy.wait_send()


def reduce_all(keep, give, g):
    rows, width = g.shape
    g = g.reshape(2, 4, rows // 8, width)
    return pl.pallas_call(
        reduce_kernel,
        out_shape=(
            jax.ShapeDtypeStruct((2 * HALF_ROWS, 128), BF16),
            jax.ShapeDtypeStruct((rows // 8, width), F32),
        ),
        in_specs=[ANY] * 3,
        out_specs=[ANY, VMEM],
        scratch_shapes=[
            pltpu.VMEM((HALF_ROWS, 128), F32),
            pltpu.VMEM((2, rows // 8, width), BF16),
            pltpu.VMEM((HALF_ROWS, 128), BF16),
            pltpu.VMEM((HALF_ROWS, 128), BF16),
            pltpu.VMEM((3, HALF_ROWS // 4, 128), BF16),
            pltpu.VMEM((HALF_ROWS // 4, 128), F32),
            pltpu.VMEM((3, HALF_ROWS // 16, 128), F32),
            pltpu.VMEM((HALF_ROWS // 16, 128), F32),
            pltpu.VMEM((3, HALF_ROWS // 64, 128), F32),
            pltpu.VMEM((HALF_ROWS // 64, 128), BF16),
            pltpu.VMEM((3, 2, rows // 8, width), BF16),
            pltpu.VMEM((2, rows // 8, width), F32),
            pltpu.VMEM((rows // 8, width), F32),
            DMA((12,)), DMA((12,)),
            *[DMA((9,)) for _ in range(12)],
            DMA((12,)), DMA((12,)), DMA((3,)), DMA((3,)), DMA, DMA, DMA((3,)), DMA((13,)),
        ],
        compiler_params=pltpu.CompilerParams(
            collective_id=1, has_side_effects=True, vmem_limit_bytes=VMEM_BYTES
        ),
        name="reduce_all",
    )(keep, give, g)


def unpack_kernel(
    full_hbm, w_hbm, r_out, l_out, full, w_out, in_sem, out_sem, *, edge_scale, self_scale, rel_scale
):
    rels, width = r_out.shape
    chunks = width // 128
    per = width // 16
    pieces = in_sem.shape[0]
    size = full.shape[0] // pieces
    loads = []
    for i in range(pieces):
        where = pl.ds(i * size, size)
        loads.append(pltpu.make_async_copy(full_hbm.at[where], full.at[where], in_sem.at[i]))
        loads[-1].start()
    waited = [0]

    def start_of(block):
        half = block // HALF_BLOCKS
        return half * HALF_ROWS + (block - half * HALF_BLOCKS) * chunks * 16

    def need(blocks):
        end = start_of(blocks - 1) + chunks * 16
        while waited[0] * size < end:
            loads[waited[0]].wait()
            waited[0] += 1

    def tile(block, c):
        half = block // HALF_BLOCKS
        row = half * HALF_ROWS + ((block - half * HALF_BLOCKS) * chunks + c) * 16
        return full[pl.ds(pl.multiple_of(row, 16), 16), :].astype(F32)

    stores = []
    for d, scale in enumerate((edge_scale, edge_scale, self_scale)):
        for k in range(3):
            group = per // 3
            need(d * per + (k + 1) * group)

            @pl.loop(k * group, (k + 1) * group)
            def _(i, d=d, scale=scale):
                for c in range(chunks):
                    w_out[d, pl.ds(pl.multiple_of(i * 16, 16), 16), c * 128 : (c + 1) * 128] = (
                        tile(d * per + i, c) * scale
                    )

            where = pl.ds(k * group * 16, group * 16)
            stores.append(
                pltpu.make_async_copy(w_out.at[d, where], w_hbm.at[d, where], out_sem.at[d * 3 + k])
            )
            stores[-1].start()

    whole = rels // 16
    need(W_BLOCKS + whole + 1)

    @pl.loop(0, whole)
    def _(i):
        for c in range(chunks):
            r_out[pl.ds(pl.multiple_of(i * 16, 16), 16), c * 128 : (c + 1) * 128] = (
                tile(W_BLOCKS + i, c) * rel_scale
            )

    rest = rels - whole * 16
    for c in range(chunks):
        last = tile(W_BLOCKS + whole, c)
        cols = slice(c * 128, (c + 1) * 128)
        if rest:
            r_out[whole * 16 : rels, cols] = last[:rest] * rel_scale
        l_out[cols] = (last[rest : rest + 1] * self_scale).reshape(128)
    while waited[0] < pieces:
        loads[waited[0]].wait()
        waited[0] += 1
    for store in stores:
        store.wait()


def unpack(full, rels, width, **scales):
    return pl.pallas_call(
        functools.partial(unpack_kernel, **scales),
        out_shape=(
            jax.ShapeDtypeStruct((3, width, width), F32),
            jax.ShapeDtypeStruct((rels, width), F32),
            jax.ShapeDtypeStruct((width,), F32),
        ),
        in_specs=[ANY],
        out_specs=[ANY, VMEM, VMEM],
        scratch_shapes=[
            pltpu.VMEM(full.shape, BF16),
            pltpu.VMEM((3, width, width), F32),
            DMA((11,)),
            DMA((9,)),
        ],
        compiler_params=pltpu.CompilerParams(vmem_limit_bytes=VMEM_BYTES),
        name="unpack",
    )(full)


def body(
    h_src, rel_table, cotangent, h_tgt, loop_rel, weights, src_index, tgt_index, rel_ids, direction, counts
):
    width = weights.shape[1]
    tiles, edge = src_index.shape[2:]
    rels = rel_table.shape[0]
    h_all, c_all, s8, t8, r8 = gather(
        h_src, cotangent, *[a.reshape(tiles, edge) for a in (src_index, tgt_index, rel_ids, direction)]
    )
    g, grad_tgt, keep, give = edges(
        counts.reshape(1), s8, t8, r8, h_all, c_all, weights, rel_table, cotangent, h_tgt, loop_rel
    )
    full, grad_src = reduce_all(keep, give, g)
    devices = lax.axis_size("src") * lax.axis_size("tgt")
    edges_all = float(devices * tiles * edge)
    targets_all = float(devices * cotangent.shape[0])
    grad_weights, grad_rel, grad_loop = unpack(
        full,
        rels,
        width,
        edge_scale=edges_all**-0.5,
        self_scale=targets_all**-0.5,
        rel_scale=(float(rels) / edges_all) ** 0.5,
    )
    return grad_src, grad_tgt, grad_weights, grad_rel, grad_loop


def solution(mesh):
    return jax.shard_map(
        body,
        mesh=mesh,
        in_specs=(
            P(("src", "tgt"), None),
            P(),
            P(("tgt", "src"), None),
            P(("tgt", "src"), None),
            P(),
            P(),
            P("src", "tgt", None, None),
            P("src", "tgt", None, None),
            P("src", "tgt", None, None),
            P("src", "tgt", None, None),
            P("src", "tgt"),
        ),
        out_specs=(P(("src", "tgt"), None), P(("tgt", "src"), None), P(), P(), P()),
        check_vma=False,
    )
```

```python
import functools

import jax
import jax.numpy as jnp
from jax import lax
from jax.experimental import pallas as pl
from jax.experimental.pallas import tpu as pltpu
from jax.sharding import PartitionSpec as P

F32 = jnp.float32
BF16 = jnp.bfloat16
MESH = pl.DeviceIdType.MESH
ANY = pl.BlockSpec(memory_space=pl.ANY)
VMEM = pl.BlockSpec(memory_space=pltpu.VMEM)
SMEM = pl.BlockSpec(memory_space=pltpu.SMEM)
DMA = pltpu.SemaphoreType.DMA

HALF_BLOCKS = 116
HALF_ROWS = 11264
W_BLOCKS = 144
PARTS = ((("x", "y", "z"), 64), (("y", "z", "x"), 64), (("z", "x", "y"), 48))
BASES = (0, 4096, 8192)
UNROLL = 16
EDGE = 128
VMEM_BYTES = 63 * 2**20


class Place:
    def __init__(self):
        s, t = lax.axis_index("src"), lax.axis_index("tgt")
        self.x_lo, self.core = s // 8, s % 2
        self.x_hi = t // 4
        self.at = {"x": self.x_hi * 2 + self.x_lo, "y": (s // 2) % 4, "z": t % 4}

    def device(self, at, core):
        return ((at["x"] % 2) * 8 + at["y"] * 2 + core, (at["x"] // 2) * 4 + at["z"])

    def along(self, axis, offset):
        at = dict(self.at)
        at[axis] = (at[axis] + offset) % 4
        return self.device(at, self.core)

    def sibling(self):
        return self.device(self.at, 1 - self.core)

    def x_lo_partner(self):
        at = dict(self.at)
        at["x"] = self.x_hi * 2 + (1 - self.x_lo)
        return self.device(at, self.core)


def greet(partners):
    barrier = pltpu.get_barrier_semaphore()
    for partner in partners:
        pl.semaphore_signal(barrier, inc=1, device_id=partner, device_id_type=MESH)
    pl.semaphore_wait(barrier, len(partners))


def push(src, dst, send, recv, device):
    return pltpu.make_async_remote_copy(
        src_ref=src, dst_ref=dst, send_sem=send, recv_sem=recv, device_id=device, device_id_type=MESH
    )


def gather_kernel(
    h_ref, c_ref, src_ref, tgt_ref, rel_ref, dir_ref, h_all, c_all, s8, t8, r8, local, hx_s, hx_r, hz_s, hz_r, cy_s, cy_r, cx_s, cx_r, cs_s, cs_r
):
    me = Place()
    x_lo, x_hi, core, y, z = me.x_lo, me.x_hi, me.core, me.at["y"], me.at["z"]
    sibling, across = me.sibling(), me.x_lo_partner()
    own_h = pltpu.make_async_copy(h_ref, h_all.at[x_hi, z], local.at[0])
    own_c = pltpu.make_async_copy(c_ref, c_all.at[x_lo, y, core], local.at[1])
    own_h.start()
    own_c.start()
    s8[...] = src_ref[...] * 8
    t8[...] = (tgt_ref[...] + dir_ref[...] * (16 * c_ref.shape[0])) * 8
    r8[...] = rel_ref[...] * 8
    greet(
        [me.along("x", 2), across, sibling]
        + [me.along("y", k) for k in (1, 2, 3)]
        + [me.along("z", k) for k in (1, 2, 3)]
    )
    mine, theirs = h_all.at[x_hi, z], h_all.at[1 - x_hi, z]
    hx = push(h_ref, mine, hx_s, hx_r, me.along("x", 2))
    hx.start()
    cy, hz = [], []
    for k in (1, 3, 2):
        copy = push(h_ref, mine, hz_s.at[k - 1], hz_r.at[k - 1], me.along("z", k))
        copy.start()
        hz.append(copy)
        copy = push(c_ref, c_all.at[x_lo, y, core], cy_s.at[k - 1], cy_r.at[k - 1], me.along("y", k))
        copy.start()
        cy.append(copy)
    hx.wait()
    for k in (1, 3, 2):
        copy = push(theirs, theirs, hz_s.at[k + 2], hz_r.at[k + 2], me.along("z", k))
        copy.start()
        hz.append(copy)
    own_c.wait()
    for copy in cy:
        copy.wait()
    near = c_all.at[x_lo, :, core]
    far = c_all.at[1 - x_lo, :, core]
    cx = push(near, near, cx_s, cx_r, across)
    cx.start()
    first = push(near, near, cs_s.at[0], cs_r.at[0], sibling)
    first.start()
    cx.wait()
    second = push(far, far, cs_s.at[1], cs_r.at[1], sibling)
    second.start()
    first.wait()
    second.wait()
    own_h.wait()
    for copy in hz:
        copy.wait()


def gather(h_src, cotangent, *indices):
    rows, width = h_src.shape
    trows = cotangent.shape[0]
    h_all, c_all, s8, t8, r8 = pl.pallas_call(
        gather_kernel,
        out_shape=(
            jax.ShapeDtypeStruct((2, 4, rows, width), BF16),
            jax.ShapeDtypeStruct((2, 4, 2, trows, width), BF16),
            *[jax.ShapeDtypeStruct(indices[0].shape, jnp.int32)] * 3,
        ),
        in_specs=[ANY] * 2 + [VMEM] * 4,
        out_specs=[ANY] * 2 + [VMEM] * 3,
        scratch_shapes=[
            DMA((2,)), DMA, DMA, DMA((6,)), DMA((6,)), DMA((3,)), DMA((3,)), DMA, DMA, DMA((2,)), DMA((2,)),
        ],
        compiler_params=pltpu.CompilerParams(collective_id=0, has_side_effects=True, vmem_limit_bytes=VMEM_BYTES),
        name="gather_panels",
    )(h_src, cotangent, *indices)
    flat = [a.reshape(-1) for a in (s8, t8, r8)]
    return h_all.reshape(8 * rows, width), c_all.reshape(16 * trows, width), *flat


def edge_kernel(
    live_ref, src_ref, tgt_ref, rel_ref, h_hbm, c_hbm, w_hbm, z_hbm, own_c, own_h, loop_ref,
    g_out, t_out, keep_out, give_out,
    h_ref, c_ref, w_ref, z_ref, g_ref, keep, give, hx, px, zx, gs, aa, rr, hi, lo, in_sem, out_sem,
):
    loads = [
        pltpu.make_async_copy(a, b, in_sem.at[i])
        for i, (a, b) in enumerate(((h_hbm, h_ref), (z_hbm, z_ref), (c_hbm, c_ref), (w_hbm, w_ref)))
    ]
    for load in loads:
        load.start()
    core = lax.axis_index("src") % 2
    rows = h_ref.shape[0]
    trows = c_ref.shape[0]
    rels, width = z_ref.shape
    chunks = width // 128

    def spread(dst, row, value):
        for c in range(chunks):
            dst[pl.ds(row * 8 + c, value.shape[0], stride=8), :] = value[:, c * 128 : (c + 1) * 128]

    def put(half, row, tile):
        @pl.when(core == half)
        def _():
            keep[pl.ds(row, 16), :] = tile

        @pl.when(core != half)
        def _():
            give[pl.ds(row, 16), :] = tile.astype(BF16)

    def put_blocks(block, value):
        for half in range(2):
            first = max(block, half * HALF_BLOCKS)
            last = min(block + value.shape[0] // 16, (half + 1) * HALF_BLOCKS)
            if first >= last:
                continue

            def store(ref, half=half, first=first, last=last):
                for b in range(first, last):
                    for c in range(chunks):
                        row = ((b - half * HALF_BLOCKS) * chunks + c) * 16
                        part = value[(b - block) * 16 : (b - block + 1) * 16, c * 128 : (c + 1) * 128]
                        ref[row : row + 16, :] = part.astype(ref.dtype)

            @pl.when(core == half)
            def _(store=store):
                store(keep)

            @pl.when(core != half)
            def _(store=store):
                store(give)

    flushed = []

    def flush(half, first, last):
        n = len(flushed)
        where = pl.ds(first, last - first)
        kept = pltpu.make_async_copy(keep.at[where], keep_out.at[where], out_sem.at[2 * n])
        given = pltpu.make_async_copy(give.at[where], give_out.at[where], out_sem.at[2 * n + 1])
        flushed.append((half, kept, given))
        pl.when(core == half)(kept.start)
        pl.when(core != half)(given.start)

    zero = jnp.zeros((64, 128), F32)
    for ref in (gs, aa, rr):

        @pl.loop(0, ref.shape[0] // 64)
        def _(i, ref=ref):
            ref[pl.ds(pl.multiple_of(i * 64, 64), 64), :] = zero

    loads[0].wait()

    @pl.loop(0, rows // 16)
    def _(i):
        r = pl.multiple_of(i * 16, 16)
        spread(hx, r, h_ref[pl.ds(r, 16), :].astype(F32))

    loads[1].wait()

    @pl.loop(0, rels // 16)
    def _(i):
        r = pl.multiple_of(i * 16, 16)
        spread(zx, r, z_ref[pl.ds(r, 16), :].astype(F32))

    tail = rels // 16 * 16
    if tail < rels:
        spread(zx, tail, z_ref[tail:rels, :].astype(F32))
    loads[2].wait()
    loads[3].wait()
    for d in range(2):
        for k in range(width // 256):
            p = lax.dot_general(
                c_ref[...], w_ref[d, k * 256 : (k + 1) * 256, :], (((1,), (1,)), ((), ())),
                preferred_element_type=F32,
            )
            for h in range(2):
                px[pl.ds(d * trows * 8 + 2 * k + h, trows, stride=8), :] = p[:, h * 128 : (h + 1) * 128]
    def row(at):
        return pl.ds(pl.multiple_of(at, 8), 8)

    @pl.loop(0, live_ref[0] * (EDGE // UNROLL))
    def _(i):
        start = i * UNROLL
        for u in range(0, UNROLL, 2):
            s0, s1 = src_ref[start + u], src_ref[start + u + 1]
            t0, t1 = tgt_ref[start + u], tgt_ref[start + u + 1]
            r0, r1 = rel_ref[start + u], rel_ref[start + u + 1]
            h0, h1 = hx[row(s0), :], hx[row(s1), :]
            p0, p1 = px[row(t0), :], px[row(t1), :]
            z0, z1 = zx[row(r0), :], zx[row(r1), :]
            for ref, at0, at1, v0, v1 in (
                (gs, s0, s1, p0 * z0, p1 * z1),
                (aa, t0, t1, (h0 * z0).astype(BF16).astype(F32), (h1 * z1).astype(BF16).astype(F32)),
                (rr, r0, r1, p0 * h0, p1 * h1),
            ):
                sum0 = ref[row(at0), :] + v0
                sum1 = ref[row(at1), :] + v1 + jnp.where(at0 == at1, v0, jnp.zeros_like(v0))
                ref[row(at0), :] = sum0
                ref[row(at1), :] = sum1

    loop_wide = loop_ref[...].astype(F32).reshape(1, width)
    h_wide = own_h[...].astype(F32)
    back = lax.dot_general(
        own_c[...], w_ref[2], (((1,), (1,)), ((), ())), preferred_element_type=F32
    )
    t_out[...] = back * loop_wide
    lsum = jnp.sum(back * h_wide, axis=0, keepdims=True)
    for c in range(chunks):
        rr[rels * 8 + c : rels * 8 + c + 1, :] = lsum[:, c * 128 : (c + 1) * 128]
    rel_base = (W_BLOCKS - HALF_BLOCKS) * chunks * 16

    @pl.loop(0, rr.shape[0] // 128)
    def _(i):
        for c in range(chunks):
            put(
                1,
                pl.multiple_of(rel_base + (i * chunks + c) * 16, 16),
                rr[pl.ds(i * 128 + c, 16, stride=8), :],
            )

    low = rel_base + rr.shape[0] // 128 * chunks * 16
    high = HALF_BLOCKS * chunks * 16
    for half, end in ((0, high), (1, low)):

        @pl.when(core == half)
        def _(end=end):
            keep[end:, :] = jnp.zeros((HALF_ROWS - end, 128), F32)

        @pl.when(core != half)
        def _(end=end):
            give[end:, :] = jnp.zeros((HALF_ROWS - end, 128), BF16)

    flush(1, rel_base, HALF_ROWS)
    self_comp = (h_wide * loop_wide).astype(BF16)
    for k in range(width // 256):
        wself = lax.dot_general(
            self_comp[:, k * 256 : (k + 1) * 256], own_c[...], (((0,), (0,)), ((), ())),
            preferred_element_type=F32,
        )
        put_blocks(96 + k * 16, wself)
    flush(0, 96 * chunks * 16, HALF_ROWS)
    flush(1, 0, rel_base)

    @pl.loop(0, rows // 16)
    def _(i):
        r = pl.multiple_of(i * 16, 16)
        for c in range(chunks):
            g_ref[pl.ds(r, 16), c * 128 : (c + 1) * 128] = gs[pl.ds(r * 8 + c, 16, stride=8), :].astype(BF16)

    g_copy = pltpu.make_async_copy(g_ref, g_out, in_sem.at[4])
    g_copy.start()

    @pl.loop(0, 2 * trows // 16)
    def _(i):
        r = pl.multiple_of(i * 16, 16)
        for c in range(chunks):
            a = aa[pl.ds(r * 8 + c, 16, stride=8), :]
            top = a.astype(BF16)
            hi[pl.ds(r, 16), c * 128 : (c + 1) * 128] = top
            lo[pl.ds(r, 16), c * 128 : (c + 1) * 128] = (a - top.astype(F32)).astype(BF16)

    for d in range(2):
        at = slice(d * trows, (d + 1) * trows)
        for k in range(width // 256):
            cols = slice(k * 256, (k + 1) * 256)
            w = lax.dot_general(
                hi[at, cols], c_ref[...], (((0,), (0,)), ((), ())), preferred_element_type=F32
            ) + lax.dot_general(
                lo[at, cols], c_ref[...], (((0,), (0,)), ((), ())), preferred_element_type=F32
            )
            put_blocks(d * 48 + k * 16, w)
        flush(0, d * 48 * chunks * 16, (d + 1) * 48 * chunks * 16)

    g_copy.wait()
    for half, kept, given in flushed:
        pl.when(core == half)(kept.wait)
        pl.when(core != half)(given.wait)


def edges(live, s8, t8, r8, h, c, w, z, own_c, own_h, loop):
    rows, width = h.shape
    trows = c.shape[0]
    rpad = (z.shape[0] + 16) // 16 * 16
    return pl.pallas_call(
        edge_kernel,
        out_shape=(
            jax.ShapeDtypeStruct((rows, width), BF16),
            jax.ShapeDtypeStruct((own_c.shape[0], width), F32),
            jax.ShapeDtypeStruct((HALF_ROWS, 128), F32),
            jax.ShapeDtypeStruct((HALF_ROWS, 128), BF16),
        ),
        in_specs=[SMEM] * 4 + [ANY] * 4 + [VMEM] * 3,
        out_specs=[ANY, VMEM, ANY, ANY],
        scratch_shapes=[
            pltpu.VMEM(h.shape, BF16),
            pltpu.VMEM(c.shape, BF16),
            pltpu.VMEM(w.shape, BF16),
            pltpu.VMEM(z.shape, BF16),
            pltpu.VMEM((rows, width), BF16),
            pltpu.VMEM((HALF_ROWS, 128), F32),
            pltpu.VMEM((HALF_ROWS, 128), BF16),
            pltpu.VMEM((rows * 8, 128), F32),
            pltpu.VMEM((2 * trows * 8, 128), F32),
            pltpu.VMEM((rpad * 8, 128), F32),
            pltpu.VMEM((rows * 8, 128), F32),
            pltpu.VMEM((2 * trows * 8, 128), F32),
            pltpu.VMEM((rpad * 8, 128), F32),
            pltpu.VMEM((2 * trows, width), BF16),
            pltpu.VMEM((2 * trows, width), BF16),
            DMA((5,)),
            DMA((10,)),
        ],
        compiler_params=pltpu.CompilerParams(vmem_limit_bytes=VMEM_BYTES),
        name="edges",
    )(live, s8, t8, r8, h, c, w, z, own_c, own_h, loop)


def reduce_kernel(
    keep_hbm, give, g_ref, full, g_out,
    keep, g_own, pair, out1, in1, acc1, in2, acc2, in3, unit, g_in, g_acc, g_side,
    pair_s, pair_r, s1, r1, s2, r2, s3, r3, s4, r4, s5, r5, s6, r6, sib_s, sib_r, gz_s, gz_r, gx_s, gx_r,
    local, kept,
):
    me = Place()
    core = me.core
    sibling = me.sibling()
    x_hi, z = me.x_hi, me.at["z"]

    def rows_of(p, a):
        size = PARTS[p][1] * 16
        return pl.ds(pl.multiple_of(BASES[p] + a * size, 16), size)

    def first(p):
        return me.at[PARTS[p][0][0]]

    def second(p):
        return me.at[PARTS[p][0][1]]

    def third(p):
        return me.at[PARTS[p][0][2]]

    order = [(p, j) for j in (1, 2, 3, 0) for p in range(3)]
    keeps = {}
    for p, j in order:
        where = rows_of(p, (first(p) + j) % 4)
        keeps[p, j] = pltpu.make_async_copy(keep_hbm.at[where], keep.at[where], kept.at[p * 4 + j])
        keeps[p, j].start()
    own_g = pltpu.make_async_copy(g_ref.at[:, z], g_own, kept.at[12])
    own_g.start()
    greet([me.along(axis, k) for axis in ("x", "y", "z") for k in (1, 2, 3)] + [sibling])

    pairs = {}
    for p, j in order:
        where = rows_of(p, (first(p) + j) % 4)
        copy = push(give.at[where], pair.at[where], pair_s.at[p * 4 + j], pair_r.at[p * 4 + j], sibling)
        copy.start()
        pairs[p, j] = copy

    step1 = {}
    for j in (1, 2, 3):
        for p in range(3):
            axis, unit_rows = PARTS[p][0][0], PARTS[p][1]
            base = BASES[p] + ((first(p) + j) % 4) * (unit_rows * 16)
            keeps[p, j].wait()
            pairs[p, j].wait_recv()

            @pl.loop(0, unit_rows * 16 // 128)
            def _(i, base=base):
                r = pl.ds(pl.multiple_of(base + i * 128, 16), 128)
                out1[r, :] = (keep[r, :] + pair[r, :].astype(F32)).astype(BF16)

            where = rows_of(p, (first(p) + j) % 4)
            copy = push(
                out1.at[where],
                in1.at[j - 1, pl.ds(BASES[p] // 4, unit_rows * 16)],
                s1.at[p * 3 + j - 1],
                r1.at[p * 3 + j - 1],
                me.along(axis, j),
            )
            copy.start()
            step1[p, j] = copy

    step2 = {}
    for p in range(3):
        axis, unit_rows = PARTS[p][0][1], PARTS[p][1]
        base = BASES[p] + first(p) * (unit_rows * 16)
        low = BASES[p] // 4
        keeps[p, 0].wait()
        pairs[p, 0].wait_recv()
        for j in (1, 2, 3):
            step1[p, j].wait_recv()

        @pl.loop(0, unit_rows * 16 // 128)
        def _(i, base=base, low=low):
            r = pl.ds(pl.multiple_of(base + i * 128, 16), 128)
            q = pl.ds(pl.multiple_of(low + i * 128, 16), 128)
            acc1[q, :] = (
                keep[r, :]
                + pair[r, :].astype(F32)
                + in1[0, q, :].astype(F32)
                + in1[1, q, :].astype(F32)
                + in1[2, q, :].astype(F32)
            )

        for j in (1, 2, 3):
            where = pl.ds(pl.multiple_of(low + ((second(p) + j) % 4) * (unit_rows * 4), 16), unit_rows * 4)
            copy = push(
                acc1.at[where],
                in2.at[j - 1, pl.ds(BASES[p] // 16, unit_rows * 4)],
                s2.at[p * 3 + j - 1],
                r2.at[p * 3 + j - 1],
                me.along(axis, j),
            )
            copy.start()
            step2[p, j] = copy

    gz = []
    for k in (1, 2, 3):
        copy = push(
            g_ref.at[:, (z + k) % 4], g_in.at[k - 1], gz_s.at[k - 1], gz_r.at[k - 1], me.along("z", k)
        )
        copy.start()
        gz.append(copy)

    step3 = {}
    for p in range(3):
        axis, unit_rows = PARTS[p][0][2], PARTS[p][1]
        for j in (1, 2, 3):
            step2[p, j].wait_recv()
        size = unit_rows * 4
        q = pl.ds(BASES[p] // 16, size)
        mine = pl.ds(pl.multiple_of(BASES[p] // 4 + second(p) * size, 16), size)
        acc2[q, :] = acc1[mine, :] + in2[0, q, :] + in2[1, q, :] + in2[2, q, :]
        for j in (1, 2, 3):
            where = pl.ds(
                pl.multiple_of(BASES[p] // 16 + ((third(p) + j) % 4) * unit_rows, 16), unit_rows
            )
            copy = push(
                acc2.at[where],
                in3.at[j - 1, pl.ds(BASES[p] // 64, unit_rows)],
                s3.at[p * 3 + j - 1],
                r3.at[p * 3 + j - 1],
                me.along(axis, j),
            )
            copy.start()
            step3[p, j] = copy

    def place(p, depth):
        unit_rows = PARTS[p][1]
        row = core * HALF_ROWS + BASES[p] + first(p) * (unit_rows * 16)
        if depth > 1:
            row = row + second(p) * (unit_rows * 4)
        if depth > 2:
            row = row + third(p) * unit_rows
        size = (unit_rows * 16, unit_rows * 4, unit_rows)[depth - 1]
        return pl.ds(pl.multiple_of(row, 16), size)

    step4, own = {}, {}
    for p in range(3):
        axis, unit_rows = PARTS[p][0][2], PARTS[p][1]
        for j in (1, 2, 3):
            step3[p, j].wait_recv()
        q = pl.ds(BASES[p] // 64, unit_rows)
        mine = pl.ds(pl.multiple_of(BASES[p] // 16 + third(p) * unit_rows, 16), unit_rows)
        unit[q, :] = (acc2[mine, :] + in3[0, q, :] + in3[1, q, :] + in3[2, q, :]).astype(BF16)
        own[p] = pltpu.make_async_copy(unit.at[q], full.at[place(p, 3)], local.at[p])
        own[p].start()
        for j in (1, 2, 3):
            copy = push(
                unit.at[q], full.at[place(p, 3)], s4.at[p * 3 + j - 1], r4.at[p * 3 + j - 1], me.along(axis, j)
            )
            copy.start()
            step4[p, j] = copy

    own_g.wait()
    for copy in gz:
        copy.wait_recv()
    for half in range(2):
        g_acc[half] = (
            g_own[half].astype(F32)
            + g_in[0, half].astype(F32)
            + g_in[1, half].astype(F32)
            + g_in[2, half].astype(F32)
        )
    gx = push(g_acc.at[1 - x_hi], g_side, gx_s, gx_r, me.along("x", 2))
    gx.start()

    step5 = {}
    for p in range(3):
        own[p].wait()
        for j in (1, 2, 3):
            step4[p, j].wait_recv()
        for j in (1, 2, 3):
            block = full.at[place(p, 2)]
            copy = push(block, block, s5.at[p * 3 + j - 1], r5.at[p * 3 + j - 1], me.along(PARTS[p][0][1], j))
            copy.start()
            step5[p, j] = copy

    def half_of(p, offset, half):
        size = PARTS[p][1] * 8
        row = core * HALF_ROWS + BASES[p] + ((first(p) + 4 + offset) % 4) * (2 * size) + half * size
        return full.at[pl.ds(pl.multiple_of(row, 16), size)]

    step6, side = {}, {}
    for p in range(3):
        for j in (1, 2, 3):
            step5[p, j].wait_recv()
        for n, (to, half) in enumerate(((1, 0), (3, 1), (1, 1), (3, 0))):
            block = half_of(p, 0, half)
            copy = push(block, block, s6.at[p * 6 + n], r6.at[p * 6 + n], me.along(PARTS[p][0][0], to))
            copy.start()
            step6[p, n] = copy
        block = full.at[place(p, 1)]
        side[p, 0] = push(block, block, sib_s.at[p * 7], sib_r.at[p * 7], sibling)
        side[p, 0].start()

    def across(p, n, offset, half):
        block = half_of(p, offset, half)
        side[p, n] = push(block, block, sib_s.at[p * 7 + n], sib_r.at[p * 7 + n], sibling)
        side[p, n].start()

    for p in range(3):
        for n, (to, half) in enumerate(((1, 0), (3, 1))):
            step6[p, n].wait_recv()
            block = half_of(p, -to, half)
            copy = push(block, block, s6.at[p * 6 + 4 + n], r6.at[p * 6 + 4 + n], me.along(PARTS[p][0][0], to))
            copy.start()
            step6[p, 4 + n] = copy
            across(p, 1 + n, -to, half)

    gx.wait_recv()
    g_out[...] = g_acc[x_hi] + g_side[...]

    for p in range(3):
        for n, (to, half) in enumerate(((1, 1), (3, 0))):
            step6[p, 2 + n].wait_recv()
            across(p, 3 + n, -to, half)
    for p in range(3):
        for half in range(2):
            step6[p, 4 + half].wait_recv()
            across(p, 5 + half, 2, half)

    for copy in side.values():
        copy.wait_recv()
    gx.wait_send()
    for group in (gz, pairs.values(), step1.values(), step2.values(), step3.values(), step4.values()):
        for copy in group:
            copy.wait_send()
    for group in (step5.values(), step6.values(), side.values()):
        for copy in group:
            copy.wait_send()


def reduce_all(keep, give, g):
    rows, width = g.shape
    g = g.reshape(2, 4, rows // 8, width)
    return pl.pallas_call(
        reduce_kernel,
        out_shape=(
            jax.ShapeDtypeStruct((2 * HALF_ROWS, 128), BF16),
            jax.ShapeDtypeStruct((rows // 8, width), F32),
        ),
        in_specs=[ANY] * 3,
        out_specs=[ANY, VMEM],
        scratch_shapes=[
            pltpu.VMEM((HALF_ROWS, 128), F32),
            pltpu.VMEM((2, rows // 8, width), BF16),
            pltpu.VMEM((HALF_ROWS, 128), BF16),
            pltpu.VMEM((HALF_ROWS, 128), BF16),
            pltpu.VMEM((3, HALF_ROWS // 4, 128), BF16),
            pltpu.VMEM((HALF_ROWS // 4, 128), F32),
            pltpu.VMEM((3, HALF_ROWS // 16, 128), F32),
            pltpu.VMEM((HALF_ROWS // 16, 128), F32),
            pltpu.VMEM((3, HALF_ROWS // 64, 128), F32),
            pltpu.VMEM((HALF_ROWS // 64, 128), BF16),
            pltpu.VMEM((3, 2, rows // 8, width), BF16),
            pltpu.VMEM((2, rows // 8, width), F32),
            pltpu.VMEM((rows // 8, width), F32),
            DMA((12,)), DMA((12,)),
            *[DMA((9,)) for _ in range(10)],
            *[DMA((18,))] * 2, *[DMA((21,))] * 2, DMA((3,)), DMA((3,)), DMA, DMA, DMA((3,)), DMA((13,)),
        ],
        compiler_params=pltpu.CompilerParams(
            collective_id=1, has_side_effects=True, vmem_limit_bytes=VMEM_BYTES
        ),
        name="reduce_all",
    )(keep, give, g)


def unpack_kernel(
    full_hbm, w_hbm, r_out, l_out, full, w_out, in_sem, out_sem, *, edge_scale, self_scale, rel_scale
):
    rels, width = r_out.shape
    chunks = width // 128
    per = width // 16
    pieces = in_sem.shape[0]
    size = full.shape[0] // pieces
    loads = []
    for i in range(pieces):
        where = pl.ds(i * size, size)
        loads.append(pltpu.make_async_copy(full_hbm.at[where], full.at[where], in_sem.at[i]))
        loads[-1].start()
    waited = [0]

    def start_of(block):
        half = block // HALF_BLOCKS
        return half * HALF_ROWS + (block - half * HALF_BLOCKS) * chunks * 16

    def need(blocks):
        end = start_of(blocks - 1) + chunks * 16
        while waited[0] * size < end:
            loads[waited[0]].wait()
            waited[0] += 1

    def tile(block, c):
        half = block // HALF_BLOCKS
        row = half * HALF_ROWS + ((block - half * HALF_BLOCKS) * chunks + c) * 16
        return full[pl.ds(pl.multiple_of(row, 16), 16), :].astype(F32)

    stores = []
    for d, scale in enumerate((edge_scale, edge_scale, self_scale)):
        for k in range(3):
            group = per // 3
            need(d * per + (k + 1) * group)

            @pl.loop(k * group, (k + 1) * group)
            def _(i, d=d, scale=scale):
                for c in range(chunks):
                    w_out[d, pl.ds(pl.multiple_of(i * 16, 16), 16), c * 128 : (c + 1) * 128] = (
                        tile(d * per + i, c) * scale
                    )

            where = pl.ds(k * group * 16, group * 16)
            stores.append(
                pltpu.make_async_copy(w_out.at[d, where], w_hbm.at[d, where], out_sem.at[d * 3 + k])
            )
            stores[-1].start()

    whole = rels // 16
    need(W_BLOCKS + whole + 1)

    @pl.loop(0, whole)
    def _(i):
        for c in range(chunks):
            r_out[pl.ds(pl.multiple_of(i * 16, 16), 16), c * 128 : (c + 1) * 128] = (
                tile(W_BLOCKS + i, c) * rel_scale
            )

    rest = rels - whole * 16
    for c in range(chunks):
        last = tile(W_BLOCKS + whole, c)
        cols = slice(c * 128, (c + 1) * 128)
        if rest:
            r_out[whole * 16 : rels, cols] = last[:rest] * rel_scale
        l_out[cols] = (last[rest : rest + 1] * self_scale).reshape(128)
    while waited[0] < pieces:
        loads[waited[0]].wait()
        waited[0] += 1
    for store in stores:
        store.wait()


def unpack(full, rels, width, **scales):
    return pl.pallas_call(
        functools.partial(unpack_kernel, **scales),
        out_shape=(
            jax.ShapeDtypeStruct((3, width, width), F32),
            jax.ShapeDtypeStruct((rels, width), F32),
            jax.ShapeDtypeStruct((width,), F32),
        ),
        in_specs=[ANY],
        out_specs=[ANY, VMEM, VMEM],
        scratch_shapes=[
            pltpu.VMEM(full.shape, BF16),
            pltpu.VMEM((3, width, width), F32),
            DMA((11,)),
            DMA((9,)),
        ],
        compiler_params=pltpu.CompilerParams(vmem_limit_bytes=VMEM_BYTES),
        name="unpack",
    )(full)


def body(
    h_src, rel_table, cotangent, h_tgt, loop_rel, weights, src_index, tgt_index, rel_ids, direction, counts
):
    width = weights.shape[1]
    tiles, edge = src_index.shape[2:]
    rels = rel_table.shape[0]
    h_all, c_all, s8, t8, r8 = gather(
        h_src, cotangent, *[a.reshape(tiles, edge) for a in (src_index, tgt_index, rel_ids, direction)]
    )
    g, grad_tgt, keep, give = edges(
        counts.reshape(1), s8, t8, r8, h_all, c_all, weights, rel_table, cotangent, h_tgt, loop_rel
    )
    full, grad_src = reduce_all(keep, give, g)
    devices = lax.axis_size("src") * lax.axis_size("tgt")
    edges_all = float(devices * tiles * edge)
    targets_all = float(devices * cotangent.shape[0])
    grad_weights, grad_rel, grad_loop = unpack(
        full,
        rels,
        width,
        edge_scale=edges_all**-0.5,
        self_scale=targets_all**-0.5,
        rel_scale=(float(rels) / edges_all) ** 0.5,
    )
    return grad_src, grad_tgt, grad_weights, grad_rel, grad_loop


def solution(mesh):
    return jax.shard_map(
        body,
        mesh=mesh,
        in_specs=(
            P(("src", "tgt"), None),
            P(),
            P(("tgt", "src"), None),
            P(("tgt", "src"), None),
            P(),
            P(),
            P("src", "tgt", None, None),
            P("src", "tgt", None, None),
            P("src", "tgt", None, None),
            P("src", "tgt", None, None),
            P("src", "tgt"),
        ),
        out_specs=(P(("src", "tgt"), None), P(("tgt", "src"), None), P(), P(), P()),
        check_vma=False,
    )
```

```python
import functools

import jax
import jax.numpy as jnp
from jax import lax
from jax.experimental import pallas as pl
from jax.experimental.pallas import tpu as pltpu
from jax.sharding import PartitionSpec as P

F32 = jnp.float32
BF16 = jnp.bfloat16
MESH = pl.DeviceIdType.MESH
ANY = pl.BlockSpec(memory_space=pl.ANY)
VMEM = pl.BlockSpec(memory_space=pltpu.VMEM)
SMEM = pl.BlockSpec(memory_space=pltpu.SMEM)
DMA = pltpu.SemaphoreType.DMA

WAVE_HALF = (4096, 7168)
HALF_ROWS = sum(WAVE_HALF)
FIRST_TILES = 2 * WAVE_HALF[0] // 16
SECOND_HALF_TILES = WAVE_HALF[1] // 16
W_TILES = 864
PARTS = (
    (("x", "y", "z"), 32),
    (("y", "z", "x"), 32),
    (("x", "y", "z"), 32),
    (("y", "z", "x"), 32),
    (("z", "x", "y"), 48),
)
BASES = (0, 2048, 4096, 6144, 8192)
UNROLL = 16
EDGE = 128
VMEM_BYTES = 63 * 2**20


class Place:
    def __init__(self):
        s, t = lax.axis_index("src"), lax.axis_index("tgt")
        self.x_lo, self.core = s // 8, s % 2
        self.x_hi = t // 4
        self.at = {"x": self.x_hi * 2 + self.x_lo, "y": (s // 2) % 4, "z": t % 4}

    def device(self, at, core):
        return ((at["x"] % 2) * 8 + at["y"] * 2 + core, (at["x"] // 2) * 4 + at["z"])

    def along(self, axis, offset):
        at = dict(self.at)
        at[axis] = (at[axis] + offset) % 4
        return self.device(at, self.core)

    def sibling(self):
        return self.device(self.at, 1 - self.core)

    def x_lo_partner(self):
        at = dict(self.at)
        at["x"] = self.x_hi * 2 + (1 - self.x_lo)
        return self.device(at, self.core)


def greet(partners):
    barrier = pltpu.get_barrier_semaphore()
    for partner in partners:
        pl.semaphore_signal(barrier, inc=1, device_id=partner, device_id_type=MESH)
    pl.semaphore_wait(barrier, len(partners))


def push(src, dst, send, recv, device):
    return pltpu.make_async_remote_copy(
        src_ref=src, dst_ref=dst, send_sem=send, recv_sem=recv, device_id=device, device_id_type=MESH
    )


def gather_kernel(
    h_ref, c_ref, src_ref, tgt_ref, rel_ref, dir_ref, h_all, c_all, s8, t8, r8, local, hx_s, hx_r, hz_s, hz_r, cy_s, cy_r, cx_s, cx_r, cs_s, cs_r
):
    me = Place()
    x_lo, x_hi, core, y, z = me.x_lo, me.x_hi, me.core, me.at["y"], me.at["z"]
    sibling, across = me.sibling(), me.x_lo_partner()
    own_h = pltpu.make_async_copy(h_ref, h_all.at[x_hi, z], local.at[0])
    own_c = pltpu.make_async_copy(c_ref, c_all.at[x_lo, y, core], local.at[1])
    own_h.start()
    own_c.start()
    s8[...] = src_ref[...] * 8
    t8[...] = (tgt_ref[...] + dir_ref[...] * (16 * c_ref.shape[0])) * 8
    r8[...] = rel_ref[...] * 8
    greet(
        [me.along("x", 2), across, sibling]
        + [me.along("y", k) for k in (1, 2, 3)]
        + [me.along("z", k) for k in (1, 2, 3)]
    )
    mine, theirs = h_all.at[x_hi, z], h_all.at[1 - x_hi, z]
    hx = push(h_ref, mine, hx_s, hx_r, me.along("x", 2))
    hx.start()
    cy, hz = [], []
    for k in (1, 3, 2):
        copy = push(h_ref, mine, hz_s.at[k - 1], hz_r.at[k - 1], me.along("z", k))
        copy.start()
        hz.append(copy)
        copy = push(c_ref, c_all.at[x_lo, y, core], cy_s.at[k - 1], cy_r.at[k - 1], me.along("y", k))
        copy.start()
        cy.append(copy)
    hx.wait()
    for k in (1, 3, 2):
        copy = push(theirs, theirs, hz_s.at[k + 2], hz_r.at[k + 2], me.along("z", k))
        copy.start()
        hz.append(copy)
    own_c.wait()
    for copy in cy:
        copy.wait()
    near = c_all.at[x_lo, :, core]
    far = c_all.at[1 - x_lo, :, core]
    cx = push(near, near, cx_s, cx_r, across)
    cx.start()
    first = push(near, near, cs_s.at[0], cs_r.at[0], sibling)
    first.start()
    cx.wait()
    second = push(far, far, cs_s.at[1], cs_r.at[1], sibling)
    second.start()
    first.wait()
    second.wait()
    own_h.wait()
    for copy in hz:
        copy.wait()


def gather(h_src, cotangent, *indices):
    rows, width = h_src.shape
    trows = cotangent.shape[0]
    h_all, c_all, s8, t8, r8 = pl.pallas_call(
        gather_kernel,
        out_shape=(
            jax.ShapeDtypeStruct((2, 4, rows, width), BF16),
            jax.ShapeDtypeStruct((2, 4, 2, trows, width), BF16),
            *[jax.ShapeDtypeStruct(indices[0].shape, jnp.int32)] * 3,
        ),
        in_specs=[ANY] * 2 + [VMEM] * 4,
        out_specs=[ANY] * 2 + [VMEM] * 3,
        scratch_shapes=[
            DMA((2,)), DMA, DMA, DMA((6,)), DMA((6,)), DMA((3,)), DMA((3,)), DMA, DMA, DMA((2,)), DMA((2,)),
        ],
        compiler_params=pltpu.CompilerParams(collective_id=0, has_side_effects=True, vmem_limit_bytes=VMEM_BYTES),
        name="gather_panels",
    )(h_src, cotangent, *indices)
    flat = [a.reshape(-1) for a in (s8, t8, r8)]
    return h_all.reshape(8 * rows, width), c_all.reshape(16 * trows, width), *flat


def edge_kernel(
    live_ref, src_ref, tgt_ref, rel_ref, h_hbm, c_hbm, w_hbm, z_hbm, own_c, own_h, loop_ref,
    g_out, t_out, hi_out, lo_out, rest_out, keep_out, give_out,
    h_ref, c_ref, w_ref, z_ref, g_ref, keep, give, hx, px, zx, gs, aa, rr, hi, lo, in_sem, out_sem,
):
    loads = [
        pltpu.make_async_copy(a, b, in_sem.at[i])
        for i, (a, b) in enumerate(((h_hbm, h_ref), (z_hbm, z_ref), (c_hbm, c_ref), (w_hbm, w_ref)))
    ]
    for load in loads:
        load.start()
    core = lax.axis_index("src") % 2
    rows = h_ref.shape[0]
    trows = c_ref.shape[0]
    rels, width = z_ref.shape
    chunks = width // 128

    def spread(dst, row, value):
        for c in range(chunks):
            dst[pl.ds(row * 8 + c, value.shape[0], stride=8), :] = value[:, c * 128 : (c + 1) * 128]

    zero = jnp.zeros((64, 128), F32)
    for ref in (gs, aa, rr):

        @pl.loop(0, ref.shape[0] // 64)
        def _(i, ref=ref):
            ref[pl.ds(pl.multiple_of(i * 64, 64), 64), :] = zero

    loads[0].wait()

    @pl.loop(0, rows // 16)
    def _(i):
        r = pl.multiple_of(i * 16, 16)
        spread(hx, r, h_ref[pl.ds(r, 16), :].astype(F32))

    loads[1].wait()

    @pl.loop(0, rels // 16)
    def _(i):
        r = pl.multiple_of(i * 16, 16)
        spread(zx, r, z_ref[pl.ds(r, 16), :].astype(F32))

    tail = rels // 16 * 16
    if tail < rels:
        spread(zx, tail, z_ref[tail:rels, :].astype(F32))
    loads[2].wait()
    loads[3].wait()
    for d in range(2):
        for k in range(width // 256):
            p = lax.dot_general(
                c_ref[...], w_ref[d, k * 256 : (k + 1) * 256, :], (((1,), (1,)), ((), ())),
                preferred_element_type=F32,
            )
            for h in range(2):
                px[pl.ds(d * trows * 8 + 2 * k + h, trows, stride=8), :] = p[:, h * 128 : (h + 1) * 128]
    def row(at):
        return pl.ds(pl.multiple_of(at, 8), 8)

    @pl.loop(0, live_ref[0] * (EDGE // UNROLL))
    def _(i):
        start = i * UNROLL
        for u in range(0, UNROLL, 2):
            s0, s1 = src_ref[start + u], src_ref[start + u + 1]
            t0, t1 = tgt_ref[start + u], tgt_ref[start + u + 1]
            r0, r1 = rel_ref[start + u], rel_ref[start + u + 1]
            h0, h1 = hx[row(s0), :], hx[row(s1), :]
            p0, p1 = px[row(t0), :], px[row(t1), :]
            z0, z1 = zx[row(r0), :], zx[row(r1), :]
            for ref, at0, at1, v0, v1 in (
                (gs, s0, s1, p0 * z0, p1 * z1),
                (aa, t0, t1, (h0 * z0).astype(BF16).astype(F32), (h1 * z1).astype(BF16).astype(F32)),
                (rr, r0, r1, p0 * h0, p1 * h1),
            ):
                sum0 = ref[row(at0), :] + v0
                sum1 = ref[row(at1), :] + v1 + jnp.where(at0 == at1, v0, jnp.zeros_like(v0))
                ref[row(at0), :] = sum0
                ref[row(at1), :] = sum1

    loop_wide = loop_ref[...].astype(F32).reshape(1, width)
    h_wide = own_h[...].astype(F32)
    back = lax.dot_general(
        own_c[...], w_ref[2], (((1,), (1,)), ((), ())), preferred_element_type=F32
    )
    t_out[...] = back * loop_wide
    lsum = jnp.sum(back * h_wide, axis=0, keepdims=True)
    for c in range(chunks):
        rr[rels * 8 + c : rels * 8 + c + 1, :] = lsum[:, c * 128 : (c + 1) * 128]
    blocks = rr.shape[0] // 128

    def rel_tile(block, c):
        return rr[pl.ds(block * 128 + c, 16, stride=8), :]

    def collect(half, ref):
        first = half * (FIRST_TILES // 2)
        last = first + FIRST_TILES // 2

        @pl.loop(-(-first // chunks), last // chunks)
        def _(i):
            for c in range(chunks):
                row = pl.multiple_of((i * chunks + c - first) * 16, 16)
                ref[pl.ds(row, 16), :] = rel_tile(i, c).astype(ref.dtype)

        edge_tiles = [*range(first, -(-first // chunks) * chunks), *range(last // chunks * chunks, last)]
        for t in edge_tiles:
            row = (t - first) * 16
            ref[row : row + 16, :] = rel_tile(t // chunks, t % chunks).astype(ref.dtype)

    @pl.when(core == 0)
    def _():
        collect(0, keep)
        collect(1, give)

    @pl.when(core != 0)
    def _():
        collect(1, keep)
        collect(0, give)

    stores = [
        pltpu.make_async_copy(keep, keep_out, out_sem.at[0]),
        pltpu.make_async_copy(give, give_out, out_sem.at[1]),
    ]
    for store in stores:
        store.start()
    for t in range(FIRST_TILES, blocks * chunks):
        row = (t - FIRST_TILES) * 16
        rest_out[row : row + 16, :] = rel_tile(t // chunks, t % chunks)

    @pl.loop(0, 2 * trows // 16)
    def _(i):
        r = pl.multiple_of(i * 16, 16)
        for c in range(chunks):
            a = aa[pl.ds(r * 8 + c, 16, stride=8), :]
            top = a.astype(BF16)
            hi[pl.ds(r, 16), c * 128 : (c + 1) * 128] = top
            lo[pl.ds(r, 16), c * 128 : (c + 1) * 128] = (a - top.astype(F32)).astype(BF16)

    stores.append(pltpu.make_async_copy(hi, hi_out, out_sem.at[2]))
    stores.append(pltpu.make_async_copy(lo, lo_out, out_sem.at[3]))
    stores[2].start()
    stores[3].start()

    @pl.loop(0, rows // 16)
    def _(i):
        r = pl.multiple_of(i * 16, 16)
        for c in range(chunks):
            g_ref[pl.ds(r, 16), c * 128 : (c + 1) * 128] = gs[pl.ds(r * 8 + c, 16, stride=8), :].astype(BF16)

    stores.append(pltpu.make_async_copy(g_ref, g_out, out_sem.at[4]))
    stores[4].start()
    for store in stores:
        store.wait()


def edges(live, s8, t8, r8, h, c, w, z, own_c, own_h, loop):
    rows, width = h.shape
    trows = c.shape[0]
    rpad = (z.shape[0] + 16) // 16 * 16
    return pl.pallas_call(
        edge_kernel,
        out_shape=(
            jax.ShapeDtypeStruct((rows, width), BF16),
            jax.ShapeDtypeStruct((own_c.shape[0], width), F32),
            jax.ShapeDtypeStruct((2 * trows, width), BF16),
            jax.ShapeDtypeStruct((2 * trows, width), BF16),
            jax.ShapeDtypeStruct((rpad // 16 * (width // 128) * 16 - FIRST_TILES * 16, 128), F32),
            jax.ShapeDtypeStruct((WAVE_HALF[0], 128), F32),
            jax.ShapeDtypeStruct((WAVE_HALF[0], 128), BF16),
        ),
        in_specs=[SMEM] * 4 + [ANY] * 4 + [VMEM] * 3,
        out_specs=[ANY, VMEM, ANY, ANY, VMEM, ANY, ANY],
        scratch_shapes=[
            pltpu.VMEM(h.shape, BF16),
            pltpu.VMEM(c.shape, BF16),
            pltpu.VMEM(w.shape, BF16),
            pltpu.VMEM(z.shape, BF16),
            pltpu.VMEM((rows, width), BF16),
            pltpu.VMEM((WAVE_HALF[0], 128), F32),
            pltpu.VMEM((WAVE_HALF[0], 128), BF16),
            pltpu.VMEM((rows * 8, 128), F32),
            pltpu.VMEM((2 * trows * 8, 128), F32),
            pltpu.VMEM((rpad * 8, 128), F32),
            pltpu.VMEM((rows * 8, 128), F32),
            pltpu.VMEM((2 * trows * 8, 128), F32),
            pltpu.VMEM((rpad * 8, 128), F32),
            pltpu.VMEM((2 * trows, width), BF16),
            pltpu.VMEM((2 * trows, width), BF16),
            DMA((4,)),
            DMA((5,)),
        ],
        compiler_params=pltpu.CompilerParams(vmem_limit_bytes=VMEM_BYTES),
        name="edges",
    )(live, s8, t8, r8, h, c, w, z, own_c, own_h, loop)


def reduce_kernel(
    keep_hbm, give, g_ref, hi_hbm, lo_hbm, c_hbm, rest, own_c, own_h, loop_ref, full, g_out,
    keep, given, hi, lo, c_all, g_own, pair, out1, in1, acc1, in2, acc2, in3, unit, g_in, g_acc, g_side,
    pair_s, pair_r, s1, r1, s2, r2, s3, r3, s4, r4, s5, r5, s6, r6, sib_s, sib_r, gz_s, gz_r, gx_s, gx_r,
    local, kept,
):
    me = Place()
    core = me.core
    sibling = me.sibling()
    x_hi, z = me.x_hi, me.at["z"]
    width = c_all.shape[1]
    trows = c_all.shape[0]
    chunks = width // 128
    parts = range(len(PARTS))

    def at(p, depth):
        return me.at[PARTS[p][0][depth]]

    def along(p, depth, j):
        return me.along(PARTS[p][0][depth], j)

    def rows_of(p, a):
        size = PARTS[p][1] * 16
        return pl.ds(pl.multiple_of(BASES[p] + a * size, 16), size)

    first_rows = pl.ds(0, WAVE_HALF[0])
    loads = [
        pltpu.make_async_copy(a, b, kept.at[n])
        for n, (a, b) in enumerate(
            (
                (keep_hbm, keep.at[first_rows]),
                (hi_hbm, hi),
                (c_hbm, c_all),
                (lo_hbm, lo),
                (g_ref.at[:, z], g_own),
            )
        )
    ]
    for load in loads:
        load.start()
    greet([me.along(axis, k) for axis in ("x", "y", "z") for k in (1, 2, 3)] + [sibling])

    pairs, step1, step2, step3, step4, step5, step6, side, own = {}, {}, {}, {}, {}, {}, {}, {}, {}

    def send_pair(some):
        for j in (1, 2, 3, 0):
            for p in some:
                where = rows_of(p, (at(p, 0) + j) % 4)
                if BASES[p] < WAVE_HALF[0]:
                    source = give.at[where]
                else:
                    row = BASES[p] - WAVE_HALF[0] + ((at(p, 0) + j) % 4) * (PARTS[p][1] * 16)
                    source = given.at[pl.ds(pl.multiple_of(row, 16), PARTS[p][1] * 16)]
                copy = push(source, pair.at[where], pair_s.at[p * 4 + j], pair_r.at[p * 4 + j], sibling)
                copy.start()
                pairs[p, j] = copy

    def send_first(some):
        for j in (1, 2, 3):
            for p in some:
                size = PARTS[p][1] * 16
                base = BASES[p] + ((at(p, 0) + j) % 4) * size
                pairs[p, j].wait_recv()

                @pl.loop(0, size // 128)
                def _(i, base=base):
                    r = pl.ds(pl.multiple_of(base + i * 128, 16), 128)
                    out1[r, :] = (keep[r, :] + pair[r, :].astype(F32)).astype(BF16)

                copy = push(
                    out1.at[rows_of(p, (at(p, 0) + j) % 4)],
                    in1.at[j - 1, pl.ds(BASES[p] // 4, size)],
                    s1.at[p * 3 + j - 1],
                    r1.at[p * 3 + j - 1],
                    along(p, 0, j),
                )
                copy.start()
                step1[p, j] = copy

    def send_second(p):
        size = PARTS[p][1] * 4
        base = BASES[p] + at(p, 0) * (size * 4)
        low = BASES[p] // 4
        pairs[p, 0].wait_recv()
        for j in (1, 2, 3):
            step1[p, j].wait_recv()

        @pl.loop(0, size * 4 // 128)
        def _(i):
            r = pl.ds(pl.multiple_of(base + i * 128, 16), 128)
            q = pl.ds(pl.multiple_of(low + i * 128, 16), 128)
            acc1[q, :] = (
                keep[r, :]
                + pair[r, :].astype(F32)
                + in1[0, q, :].astype(F32)
                + in1[1, q, :].astype(F32)
                + in1[2, q, :].astype(F32)
            )

        for j in (1, 2, 3):
            where = pl.ds(pl.multiple_of(low + ((at(p, 1) + j) % 4) * size, 16), size)
            copy = push(
                acc1.at[where],
                in2.at[j - 1, pl.ds(BASES[p] // 16, size)],
                s2.at[p * 3 + j - 1],
                r2.at[p * 3 + j - 1],
                along(p, 1, j),
            )
            copy.start()
            step2[p, j] = copy

    def send_third(p):
        size = PARTS[p][1]
        for j in (1, 2, 3):
            step2[p, j].wait_recv()
        q = pl.ds(BASES[p] // 16, size * 4)
        mine = pl.ds(pl.multiple_of(BASES[p] // 4 + at(p, 1) * (size * 4), 16), size * 4)
        acc2[q, :] = acc1[mine, :] + in2[0, q, :] + in2[1, q, :] + in2[2, q, :]
        for j in (1, 2, 3):
            where = pl.ds(pl.multiple_of(BASES[p] // 16 + ((at(p, 2) + j) % 4) * size, 16), size)
            copy = push(
                acc2.at[where],
                in3.at[j - 1, pl.ds(BASES[p] // 64, size)],
                s3.at[p * 3 + j - 1],
                r3.at[p * 3 + j - 1],
                along(p, 2, j),
            )
            copy.start()
            step3[p, j] = copy

    def start_of(p):
        if BASES[p] < WAVE_HALF[0]:
            return core * WAVE_HALF[0] + BASES[p]
        return 2 * WAVE_HALF[0] + core * WAVE_HALF[1] + (BASES[p] - WAVE_HALF[0])

    def place(p, depth):
        size = PARTS[p][1]
        row = start_of(p) + at(p, 0) * (size * 16)
        if depth > 1:
            row = row + at(p, 1) * (size * 4)
        if depth > 2:
            row = row + at(p, 2) * size
        return full.at[pl.ds(pl.multiple_of(row, 16), (size * 16, size * 4, size)[depth - 1])]

    def half_of(p, offset, half):
        size = PARTS[p][1] * 8
        row = start_of(p) + ((at(p, 0) + 4 + offset) % 4) * (2 * size) + half * size
        return full.at[pl.ds(pl.multiple_of(row, 16), size)]

    def share_third(p):
        size = PARTS[p][1]
        for j in (1, 2, 3):
            step3[p, j].wait_recv()
        q = pl.ds(BASES[p] // 64, size)
        mine = pl.ds(pl.multiple_of(BASES[p] // 16 + at(p, 2) * size, 16), size)
        unit[q, :] = (acc2[mine, :] + in3[0, q, :] + in3[1, q, :] + in3[2, q, :]).astype(BF16)
        own[p] = pltpu.make_async_copy(unit.at[q], place(p, 3), local.at[p])
        own[p].start()
        for j in (1, 2, 3):
            copy = push(unit.at[q], place(p, 3), s4.at[p * 3 + j - 1], r4.at[p * 3 + j - 1], along(p, 2, j))
            copy.start()
            step4[p, j] = copy

    def share_second(p):
        own[p].wait()
        for j in (1, 2, 3):
            step4[p, j].wait_recv()
        for j in (1, 2, 3):
            block = place(p, 2)
            copy = push(block, block, s5.at[p * 3 + j - 1], r5.at[p * 3 + j - 1], along(p, 1, j))
            copy.start()
            step5[p, j] = copy

    def to_other_core(p, n, block):
        side[p, n] = push(block, block, sib_s.at[p * 7 + n], sib_r.at[p * 7 + n], sibling)
        side[p, n].start()

    def share_first(p):
        for j in (1, 2, 3):
            step5[p, j].wait_recv()
        for n, (to, half) in enumerate(((1, 0), (3, 1), (1, 1), (3, 0))):
            block = half_of(p, 0, half)
            copy = push(block, block, s6.at[p * 6 + n], r6.at[p * 6 + n], along(p, 0, to))
            copy.start()
            step6[p, n] = copy
        to_other_core(p, 0, place(p, 1))

    def forward(p):
        for n, (to, half) in enumerate(((1, 0), (3, 1))):
            step6[p, n].wait_recv()
            block = half_of(p, -to, half)
            copy = push(block, block, s6.at[p * 6 + 4 + n], r6.at[p * 6 + 4 + n], along(p, 0, to))
            copy.start()
            step6[p, 4 + n] = copy
            to_other_core(p, 1 + n, block)

    def finish(p):
        for n, (to, half) in enumerate(((1, 1), (3, 0))):
            step6[p, 2 + n].wait_recv()
            to_other_core(p, 3 + n, half_of(p, -to, half))
        for half in range(2):
            step6[p, 4 + half].wait_recv()
            to_other_core(p, 5 + half, half_of(p, 2, half))

    def put(first, value):
        here = value.shape[0] // 16 * chunks
        for half in range(2):
            begin = max(first, half * SECOND_HALF_TILES)
            end = min(first + here, (half + 1) * SECOND_HALF_TILES)
            if begin >= end:
                continue

            def store(ref, base, half=half, begin=begin, end=end):
                for t in range(begin, end):
                    row = base + (t - half * SECOND_HALF_TILES) * 16
                    b, c = (t - first) // chunks, (t - first) % chunks
                    ref[row : row + 16, :] = value[b * 16 : b * 16 + 16, c * 128 : c * 128 + 128].astype(ref.dtype)

            @pl.when(core == half)
            def _(store=store):
                store(keep, WAVE_HALF[0])

            @pl.when(core != half)
            def _(store=store):
                store(given, 0)

    def make_wsum(d):
        rows = slice(d * trows, (d + 1) * trows)
        for k in range(width // 256):
            cols = slice(k * 256, (k + 1) * 256)
            w = lax.dot_general(
                hi[rows, cols], c_all[...], (((0,), (0,)), ((), ())), preferred_element_type=F32
            ) + lax.dot_general(
                lo[rows, cols], c_all[...], (((0,), (0,)), ((), ())), preferred_element_type=F32
            )
            put((d * 48 + k * 16) * chunks, w)

    def make_wself():
        self_comp = (own_h[...].astype(F32) * loop_ref[...].astype(F32).reshape(1, width)).astype(BF16)
        for k in range(width // 256):
            w = lax.dot_general(
                self_comp[:, k * 256 : (k + 1) * 256], own_c[...], (((0,), (0,)), ((), ())),
                preferred_element_type=F32,
            )
            put((96 + k * 16) * chunks, w)
        low = (W_TILES - SECOND_HALF_TILES) * 16
        n = rest.shape[0]

        def store(ref, base):
            ref[base + low : base + low + n, :] = rest[...].astype(ref.dtype)
            ref[base + low + n : base + WAVE_HALF[1], :] = jnp.zeros((WAVE_HALF[1] - low - n, 128), ref.dtype)

        @pl.when(core == 1)
        def _():
            store(keep, WAVE_HALF[0])

        @pl.when(core != 1)
        def _():
            store(given, 0)

    send_pair((0, 1))
    gz = []
    for k in (1, 3, 2):
        copy = push(g_ref.at[:, (z + k) % 4], g_in.at[k - 1], gz_s.at[k - 1], gz_r.at[k - 1], me.along("z", k))
        copy.start()
        gz.append(copy)
    loads[0].wait()
    send_first((0, 1))
    for load in loads[1:]:
        load.wait()
    make_wsum(0)
    make_wsum(1)
    send_pair((2,))
    send_second(0)
    send_second(1)
    make_wself()
    send_pair((3, 4))
    send_first((2,))
    send_third(0)
    send_third(1)
    send_first((3, 4))
    for copy in gz:
        copy.wait_recv()
    for half in range(2):
        g_acc[half] = (
            g_own[half].astype(F32)
            + g_in[0, half].astype(F32)
            + g_in[1, half].astype(F32)
            + g_in[2, half].astype(F32)
        )
    gx = push(g_acc.at[1 - x_hi], g_side, gx_s, gx_r, me.along("x", 2))
    gx.start()
    share_third(0)
    share_third(1)
    send_second(2)
    share_second(0)
    share_second(1)
    send_second(3)
    send_second(4)
    share_first(0)
    share_first(1)
    send_third(2)
    send_third(3)
    send_third(4)
    forward(0)
    forward(1)
    for p in (2, 3, 4):
        share_third(p)
    finish(0)
    finish(1)
    for p in (2, 3, 4):
        share_second(p)
    for p in (2, 3, 4):
        share_first(p)
    gx.wait_recv()
    g_out[...] = g_acc[x_hi] + g_side[...]
    for p in (2, 3, 4):
        forward(p)
    for p in (2, 3, 4):
        finish(p)

    for copy in side.values():
        copy.wait_recv()
    gx.wait_send()
    for copy in gz:
        copy.wait_send()
    for group in (pairs, step1, step2, step3, step4, step5, step6, side):
        for copy in group.values():
            copy.wait_send()


def reduce_all(keep, give, g, hi, lo, c_all, rest, own_c, own_h, loop):
    rows, width = g.shape
    g = g.reshape(2, 4, rows // 8, width)
    n = len(PARTS)
    return pl.pallas_call(
        reduce_kernel,
        out_shape=(
            jax.ShapeDtypeStruct((2 * HALF_ROWS, 128), BF16),
            jax.ShapeDtypeStruct((rows // 8, width), F32),
        ),
        in_specs=[ANY] * 6 + [VMEM] * 4,
        out_specs=[ANY, VMEM],
        scratch_shapes=[
            pltpu.VMEM((HALF_ROWS, 128), F32),
            pltpu.VMEM((WAVE_HALF[1], 128), BF16),
            pltpu.VMEM(hi.shape, BF16),
            pltpu.VMEM(lo.shape, BF16),
            pltpu.VMEM(c_all.shape, BF16),
            pltpu.VMEM((2, rows // 8, width), BF16),
            pltpu.VMEM((HALF_ROWS, 128), BF16),
            pltpu.VMEM((HALF_ROWS, 128), BF16),
            pltpu.VMEM((3, HALF_ROWS // 4, 128), BF16),
            pltpu.VMEM((HALF_ROWS // 4, 128), F32),
            pltpu.VMEM((3, HALF_ROWS // 16, 128), F32),
            pltpu.VMEM((HALF_ROWS // 16, 128), F32),
            pltpu.VMEM((3, HALF_ROWS // 64, 128), F32),
            pltpu.VMEM((HALF_ROWS // 64, 128), BF16),
            pltpu.VMEM((3, 2, rows // 8, width), BF16),
            pltpu.VMEM((2, rows // 8, width), F32),
            pltpu.VMEM((rows // 8, width), F32),
            *[DMA((4 * n,))] * 2, *[DMA((3 * n,))] * 10, *[DMA((6 * n,))] * 2, *[DMA((7 * n,))] * 2,
            DMA((3,)), DMA((3,)), DMA, DMA, DMA((n,)), DMA((5,)),
        ],
        compiler_params=pltpu.CompilerParams(
            collective_id=1, has_side_effects=True, vmem_limit_bytes=VMEM_BYTES
        ),
        name="reduce_all",
    )(keep, give, g, hi, lo, c_all, rest, own_c, own_h, loop)


def unpack_kernel(
    full_hbm, w_hbm, r_out, l_out, full, w_out, in_sem, out_sem, *, edge_scale, self_scale, rel_scale
):
    rels, width = r_out.shape
    chunks = width // 128
    per = width // 16
    pieces = in_sem.shape[0]
    size = full.shape[0] // pieces
    loads = []
    for i in range(pieces):
        where = pl.ds(i * size, size)
        loads.append(pltpu.make_async_copy(full_hbm.at[where], full.at[where], in_sem.at[i]))
        loads[-1].start()
    waited = []

    def need(first, last):
        for i in range(first // size, -(-last // size)):
            if i not in waited:
                waited.append(i)
                loads[i].wait()

    def tile(first, index):
        return full[pl.ds(pl.multiple_of(first + index * 16, 16), 16), :].astype(F32)

    w_first = 2 * WAVE_HALF[0]
    rest_first = w_first + W_TILES * 16
    stores = []
    for d, scale in enumerate((edge_scale, edge_scale, self_scale)):
        for k in range(3):
            group = per // 3
            need(w_first, w_first + (d * per + (k + 1) * group) * chunks * 16)

            @pl.loop(k * group, (k + 1) * group)
            def _(i, d=d, scale=scale):
                for c in range(chunks):
                    w_out[d, pl.ds(pl.multiple_of(i * 16, 16), 16), c * 128 : (c + 1) * 128] = (
                        tile(w_first, (d * per + i) * chunks + c) * scale
                    )

            where = pl.ds(k * group * 16, group * 16)
            stores.append(
                pltpu.make_async_copy(w_out.at[d, where], w_hbm.at[d, where], out_sem.at[d * 3 + k])
            )
            stores[-1].start()

    need(0, full.shape[0])
    whole = FIRST_TILES // chunks

    @pl.loop(0, whole)
    def _(i):
        for c in range(chunks):
            r_out[pl.ds(pl.multiple_of(i * 16, 16), 16), c * 128 : (c + 1) * 128] = (
                tile(0, i * chunks + c) * rel_scale
            )

    for t in range(whole * chunks, -(-(rels + 1) // 16) * chunks):
        b, cols = t // chunks, slice(t % chunks * 128, t % chunks * 128 + 128)
        last = tile(0, t) if t < FIRST_TILES else tile(rest_first, t - FIRST_TILES)
        n = min(16, rels - b * 16)
        if n:
            r_out[b * 16 : b * 16 + n, cols] = last[:n] * rel_scale
        if n < 16:
            l_out[cols] = (last[n : n + 1] * self_scale).reshape(128)
    for store in stores:
        store.wait()


def unpack(full, rels, width, **scales):
    return pl.pallas_call(
        functools.partial(unpack_kernel, **scales),
        out_shape=(
            jax.ShapeDtypeStruct((3, width, width), F32),
            jax.ShapeDtypeStruct((rels, width), F32),
            jax.ShapeDtypeStruct((width,), F32),
        ),
        in_specs=[ANY],
        out_specs=[ANY, VMEM, VMEM],
        scratch_shapes=[
            pltpu.VMEM(full.shape, BF16),
            pltpu.VMEM((3, width, width), F32),
            DMA((11,)),
            DMA((9,)),
        ],
        compiler_params=pltpu.CompilerParams(vmem_limit_bytes=VMEM_BYTES),
        name="unpack",
    )(full)


def body(
    h_src, rel_table, cotangent, h_tgt, loop_rel, weights, src_index, tgt_index, rel_ids, direction, counts
):
    width = weights.shape[1]
    tiles, edge = src_index.shape[2:]
    rels = rel_table.shape[0]
    h_all, c_all, s8, t8, r8 = gather(
        h_src, cotangent, *[a.reshape(tiles, edge) for a in (src_index, tgt_index, rel_ids, direction)]
    )
    g, grad_tgt, hi, lo, rest, keep, give = edges(
        counts.reshape(1), s8, t8, r8, h_all, c_all, weights, rel_table, cotangent, h_tgt, loop_rel
    )
    full, grad_src = reduce_all(
        keep, give, g, hi, lo, c_all, rest, cotangent, h_tgt, loop_rel
    )
    devices = lax.axis_size("src") * lax.axis_size("tgt")
    edges_all = float(devices * tiles * edge)
    targets_all = float(devices * cotangent.shape[0])
    grad_weights, grad_rel, grad_loop = unpack(
        full,
        rels,
        width,
        edge_scale=edges_all**-0.5,
        self_scale=targets_all**-0.5,
        rel_scale=(float(rels) / edges_all) ** 0.5,
    )
    return grad_src, grad_tgt, grad_weights, grad_rel, grad_loop


def solution(mesh):
    return jax.shard_map(
        body,
        mesh=mesh,
        in_specs=(
            P(("src", "tgt"), None),
            P(),
            P(("tgt", "src"), None),
            P(("tgt", "src"), None),
            P(),
            P(),
            P("src", "tgt", None, None),
            P("src", "tgt", None, None),
            P("src", "tgt", None, None),
            P("src", "tgt", None, None),
            P("src", "tgt"),
        ),
        out_specs=(P(("src", "tgt"), None), P(("tgt", "src"), None), P(), P(), P()),
        check_vma=False,
    )
```

```python
import functools

import jax
import jax.numpy as jnp
from jax import lax
from jax.experimental import pallas as pl
from jax.experimental.pallas import tpu as pltpu
from jax.sharding import PartitionSpec as P

F32 = jnp.float32
BF16 = jnp.bfloat16
MESH = pl.DeviceIdType.MESH
ANY = pl.BlockSpec(memory_space=pl.ANY)
VMEM = pl.BlockSpec(memory_space=pltpu.VMEM)
SMEM = pl.BlockSpec(memory_space=pltpu.SMEM)
DMA = pltpu.SemaphoreType.DMA

WAVE_HALF = (4096, 7168)
HALF_ROWS = sum(WAVE_HALF)
FIRST_TILES = 2 * WAVE_HALF[0] // 16
SECOND_HALF_TILES = WAVE_HALF[1] // 16
W_TILES = 864
PARTS = (
    (("x", "y", "z"), 32),
    (("y", "z", "x"), 32),
    (("x", "y", "z"), 32),
    (("y", "z", "x"), 32),
    (("z", "x", "y"), 48),
)
BASES = (0, 2048, 4096, 6144, 8192)
UNROLL = 16
EDGE = 128
VMEM_BYTES = 63 * 2**20


class Place:
    def __init__(self):
        s, t = lax.axis_index("src"), lax.axis_index("tgt")
        self.x_lo, self.core = s // 8, s % 2
        self.x_hi = t // 4
        self.at = {"x": self.x_hi * 2 + self.x_lo, "y": (s // 2) % 4, "z": t % 4}

    def device(self, at, core):
        return ((at["x"] % 2) * 8 + at["y"] * 2 + core, (at["x"] // 2) * 4 + at["z"])

    def along(self, axis, offset):
        at = dict(self.at)
        at[axis] = (at[axis] + offset) % 4
        return self.device(at, self.core)

    def sibling(self):
        return self.device(self.at, 1 - self.core)

    def x_lo_partner(self):
        at = dict(self.at)
        at["x"] = self.x_hi * 2 + (1 - self.x_lo)
        return self.device(at, self.core)


def greet(partners):
    barrier = pltpu.get_barrier_semaphore()
    for partner in partners:
        pl.semaphore_signal(barrier, inc=1, device_id=partner, device_id_type=MESH)
    pl.semaphore_wait(barrier, len(partners))


def push(src, dst, send, recv, device):
    return pltpu.make_async_remote_copy(
        src_ref=src, dst_ref=dst, send_sem=send, recv_sem=recv, device_id=device, device_id_type=MESH
    )


def gather_kernel(
    h_ref, c_ref, src_ref, tgt_ref, rel_ref, dir_ref, h_all, c_all, s8, t8, r8, local, hx_s, hx_r, hz_s, hz_r, cy_s, cy_r, cx_s, cx_r, cs_s, cs_r
):
    me = Place()
    x_lo, x_hi, core, y, z = me.x_lo, me.x_hi, me.core, me.at["y"], me.at["z"]
    sibling, across = me.sibling(), me.x_lo_partner()
    own_h = pltpu.make_async_copy(h_ref, h_all.at[x_hi, z], local.at[0])
    own_c = pltpu.make_async_copy(c_ref, c_all.at[x_lo, y, core], local.at[1])
    own_h.start()
    own_c.start()
    s8[...] = src_ref[...] * 8
    t8[...] = (tgt_ref[...] + dir_ref[...] * (16 * c_ref.shape[0])) * 8
    r8[...] = rel_ref[...] * 8
    greet(
        [me.along("x", 2), across, sibling]
        + [me.along("y", k) for k in (1, 2, 3)]
        + [me.along("z", k) for k in (1, 2, 3)]
    )
    mine, theirs = h_all.at[x_hi, z], h_all.at[1 - x_hi, z]
    hx = push(h_ref, mine, hx_s, hx_r, me.along("x", 2))
    hx.start()
    cy, hz = [], []
    for k in (1, 3, 2):
        copy = push(h_ref, mine, hz_s.at[k - 1], hz_r.at[k - 1], me.along("z", k))
        copy.start()
        hz.append(copy)
        copy = push(c_ref, c_all.at[x_lo, y, core], cy_s.at[k - 1], cy_r.at[k - 1], me.along("y", k))
        copy.start()
        cy.append(copy)
    hx.wait()
    for k in (1, 3, 2):
        copy = push(theirs, theirs, hz_s.at[k + 2], hz_r.at[k + 2], me.along("z", k))
        copy.start()
        hz.append(copy)
    own_c.wait()
    for copy in cy:
        copy.wait()
    near = c_all.at[x_lo, :, core]
    far = c_all.at[1 - x_lo, :, core]
    cx = push(near, near, cx_s, cx_r, across)
    cx.start()
    first = push(near, near, cs_s.at[0], cs_r.at[0], sibling)
    first.start()
    cx.wait()
    second = push(far, far, cs_s.at[1], cs_r.at[1], sibling)
    second.start()
    first.wait()
    second.wait()
    own_h.wait()
    for copy in hz:
        copy.wait()


def gather(h_src, cotangent, *indices):
    rows, width = h_src.shape
    trows = cotangent.shape[0]
    h_all, c_all, s8, t8, r8 = pl.pallas_call(
        gather_kernel,
        out_shape=(
            jax.ShapeDtypeStruct((2, 4, rows, width), BF16),
            jax.ShapeDtypeStruct((2, 4, 2, trows, width), BF16),
            *[jax.ShapeDtypeStruct(indices[0].shape, jnp.int32)] * 3,
        ),
        in_specs=[ANY] * 2 + [VMEM] * 4,
        out_specs=[ANY] * 2 + [VMEM] * 3,
        scratch_shapes=[
            DMA((2,)), DMA, DMA, DMA((6,)), DMA((6,)), DMA((3,)), DMA((3,)), DMA, DMA, DMA((2,)), DMA((2,)),
        ],
        compiler_params=pltpu.CompilerParams(collective_id=0, has_side_effects=True, vmem_limit_bytes=VMEM_BYTES),
        name="gather_panels",
    )(h_src, cotangent, *indices)
    flat = [a.reshape(-1) for a in (s8, t8, r8)]
    return h_all.reshape(8 * rows, width), c_all.reshape(16 * trows, width), *flat


def edge_kernel(
    live_ref, src_ref, tgt_ref, rel_ref, h_hbm, c_hbm, w_hbm, z_hbm, own_c, own_h, loop_ref,
    g_out, t_out, hi_out, lo_out, rest_out, keep_out, give_out,
    h_ref, c_ref, w_ref, z_ref, g_ref, keep, give, hx, px, zx, gs, aa, rr, hi, lo, in_sem, out_sem,
):
    loads = [
        pltpu.make_async_copy(a, b, in_sem.at[i])
        for i, (a, b) in enumerate(((h_hbm, h_ref), (z_hbm, z_ref), (c_hbm, c_ref), (w_hbm, w_ref)))
    ]
    for load in loads:
        load.start()
    core = lax.axis_index("src") % 2
    rows = h_ref.shape[0]
    trows = c_ref.shape[0]
    rels, width = z_ref.shape
    chunks = width // 128

    def spread(dst, row, value):
        for c in range(chunks):
            dst[pl.ds(row * 8 + c, value.shape[0], stride=8), :] = value[:, c * 128 : (c + 1) * 128]

    zero = jnp.zeros((64, 128), F32)
    for ref in (gs, aa, rr):

        @pl.loop(0, ref.shape[0] // 64)
        def _(i, ref=ref):
            ref[pl.ds(pl.multiple_of(i * 64, 64), 64), :] = zero

    loads[0].wait()

    @pl.loop(0, rows // 16)
    def _(i):
        r = pl.multiple_of(i * 16, 16)
        spread(hx, r, h_ref[pl.ds(r, 16), :].astype(F32))

    loads[1].wait()

    @pl.loop(0, rels // 16)
    def _(i):
        r = pl.multiple_of(i * 16, 16)
        spread(zx, r, z_ref[pl.ds(r, 16), :].astype(F32))

    tail = rels // 16 * 16
    if tail < rels:
        spread(zx, tail, z_ref[tail:rels, :].astype(F32))
    loads[2].wait()
    loads[3].wait()
    for d in range(2):
        for k in range(width // 256):
            p = lax.dot_general(
                c_ref[...], w_ref[d, k * 256 : (k + 1) * 256, :], (((1,), (1,)), ((), ())),
                preferred_element_type=F32,
            )
            for h in range(2):
                px[pl.ds(d * trows * 8 + 2 * k + h, trows, stride=8), :] = p[:, h * 128 : (h + 1) * 128]
    def row(at):
        return pl.ds(pl.multiple_of(at, 8), 8)

    @pl.loop(0, live_ref[0] * (EDGE // UNROLL))
    def _(i):
        start = i * UNROLL
        for u in range(0, UNROLL, 2):
            s0, s1 = src_ref[start + u], src_ref[start + u + 1]
            t0, t1 = tgt_ref[start + u], tgt_ref[start + u + 1]
            r0, r1 = rel_ref[start + u], rel_ref[start + u + 1]
            h0, h1 = hx[row(s0), :], hx[row(s1), :]
            p0, p1 = px[row(t0), :], px[row(t1), :]
            z0, z1 = zx[row(r0), :], zx[row(r1), :]
            for ref, at0, at1, v0, v1 in (
                (gs, s0, s1, p0 * z0, p1 * z1),
                (aa, t0, t1, (h0 * z0).astype(BF16).astype(F32), (h1 * z1).astype(BF16).astype(F32)),
                (rr, r0, r1, p0 * h0, p1 * h1),
            ):
                sum0 = ref[row(at0), :] + v0
                sum1 = ref[row(at1), :] + v1 + jnp.where(at0 == at1, v0, jnp.zeros_like(v0))
                ref[row(at0), :] = sum0
                ref[row(at1), :] = sum1

    loop_wide = loop_ref[...].astype(F32).reshape(1, width)
    h_wide = own_h[...].astype(F32)
    back = lax.dot_general(
        own_c[...], w_ref[2], (((1,), (1,)), ((), ())), preferred_element_type=F32
    )
    t_out[...] = back * loop_wide
    lsum = jnp.sum(back * h_wide, axis=0, keepdims=True)
    for c in range(chunks):
        rr[rels * 8 + c : rels * 8 + c + 1, :] = lsum[:, c * 128 : (c + 1) * 128]
    blocks = rr.shape[0] // 128

    def rel_tile(block, c):
        return rr[pl.ds(block * 128 + c, 16, stride=8), :]

    def collect(half, ref):
        first = half * (FIRST_TILES // 2)
        last = first + FIRST_TILES // 2

        @pl.loop(-(-first // chunks), last // chunks)
        def _(i):
            for c in range(chunks):
                row = pl.multiple_of((i * chunks + c - first) * 16, 16)
                ref[pl.ds(row, 16), :] = rel_tile(i, c).astype(ref.dtype)

        edge_tiles = [*range(first, -(-first // chunks) * chunks), *range(last // chunks * chunks, last)]
        for t in edge_tiles:
            row = (t - first) * 16
            ref[row : row + 16, :] = rel_tile(t // chunks, t % chunks).astype(ref.dtype)

    @pl.when(core == 0)
    def _():
        collect(0, keep)
        collect(1, give)

    @pl.when(core != 0)
    def _():
        collect(1, keep)
        collect(0, give)

    stores = [
        pltpu.make_async_copy(keep, keep_out, out_sem.at[0]),
        pltpu.make_async_copy(give, give_out, out_sem.at[1]),
    ]
    for store in stores:
        store.start()
    for t in range(FIRST_TILES, blocks * chunks):
        row = (t - FIRST_TILES) * 16
        rest_out[row : row + 16, :] = rel_tile(t // chunks, t % chunks)

    @pl.loop(0, 2 * trows // 16)
    def _(i):
        r = pl.multiple_of(i * 16, 16)
        for c in range(chunks):
            a = aa[pl.ds(r * 8 + c, 16, stride=8), :]
            top = a.astype(BF16)
            hi[pl.ds(r, 16), c * 128 : (c + 1) * 128] = top
            lo[pl.ds(r, 16), c * 128 : (c + 1) * 128] = (a - top.astype(F32)).astype(BF16)

    stores.append(pltpu.make_async_copy(hi, hi_out, out_sem.at[2]))
    stores.append(pltpu.make_async_copy(lo, lo_out, out_sem.at[3]))
    stores[2].start()
    stores[3].start()

    @pl.loop(0, rows // 16)
    def _(i):
        r = pl.multiple_of(i * 16, 16)
        for c in range(chunks):
            g_ref[pl.ds(r, 16), c * 128 : (c + 1) * 128] = gs[pl.ds(r * 8 + c, 16, stride=8), :].astype(BF16)

    stores.append(pltpu.make_async_copy(g_ref, g_out, out_sem.at[4]))
    stores[4].start()
    for store in stores:
        store.wait()


def edges(live, s8, t8, r8, h, c, w, z, own_c, own_h, loop):
    rows, width = h.shape
    trows = c.shape[0]
    rpad = (z.shape[0] + 16) // 16 * 16
    return pl.pallas_call(
        edge_kernel,
        out_shape=(
            jax.ShapeDtypeStruct((rows, width), BF16),
            jax.ShapeDtypeStruct((own_c.shape[0], width), F32),
            jax.ShapeDtypeStruct((2 * trows, width), BF16),
            jax.ShapeDtypeStruct((2 * trows, width), BF16),
            jax.ShapeDtypeStruct((rpad // 16 * (width // 128) * 16 - FIRST_TILES * 16, 128), F32),
            jax.ShapeDtypeStruct((WAVE_HALF[0], 128), F32),
            jax.ShapeDtypeStruct((WAVE_HALF[0], 128), F32),
        ),
        in_specs=[SMEM] * 4 + [ANY] * 4 + [VMEM] * 3,
        out_specs=[ANY, VMEM, ANY, ANY, VMEM, ANY, ANY],
        scratch_shapes=[
            pltpu.VMEM(h.shape, BF16),
            pltpu.VMEM(c.shape, BF16),
            pltpu.VMEM(w.shape, BF16),
            pltpu.VMEM(z.shape, BF16),
            pltpu.VMEM((rows, width), BF16),
            pltpu.VMEM((WAVE_HALF[0], 128), F32),
            pltpu.VMEM((WAVE_HALF[0], 128), F32),
            pltpu.VMEM((rows * 8, 128), F32),
            pltpu.VMEM((2 * trows * 8, 128), F32),
            pltpu.VMEM((rpad * 8, 128), F32),
            pltpu.VMEM((rows * 8, 128), F32),
            pltpu.VMEM((2 * trows * 8, 128), F32),
            pltpu.VMEM((rpad * 8, 128), F32),
            pltpu.VMEM((2 * trows, width), BF16),
            pltpu.VMEM((2 * trows, width), BF16),
            DMA((4,)),
            DMA((5,)),
        ],
        compiler_params=pltpu.CompilerParams(vmem_limit_bytes=VMEM_BYTES),
        name="edges",
    )(live, s8, t8, r8, h, c, w, z, own_c, own_h, loop)


def reduce_kernel(
    keep_hbm, give, g_ref, hi_hbm, lo_hbm, c_hbm, rest, own_c, own_h, loop_ref, full, g_out,
    keep, given, hi, lo, c_all, g_own, pair, out1, in1, acc1, out2, in2, unit, g_in, g_acc, g_side,
    pair_s, pair_r, s1, r1, s2, r2, s4, r4, s6, r6, sib_s, sib_r, gz_s, gz_r, gx_s, gx_r,
    local, kept,
):
    me = Place()
    core = me.core
    sibling = me.sibling()
    x_hi, z = me.x_hi, me.at["z"]
    width = c_all.shape[1]
    trows = c_all.shape[0]
    chunks = width // 128
    parts = range(len(PARTS))

    def at(p, depth):
        return me.at[PARTS[p][0][depth]]

    def along(p, depth, j):
        return me.along(PARTS[p][0][depth], j)

    def in_plane(p, j, k):
        where = dict(me.at)
        where[PARTS[p][0][1]] = (at(p, 1) + j) % 4
        where[PARTS[p][0][2]] = (at(p, 2) + k) % 4
        return me.device(where, core)

    others = [(2, 2), (2, 1), (2, 3), (1, 2), (3, 2), (1, 1), (1, 3), (3, 1), (3, 3)]
    others += [(2, 0), (0, 2), (1, 0), (3, 0), (0, 1), (0, 3)]

    def rows_of(p, a):
        size = PARTS[p][1] * 16
        return pl.ds(pl.multiple_of(BASES[p] + a * size, 16), size)

    first_rows = pl.ds(0, WAVE_HALF[0])
    loads = [
        pltpu.make_async_copy(a, b, kept.at[n])
        for n, (a, b) in enumerate(
            (
                (keep_hbm, keep.at[first_rows]),
                (hi_hbm, hi),
                (c_hbm, c_all),
                (lo_hbm, lo),
                (g_ref.at[:, z], g_own),
            )
        )
    ]
    for load in loads:
        load.start()
    plane = [me.along(axis, k) for axis in ("x", "y", "z") for k in (1, 2, 3)]
    for p in (0, 1, 4):
        plane += [in_plane(p, j, k) for j, k in others[:9]]
    greet(plane + [sibling])

    pairs, step1, step6, side, own = {}, {}, {}, {}, {}

    def send_pair(some):
        for j in (1, 2, 3, 0):
            for p in some:
                where = rows_of(p, (at(p, 0) + j) % 4)
                if BASES[p] < WAVE_HALF[0]:
                    source = give.at[where]
                else:
                    row = BASES[p] - WAVE_HALF[0] + ((at(p, 0) + j) % 4) * (PARTS[p][1] * 16)
                    source = given.at[pl.ds(pl.multiple_of(row, 16), PARTS[p][1] * 16)]
                copy = push(source, pair.at[where], pair_s.at[p * 4 + j], pair_r.at[p * 4 + j], sibling)
                copy.start()
                pairs[p, j] = copy

    def send_first(some):
        for j in (1, 2, 3):
            for p in some:
                size = PARTS[p][1] * 16
                base = BASES[p] + ((at(p, 0) + j) % 4) * size
                pairs[p, j].wait_recv()

                @pl.loop(0, size // 128)
                def _(i, base=base):
                    r = pl.ds(pl.multiple_of(base + i * 128, 16), 128)
                    out1[r, :] = (keep[r, :] + pair[r, :]).astype(BF16)

                copy = push(
                    out1.at[rows_of(p, (at(p, 0) + j) % 4)],
                    in1.at[j - 1, pl.ds(BASES[p] // 4, size)],
                    s1.at[p * 3 + j - 1],
                    r1.at[p * 3 + j - 1],
                    along(p, 0, j),
                )
                copy.start()
                step1[p, j] = copy

    def send_second(p):
        size = PARTS[p][1]
        base = BASES[p] + at(p, 0) * (size * 16)
        low = BASES[p] // 4
        pairs[p, 0].wait_recv()
        for j in (1, 2, 3):
            step1[p, j].wait_recv()

        @pl.loop(0, size * 16 // 128)
        def _(i):
            r = pl.ds(pl.multiple_of(base + i * 128, 16), 128)
            q = pl.ds(pl.multiple_of(low + i * 128, 16), 128)
            total = (
                keep[r, :]
                + pair[r, :]
                + in1[0, q, :].astype(F32)
                + in1[1, q, :].astype(F32)
                + in1[2, q, :].astype(F32)
            )
            acc1[q, :] = total
            out2[q, :] = total.astype(BF16)

        for j, k in others:
            row = low + (((at(p, 1) + j) % 4) * 4 + (at(p, 2) + k) % 4) * size
            push(
                out2.at[pl.ds(pl.multiple_of(row, 16), size)],
                in2.at[j * 4 + k - 1, pl.ds(BASES[p] // 64, size)],
                s2.at[p],
                r2.at[p],
                in_plane(p, j, k),
            ).start()

    def second(p):
        mine = out2.at[pl.ds(BASES[p] // 4, PARTS[p][1] * 15)]
        return push(mine, in2.at[:, pl.ds(BASES[p] // 64, PARTS[p][1])], s2.at[p], r2.at[p], in_plane(p, 1, 1))

    def start_of(p):
        if BASES[p] < WAVE_HALF[0]:
            return core * WAVE_HALF[0] + BASES[p]
        return 2 * WAVE_HALF[0] + core * WAVE_HALF[1] + (BASES[p] - WAVE_HALF[0])

    def place(p, depth):
        size = PARTS[p][1]
        row = start_of(p) + at(p, 0) * (size * 16)
        if depth > 1:
            row = row + at(p, 1) * (size * 4)
        if depth > 2:
            row = row + at(p, 2) * size
        return full.at[pl.ds(pl.multiple_of(row, 16), (size * 16, size * 4, size)[depth - 1])]

    def half_of(p, offset, half):
        size = PARTS[p][1] * 8
        row = start_of(p) + ((at(p, 0) + 4 + offset) % 4) * (2 * size) + half * size
        return full.at[pl.ds(pl.multiple_of(row, 16), size)]

    def share_second(p):
        size = PARTS[p][1]
        second(p).wait_recv()
        q = pl.ds(BASES[p] // 64, size)
        mine = pl.ds(pl.multiple_of(BASES[p] // 4 + (at(p, 1) * 4 + at(p, 2)) * size, 16), size)
        total = acc1[mine, :]
        for n in range(15):
            total = total + in2[n, q, :].astype(F32)
        unit[q, :] = total.astype(BF16)
        for j, k in others:
            push(unit.at[q], place(p, 3), s4.at[p], r4.at[p], in_plane(p, j, k)).start()
        own[p] = pltpu.make_async_copy(unit.at[q], place(p, 3), local.at[p])
        own[p].start()

    def shared(p):
        where = pl.ds(pl.multiple_of(start_of(p) + at(p, 0) * (PARTS[p][1] * 16), 16), PARTS[p][1] * 15)
        return push(full.at[where], full.at[where], s4.at[p], r4.at[p], in_plane(p, 1, 1))

    def to_other_core(p, n, block):
        side[p, n] = push(block, block, sib_s.at[p * 7 + n], sib_r.at[p * 7 + n], sibling)
        side[p, n].start()

    def share_first(p):
        own[p].wait()
        shared(p).wait_recv()
        for n, (to, half) in enumerate(((1, 0), (3, 1), (1, 1), (3, 0))):
            block = half_of(p, 0, half)
            copy = push(block, block, s6.at[p * 6 + n], r6.at[p * 6 + n], along(p, 0, to))
            copy.start()
            step6[p, n] = copy
        to_other_core(p, 0, place(p, 1))

    def forward(p):
        for n, (to, half) in enumerate(((1, 0), (3, 1))):
            step6[p, n].wait_recv()
            block = half_of(p, -to, half)
            copy = push(block, block, s6.at[p * 6 + 4 + n], r6.at[p * 6 + 4 + n], along(p, 0, to))
            copy.start()
            step6[p, 4 + n] = copy
            to_other_core(p, 1 + n, block)

    def finish(p):
        for n, (to, half) in enumerate(((1, 1), (3, 0))):
            step6[p, 2 + n].wait_recv()
            to_other_core(p, 3 + n, half_of(p, -to, half))
        for half in range(2):
            step6[p, 4 + half].wait_recv()
            to_other_core(p, 5 + half, half_of(p, 2, half))

    def put(first, value):
        here = value.shape[0] // 16 * chunks
        for half in range(2):
            begin = max(first, half * SECOND_HALF_TILES)
            end = min(first + here, (half + 1) * SECOND_HALF_TILES)
            if begin >= end:
                continue

            def store(ref, base, half=half, begin=begin, end=end):
                for t in range(begin, end):
                    row = base + (t - half * SECOND_HALF_TILES) * 16
                    b, c = (t - first) // chunks, (t - first) % chunks
                    ref[row : row + 16, :] = value[b * 16 : b * 16 + 16, c * 128 : c * 128 + 128].astype(ref.dtype)

            @pl.when(core == half)
            def _(store=store):
                store(keep, WAVE_HALF[0])

            @pl.when(core != half)
            def _(store=store):
                store(given, 0)

    def make_wsum(d):
        rows = slice(d * trows, (d + 1) * trows)
        for k in range(width // 256):
            cols = slice(k * 256, (k + 1) * 256)
            w = lax.dot_general(
                hi[rows, cols], c_all[...], (((0,), (0,)), ((), ())), preferred_element_type=F32
            ) + lax.dot_general(
                lo[rows, cols], c_all[...], (((0,), (0,)), ((), ())), preferred_element_type=F32
            )
            put((d * 48 + k * 16) * chunks, w)

    def make_wself():
        self_comp = (own_h[...].astype(F32) * loop_ref[...].astype(F32).reshape(1, width)).astype(BF16)
        for k in range(width // 256):
            w = lax.dot_general(
                self_comp[:, k * 256 : (k + 1) * 256], own_c[...], (((0,), (0,)), ((), ())),
                preferred_element_type=F32,
            )
            put((96 + k * 16) * chunks, w)
        low = (W_TILES - SECOND_HALF_TILES) * 16
        n = rest.shape[0]

        def store(ref, base):
            ref[base + low : base + low + n, :] = rest[...].astype(ref.dtype)
            ref[base + low + n : base + WAVE_HALF[1], :] = jnp.zeros((WAVE_HALF[1] - low - n, 128), ref.dtype)

        @pl.when(core == 1)
        def _():
            store(keep, WAVE_HALF[0])

        @pl.when(core != 1)
        def _():
            store(given, 0)

    send_pair((0, 1))
    gz = []
    for k in (1, 3, 2):
        copy = push(g_ref.at[:, (z + k) % 4], g_in.at[k - 1], gz_s.at[k - 1], gz_r.at[k - 1], me.along("z", k))
        copy.start()
        gz.append(copy)
    loads[0].wait()
    for load in loads[1:]:
        load.wait()
    make_wsum(0)
    make_wsum(1)
    make_wself()
    send_pair((2, 3, 4))
    send_first((0, 1))
    send_first((2, 3, 4))
    send_second(0)
    send_second(1)
    send_second(2)
    send_second(3)
    send_second(4)
    share_second(0)
    share_second(1)
    for copy in gz:
        copy.wait_recv()
    for half in range(2):
        g_acc[half] = (
            g_own[half].astype(F32)
            + g_in[0, half].astype(F32)
            + g_in[1, half].astype(F32)
            + g_in[2, half].astype(F32)
        )
    gx = push(g_acc.at[1 - x_hi], g_side, gx_s, gx_r, me.along("x", 2))
    gx.start()
    share_second(2)
    share_second(3)
    share_second(4)
    share_first(0)
    share_first(1)
    share_first(2)
    share_first(3)
    share_first(4)
    forward(0)
    forward(1)
    forward(2)
    forward(3)
    forward(4)
    finish(0)
    finish(1)
    gx.wait_recv()
    g_out[...] = g_acc[x_hi] + g_side[...]
    finish(2)
    finish(3)
    finish(4)
    for copy in side.values():
        copy.wait_recv()
    gx.wait_send()
    for copy in gz:
        copy.wait_send()
    for group in (pairs, step1, step6, side):
        for copy in group.values():
            copy.wait_send()
    for p in parts:
        second(p).wait_send()
        shared(p).wait_send()


def reduce_all(keep, give, g, hi, lo, c_all, rest, own_c, own_h, loop):
    rows, width = g.shape
    g = g.reshape(2, 4, rows // 8, width)
    n = len(PARTS)
    return pl.pallas_call(
        reduce_kernel,
        out_shape=(
            jax.ShapeDtypeStruct((2 * HALF_ROWS, 128), BF16),
            jax.ShapeDtypeStruct((rows // 8, width), F32),
        ),
        in_specs=[ANY] * 6 + [VMEM] * 4,
        out_specs=[ANY, VMEM],
        scratch_shapes=[
            pltpu.VMEM((HALF_ROWS, 128), F32),
            pltpu.VMEM((WAVE_HALF[1], 128), F32),
            pltpu.VMEM(hi.shape, BF16),
            pltpu.VMEM(lo.shape, BF16),
            pltpu.VMEM(c_all.shape, BF16),
            pltpu.VMEM((2, rows // 8, width), BF16),
            pltpu.VMEM((HALF_ROWS, 128), F32),
            pltpu.VMEM((HALF_ROWS, 128), BF16),
            pltpu.VMEM((3, HALF_ROWS // 4, 128), BF16),
            pltpu.VMEM((HALF_ROWS // 4, 128), F32),
            pltpu.VMEM((HALF_ROWS // 4, 128), BF16),
            pltpu.VMEM((15, HALF_ROWS // 64, 128), BF16),
            pltpu.VMEM((HALF_ROWS // 64, 128), BF16),
            pltpu.VMEM((3, 2, rows // 8, width), BF16),
            pltpu.VMEM((2, rows // 8, width), F32),
            pltpu.VMEM((rows // 8, width), F32),
            *[DMA((4 * n,))] * 2, *[DMA((3 * n,))] * 2, *[DMA((n,))] * 4, *[DMA((6 * n,))] * 2, *[DMA((7 * n,))] * 2,
            DMA((3,)), DMA((3,)), DMA, DMA, DMA((n,)), DMA((5,)),
        ],
        compiler_params=pltpu.CompilerParams(
            collective_id=1, has_side_effects=True, vmem_limit_bytes=VMEM_BYTES
        ),
        name="reduce_all",
    )(keep, give, g, hi, lo, c_all, rest, own_c, own_h, loop)


def unpack_kernel(
    full_hbm, w_hbm, r_out, l_out, full, w_out, in_sem, out_sem, *, edge_scale, self_scale, rel_scale
):
    rels, width = r_out.shape
    chunks = width // 128
    per = width // 16
    pieces = in_sem.shape[0]
    size = full.shape[0] // pieces
    loads = []
    for i in range(pieces):
        where = pl.ds(i * size, size)
        loads.append(pltpu.make_async_copy(full_hbm.at[where], full.at[where], in_sem.at[i]))
        loads[-1].start()
    waited = []

    def need(first, last):
        for i in range(first // size, -(-last // size)):
            if i not in waited:
                waited.append(i)
                loads[i].wait()

    def tile(first, index):
        return full[pl.ds(pl.multiple_of(first + index * 16, 16), 16), :].astype(F32)

    w_first = 2 * WAVE_HALF[0]
    rest_first = w_first + W_TILES * 16
    stores = []
    for d, scale in enumerate((edge_scale, edge_scale, self_scale)):
        for k in range(3):
            group = per // 3
            need(w_first, w_first + (d * per + (k + 1) * group) * chunks * 16)

            @pl.loop(k * group, (k + 1) * group)
            def _(i, d=d, scale=scale):
                for c in range(chunks):
                    w_out[d, pl.ds(pl.multiple_of(i * 16, 16), 16), c * 128 : (c + 1) * 128] = (
                        tile(w_first, (d * per + i) * chunks + c) * scale
                    )

            where = pl.ds(k * group * 16, group * 16)
            stores.append(
                pltpu.make_async_copy(w_out.at[d, where], w_hbm.at[d, where], out_sem.at[d * 3 + k])
            )
            stores[-1].start()

    need(0, full.shape[0])
    whole = FIRST_TILES // chunks

    @pl.loop(0, whole)
    def _(i):
        for c in range(chunks):
            r_out[pl.ds(pl.multiple_of(i * 16, 16), 16), c * 128 : (c + 1) * 128] = (
                tile(0, i * chunks + c) * rel_scale
            )

    for t in range(whole * chunks, -(-(rels + 1) // 16) * chunks):
        b, cols = t // chunks, slice(t % chunks * 128, t % chunks * 128 + 128)
        last = tile(0, t) if t < FIRST_TILES else tile(rest_first, t - FIRST_TILES)
        n = min(16, rels - b * 16)
        if n:
            r_out[b * 16 : b * 16 + n, cols] = last[:n] * rel_scale
        if n < 16:
            l_out[cols] = (last[n : n + 1] * self_scale).reshape(128)
    for store in stores:
        store.wait()


def unpack(full, rels, width, **scales):
    return pl.pallas_call(
        functools.partial(unpack_kernel, **scales),
        out_shape=(
            jax.ShapeDtypeStruct((3, width, width), F32),
            jax.ShapeDtypeStruct((rels, width), F32),
            jax.ShapeDtypeStruct((width,), F32),
        ),
        in_specs=[ANY],
        out_specs=[ANY, VMEM, VMEM],
        scratch_shapes=[
            pltpu.VMEM(full.shape, BF16),
            pltpu.VMEM((3, width, width), F32),
            DMA((11,)),
            DMA((9,)),
        ],
        compiler_params=pltpu.CompilerParams(vmem_limit_bytes=VMEM_BYTES),
        name="unpack",
    )(full)


def body(
    h_src, rel_table, cotangent, h_tgt, loop_rel, weights, src_index, tgt_index, rel_ids, direction, counts
):
    width = weights.shape[1]
    tiles, edge = src_index.shape[2:]
    rels = rel_table.shape[0]
    h_all, c_all, s8, t8, r8 = gather(
        h_src, cotangent, *[a.reshape(tiles, edge) for a in (src_index, tgt_index, rel_ids, direction)]
    )
    g, grad_tgt, hi, lo, rest, keep, give = edges(
        counts.reshape(1), s8, t8, r8, h_all, c_all, weights, rel_table, cotangent, h_tgt, loop_rel
    )
    full, grad_src = reduce_all(
        keep, give, g, hi, lo, c_all, rest, cotangent, h_tgt, loop_rel
    )
    devices = lax.axis_size("src") * lax.axis_size("tgt")
    edges_all = float(devices * tiles * edge)
    targets_all = float(devices * cotangent.shape[0])
    grad_weights, grad_rel, grad_loop = unpack(
        full,
        rels,
        width,
        edge_scale=edges_all**-0.5,
        self_scale=targets_all**-0.5,
        rel_scale=(float(rels) / edges_all) ** 0.5,
    )
    return grad_src, grad_tgt, grad_weights, grad_rel, grad_loop


def solution(mesh):
    return jax.shard_map(
        body,
        mesh=mesh,
        in_specs=(
            P(("src", "tgt"), None),
            P(),
            P(("tgt", "src"), None),
            P(("tgt", "src"), None),
            P(),
            P(),
            P("src", "tgt", None, None),
            P("src", "tgt", None, None),
            P("src", "tgt", None, None),
            P("src", "tgt", None, None),
            P("src", "tgt"),
        ),
        out_specs=(P(("src", "tgt"), None), P(("tgt", "src"), None), P(), P(), P()),
        check_vma=False,
    )
```

```python
import functools

import jax
import jax.numpy as jnp
from jax import lax
from jax.experimental import pallas as pl
from jax.experimental.pallas import tpu as pltpu
from jax.sharding import PartitionSpec as P

F32 = jnp.float32
BF16 = jnp.bfloat16
MESH = pl.DeviceIdType.MESH
ANY = pl.BlockSpec(memory_space=pl.ANY)
VMEM = pl.BlockSpec(memory_space=pltpu.VMEM)
SMEM = pl.BlockSpec(memory_space=pltpu.SMEM)
DMA = pltpu.SemaphoreType.DMA

WAVE_HALF = (4096, 7168)
HALF_ROWS = sum(WAVE_HALF)
FIRST_TILES = 2 * WAVE_HALF[0] // 16
SECOND_HALF_TILES = WAVE_HALF[1] // 16
W_TILES = 864
PARTS = (
    (("x", "y", "z"), 32),
    (("y", "z", "x"), 32),
    (("z", "x", "y"), 48),
    (("x", "y", "z"), 32),
    (("y", "z", "x"), 32),
)
BASES = (0, 2048, 4096, 7168, 9216)
UNROLL = 32
EDGE = 128
VMEM_BYTES = 63 * 2**20


class Place:
    def __init__(self):
        s, t = lax.axis_index("src"), lax.axis_index("tgt")
        self.x_lo, self.core = s // 8, s % 2
        self.x_hi = t // 4
        self.at = {"x": self.x_hi * 2 + self.x_lo, "y": (s // 2) % 4, "z": t % 4}

    def device(self, at, core):
        return ((at["x"] % 2) * 8 + at["y"] * 2 + core, (at["x"] // 2) * 4 + at["z"])

    def along(self, axis, offset):
        at = dict(self.at)
        at[axis] = (at[axis] + offset) % 4
        return self.device(at, self.core)

    def sibling(self):
        return self.device(self.at, 1 - self.core)

    def x_lo_partner(self):
        at = dict(self.at)
        at["x"] = self.x_hi * 2 + (1 - self.x_lo)
        return self.device(at, self.core)


def greet(partners):
    barrier = pltpu.get_barrier_semaphore()
    for partner in partners:
        pl.semaphore_signal(barrier, inc=1, device_id=partner, device_id_type=MESH)
    pl.semaphore_wait(barrier, len(partners))


def push(src, dst, send, recv, device):
    return pltpu.make_async_remote_copy(
        src_ref=src, dst_ref=dst, send_sem=send, recv_sem=recv, device_id=device, device_id_type=MESH
    )


def gather_kernel(
    h_ref, c_ref, w_hbm, src_ref, tgt_ref, rel_ref, dir_ref, own_c, own_h, loop_ref,
    h_all, c_all, s8, t8, r8, t_out, l_out, w_ref, local, hx_s, hx_r, hz_s, hz_r, cy_s, cy_r, cx_s, cx_r, cs_s, cs_r
):
    me = Place()
    x_lo, x_hi, core, y, z = me.x_lo, me.x_hi, me.core, me.at["y"], me.at["z"]
    sibling, across = me.sibling(), me.x_lo_partner()
    own_h_copy = pltpu.make_async_copy(h_ref, h_all.at[x_hi, z], local.at[0])
    own_c_copy = pltpu.make_async_copy(c_ref, c_all.at[x_lo, y, core], local.at[1])
    w_self = pltpu.make_async_copy(w_hbm.at[2], w_ref, local.at[2])
    w_self.start()
    own_h_copy.start()
    own_c_copy.start()
    s8[...] = src_ref[...] * 8
    t8[...] = (tgt_ref[...] + dir_ref[...] * (16 * c_ref.shape[0])) * 8
    r8[...] = rel_ref[...] * 8
    greet(
        [me.along("x", 2), across, sibling]
        + [me.along("y", k) for k in (1, 2, 3)]
        + [me.along("z", k) for k in (1, 2, 3)]
    )
    mine, theirs = h_all.at[x_hi, z], h_all.at[1 - x_hi, z]
    hx = push(h_ref, mine, hx_s, hx_r, me.along("x", 2))
    hx.start()
    cy, hz = [], []
    for k in (1, 3, 2):
        copy = push(h_ref, mine, hz_s.at[k - 1], hz_r.at[k - 1], me.along("z", k))
        copy.start()
        hz.append(copy)
        copy = push(c_ref, c_all.at[x_lo, y, core], cy_s.at[k - 1], cy_r.at[k - 1], me.along("y", k))
        copy.start()
        cy.append(copy)
    hx.wait()
    for k in (1, 3, 2):
        copy = push(theirs, theirs, hz_s.at[k + 2], hz_r.at[k + 2], me.along("z", k))
        copy.start()
        hz.append(copy)
    own_c_copy.wait()
    for copy in cy:
        copy.wait_recv()
    near = c_all.at[x_lo, :, core]
    far = c_all.at[1 - x_lo, :, core]
    cx = push(near, near, cx_s, cx_r, across)
    cx.start()
    first = push(near, near, cs_s.at[0], cs_r.at[0], sibling)
    first.start()
    w_self.wait()
    back = lax.dot_general(own_c[...], w_ref[...], (((1,), (1,)), ((), ())), preferred_element_type=F32)
    t_out[...] = back * loop_ref[...].astype(F32).reshape(1, back.shape[1])
    l_out[...] = jnp.sum(back * own_h[...].astype(F32), axis=0, keepdims=True)
    cx.wait()
    second = push(far, far, cs_s.at[1], cs_r.at[1], sibling)
    second.start()
    first.wait()
    second.wait()
    own_h_copy.wait()
    for copy in hz:
        copy.wait()
    for copy in cy:
        copy.wait_send()


def gather(h_src, cotangent, weights, h_tgt, loop, *indices):
    rows, width = h_src.shape
    trows = cotangent.shape[0]
    h_all, c_all, s8, t8, r8, grad_tgt, lsum = pl.pallas_call(
        gather_kernel,
        out_shape=(
            jax.ShapeDtypeStruct((2, 4, rows, width), BF16),
            jax.ShapeDtypeStruct((2, 4, 2, trows, width), BF16),
            *[jax.ShapeDtypeStruct(indices[0].shape, jnp.int32)] * 3,
            jax.ShapeDtypeStruct((trows, width), F32),
            jax.ShapeDtypeStruct((1, width), F32),
        ),
        in_specs=[ANY] * 3 + [VMEM] * 7,
        out_specs=[ANY] * 2 + [VMEM] * 5,
        scratch_shapes=[
            pltpu.VMEM((width, width), BF16),
            DMA((3,)), DMA, DMA, DMA((6,)), DMA((6,)), DMA((3,)), DMA((3,)), DMA, DMA, DMA((2,)), DMA((2,)),
        ],
        compiler_params=pltpu.CompilerParams(collective_id=0, has_side_effects=True, vmem_limit_bytes=VMEM_BYTES),
        name="gather_panels",
    )(h_src, cotangent, weights, *indices, cotangent, h_tgt, loop)
    flat = [a.reshape(-1) for a in (s8, t8, r8)]
    return h_all.reshape(8 * rows, width), c_all.reshape(16 * trows, width), *flat, grad_tgt, lsum


def edge_kernel(
    live_ref, src_ref, tgt_ref, rel_ref, h_hbm, c_hbm, w_hbm, z_hbm, lsum,
    g_out, hi_out, lo_out, rest_out, keep_out, give_out,
    h_ref, c_ref, w_ref, z_ref, g_ref, keep, give, hx, px, zx, gs, aa, rr, hi, lo, in_sem, out_sem,
):
    loads = [
        pltpu.make_async_copy(a, b, in_sem.at[i])
        for i, (a, b) in enumerate(((h_hbm, h_ref), (z_hbm, z_ref), (c_hbm, c_ref), (w_hbm.at[pl.ds(0, 2)], w_ref)))
    ]
    for load in loads:
        load.start()
    core = lax.axis_index("src") % 2
    rows = h_ref.shape[0]
    trows = c_ref.shape[0]
    rels, width = z_ref.shape
    chunks = width // 128

    def spread(dst, row, value):
        for c in range(chunks):
            dst[pl.ds(row * 8 + c, value.shape[0], stride=8), :] = value[:, c * 128 : (c + 1) * 128]

    zero = jnp.zeros((64, 128), F32)
    for ref in (gs, aa, rr):

        @pl.loop(0, ref.shape[0] // 64)
        def _(i, ref=ref):
            ref[pl.ds(pl.multiple_of(i * 64, 64), 64), :] = zero

    loads[0].wait()

    @pl.loop(0, rows // 16)
    def _(i):
        r = pl.multiple_of(i * 16, 16)
        spread(hx, r, h_ref[pl.ds(r, 16), :].astype(F32))

    loads[1].wait()

    @pl.loop(0, rels // 16)
    def _(i):
        r = pl.multiple_of(i * 16, 16)
        spread(zx, r, z_ref[pl.ds(r, 16), :].astype(F32))

    tail = rels // 16 * 16
    if tail < rels:
        spread(zx, tail, z_ref[tail:rels, :].astype(F32))
    loads[2].wait()
    loads[3].wait()
    for d in range(2):
        for k in range(width // 256):
            p = lax.dot_general(
                c_ref[...], w_ref[d, k * 256 : (k + 1) * 256, :], (((1,), (1,)), ((), ())),
                preferred_element_type=F32,
            )
            for h in range(2):
                px[pl.ds(d * trows * 8 + 2 * k + h, trows, stride=8), :] = p[:, h * 128 : (h + 1) * 128]
    def row(at):
        return pl.ds(pl.multiple_of(at, 8), 8)

    @pl.loop(0, live_ref[0] * (EDGE // UNROLL))
    def _(i):
        start = i * UNROLL
        for u in range(0, UNROLL, 2):
            s0, s1 = src_ref[start + u], src_ref[start + u + 1]
            t0, t1 = tgt_ref[start + u], tgt_ref[start + u + 1]
            r0, r1 = rel_ref[start + u], rel_ref[start + u + 1]
            h0, h1 = hx[row(s0), :], hx[row(s1), :]
            p0, p1 = px[row(t0), :], px[row(t1), :]
            z0, z1 = zx[row(r0), :], zx[row(r1), :]
            for ref, at0, at1, v0, v1 in (
                (gs, s0, s1, p0 * z0, p1 * z1),
                (aa, t0, t1, (h0 * z0).astype(BF16).astype(F32), (h1 * z1).astype(BF16).astype(F32)),
                (rr, r0, r1, p0 * h0, p1 * h1),
            ):
                sum0 = ref[row(at0), :] + v0
                sum1 = ref[row(at1), :] + v1 + jnp.where(at0 == at1, v0, jnp.zeros_like(v0))
                ref[row(at0), :] = sum0
                ref[row(at1), :] = sum1

    for c in range(chunks):
        rr[rels * 8 + c : rels * 8 + c + 1, :] = lsum[:, c * 128 : (c + 1) * 128]
    blocks = rr.shape[0] // 128

    def rel_tile(block, c):
        return rr[pl.ds(block * 128 + c, 16, stride=8), :]

    def collect(half, ref):
        first = half * (FIRST_TILES // 2)
        last = first + FIRST_TILES // 2

        @pl.loop(-(-first // chunks), last // chunks)
        def _(i):
            for c in range(chunks):
                row = pl.multiple_of((i * chunks + c - first) * 16, 16)
                ref[pl.ds(row, 16), :] = rel_tile(i, c).astype(ref.dtype)

        edge_tiles = [*range(first, -(-first // chunks) * chunks), *range(last // chunks * chunks, last)]
        for t in edge_tiles:
            row = (t - first) * 16
            ref[row : row + 16, :] = rel_tile(t // chunks, t % chunks).astype(ref.dtype)

    @pl.when(core == 0)
    def _():
        collect(0, keep)
        collect(1, give)

    @pl.when(core != 0)
    def _():
        collect(1, keep)
        collect(0, give)

    stores = [
        pltpu.make_async_copy(keep, keep_out, out_sem.at[0]),
        pltpu.make_async_copy(give, give_out, out_sem.at[1]),
    ]
    for store in stores:
        store.start()
    for t in range(FIRST_TILES, blocks * chunks):
        row = (t - FIRST_TILES) * 16
        rest_out[row : row + 16, :] = rel_tile(t // chunks, t % chunks)

    @pl.loop(0, 2 * trows // 16)
    def _(i):
        r = pl.multiple_of(i * 16, 16)
        for c in range(chunks):
            a = aa[pl.ds(r * 8 + c, 16, stride=8), :]
            top = a.astype(BF16)
            hi[pl.ds(r, 16), c * 128 : (c + 1) * 128] = top
            lo[pl.ds(r, 16), c * 128 : (c + 1) * 128] = (a - top.astype(F32)).astype(BF16)

    stores.append(pltpu.make_async_copy(hi, hi_out, out_sem.at[2]))
    stores.append(pltpu.make_async_copy(lo, lo_out, out_sem.at[3]))
    stores[2].start()
    stores[3].start()

    @pl.loop(0, rows // 16)
    def _(i):
        r = pl.multiple_of(i * 16, 16)
        for c in range(chunks):
            g_ref[pl.ds(r, 16), c * 128 : (c + 1) * 128] = gs[pl.ds(r * 8 + c, 16, stride=8), :].astype(BF16)

    stores.append(pltpu.make_async_copy(g_ref, g_out, out_sem.at[4]))
    stores[4].start()
    for store in stores:
        store.wait()


def edges(live, s8, t8, r8, h, c, w, z, lsum):
    rows, width = h.shape
    trows = c.shape[0]
    rpad = (z.shape[0] + 16) // 16 * 16
    return pl.pallas_call(
        edge_kernel,
        out_shape=(
            jax.ShapeDtypeStruct((rows, width), BF16),
            jax.ShapeDtypeStruct((2 * trows, width), BF16),
            jax.ShapeDtypeStruct((2 * trows, width), BF16),
            jax.ShapeDtypeStruct((rpad // 16 * (width // 128) * 16 - FIRST_TILES * 16, 128), F32),
            jax.ShapeDtypeStruct((WAVE_HALF[0], 128), F32),
            jax.ShapeDtypeStruct((WAVE_HALF[0], 128), F32),
        ),
        in_specs=[SMEM] * 4 + [ANY] * 4 + [VMEM],
        out_specs=[ANY, ANY, ANY, VMEM, ANY, ANY],
        scratch_shapes=[
            pltpu.VMEM(h.shape, BF16),
            pltpu.VMEM(c.shape, BF16),
            pltpu.VMEM((2, width, width), BF16),
            pltpu.VMEM(z.shape, BF16),
            pltpu.VMEM((rows, width), BF16),
            pltpu.VMEM((WAVE_HALF[0], 128), F32),
            pltpu.VMEM((WAVE_HALF[0], 128), F32),
            pltpu.VMEM((rows * 8, 128), F32),
            pltpu.VMEM((2 * trows * 8, 128), F32),
            pltpu.VMEM((rpad * 8, 128), F32),
            pltpu.VMEM((rows * 8, 128), F32),
            pltpu.VMEM((2 * trows * 8, 128), F32),
            pltpu.VMEM((rpad * 8, 128), F32),
            pltpu.VMEM((2 * trows, width), BF16),
            pltpu.VMEM((2 * trows, width), BF16),
            DMA((4,)),
            DMA((5,)),
        ],
        compiler_params=pltpu.CompilerParams(vmem_limit_bytes=VMEM_BYTES),
        name="edges",
    )(live, s8, t8, r8, h, c, w, z, lsum)


def reduce_kernel(
    keep_hbm, give, g_ref, hi_hbm, lo_hbm, c_hbm, rest, own_c, own_h, loop_ref, full, g_out,
    keep, given, hi, lo, c_all, g_own, pair, out1, in1, acc1, out2, in2, unit, g_in, g_acc, g_side,
    pair_s, pair_r, s1, r1, s2, r2, s4, r4, s6, r6, sib_s, sib_r, gz_s, gz_r, gx_s, gx_r,
    local, kept,
):
    me = Place()
    core = me.core
    sibling = me.sibling()
    x_hi, z = me.x_hi, me.at["z"]
    width = c_all.shape[1]
    trows = c_all.shape[0]
    chunks = width // 128
    parts = range(len(PARTS))

    def at(p, depth):
        return me.at[PARTS[p][0][depth]]

    def along(p, depth, j):
        return me.along(PARTS[p][0][depth], j)

    def in_plane(p, j, k):
        where = dict(me.at)
        where[PARTS[p][0][1]] = (at(p, 1) + j) % 4
        where[PARTS[p][0][2]] = (at(p, 2) + k) % 4
        return me.device(where, core)

    others = [(2, 2), (2, 1), (2, 3), (1, 2), (3, 2), (1, 1), (1, 3), (3, 1), (3, 3)]
    others += [(2, 0), (0, 2), (1, 0), (3, 0), (0, 1), (0, 3)]

    def rows_of(p, a):
        size = PARTS[p][1] * 16
        return pl.ds(pl.multiple_of(BASES[p] + a * size, 16), size)

    first_rows = pl.ds(0, WAVE_HALF[0])
    loads = [
        pltpu.make_async_copy(a, b, kept.at[n])
        for n, (a, b) in enumerate(
            (
                (keep_hbm, keep.at[first_rows]),
                (hi_hbm, hi),
                (c_hbm, c_all),
                (lo_hbm, lo),
                (g_ref.at[:, z], g_own),
            )
        )
    ]
    for load in loads:
        load.start()
    plane = [me.along(axis, k) for axis in ("x", "y", "z") for k in (1, 2, 3)]
    for p in (0, 1, 2):
        plane += [in_plane(p, j, k) for j, k in others[:9]]
    greet(plane + [sibling])

    pairs, step1, step6, side, own = {}, {}, {}, {}, {}

    def send_pair(some):
        for j in (1, 2, 3, 0):
            for p in some:
                where = rows_of(p, (at(p, 0) + j) % 4)
                if BASES[p] < WAVE_HALF[0]:
                    source = give.at[where]
                else:
                    row = BASES[p] - WAVE_HALF[0] + ((at(p, 0) + j) % 4) * (PARTS[p][1] * 16)
                    source = given.at[pl.ds(pl.multiple_of(row, 16), PARTS[p][1] * 16)]
                copy = push(source, pair.at[where], pair_s.at[p * 4 + j], pair_r.at[p * 4 + j], sibling)
                copy.start()
                pairs[p, j] = copy

    def send_first(some):
        for j in (1, 2, 3):
            for p in some:
                size = PARTS[p][1] * 16
                base = BASES[p] + ((at(p, 0) + j) % 4) * size
                pairs[p, j].wait_recv()

                @pl.loop(0, size // 128)
                def _(i, base=base):
                    r = pl.ds(pl.multiple_of(base + i * 128, 16), 128)
                    out1[r, :] = (keep[r, :] + pair[r, :]).astype(BF16)

                copy = push(
                    out1.at[rows_of(p, (at(p, 0) + j) % 4)],
                    in1.at[j - 1, pl.ds(BASES[p] // 4, size)],
                    s1.at[p * 3 + j - 1],
                    r1.at[p * 3 + j - 1],
                    along(p, 0, j),
                )
                copy.start()
                step1[p, j] = copy

    def send_second(p):
        size = PARTS[p][1]
        base = BASES[p] + at(p, 0) * (size * 16)
        low = BASES[p] // 4
        pairs[p, 0].wait_recv()
        for j in (1, 2, 3):
            step1[p, j].wait_recv()

        @pl.loop(0, size * 16 // 128)
        def _(i):
            r = pl.ds(pl.multiple_of(base + i * 128, 16), 128)
            q = pl.ds(pl.multiple_of(low + i * 128, 16), 128)
            total = (
                keep[r, :]
                + pair[r, :]
                + in1[0, q, :].astype(F32)
                + in1[1, q, :].astype(F32)
                + in1[2, q, :].astype(F32)
            )
            acc1[q, :] = total
            out2[q, :] = total.astype(BF16)

        for j, k in others:
            row = low + (((at(p, 1) + j) % 4) * 4 + (at(p, 2) + k) % 4) * size
            push(
                out2.at[pl.ds(pl.multiple_of(row, 16), size)],
                in2.at[j * 4 + k - 1, pl.ds(BASES[p] // 64, size)],
                s2.at[p],
                r2.at[p],
                in_plane(p, j, k),
            ).start()

    def second(p):
        mine = out2.at[pl.ds(BASES[p] // 4, PARTS[p][1] * 15)]
        return push(mine, in2.at[:, pl.ds(BASES[p] // 64, PARTS[p][1])], s2.at[p], r2.at[p], in_plane(p, 1, 1))

    def start_of(p):
        if BASES[p] < WAVE_HALF[0]:
            return core * WAVE_HALF[0] + BASES[p]
        return 2 * WAVE_HALF[0] + core * WAVE_HALF[1] + (BASES[p] - WAVE_HALF[0])

    def place(p, depth):
        size = PARTS[p][1]
        row = start_of(p) + at(p, 0) * (size * 16)
        if depth > 1:
            row = row + at(p, 1) * (size * 4)
        if depth > 2:
            row = row + at(p, 2) * size
        return full.at[pl.ds(pl.multiple_of(row, 16), (size * 16, size * 4, size)[depth - 1])]

    def half_of(p, offset, half):
        size = PARTS[p][1] * 8
        row = start_of(p) + ((at(p, 0) + 4 + offset) % 4) * (2 * size) + half * size
        return full.at[pl.ds(pl.multiple_of(row, 16), size)]

    def share_second(p):
        size = PARTS[p][1]
        second(p).wait_recv()
        q = pl.ds(BASES[p] // 64, size)
        mine = pl.ds(pl.multiple_of(BASES[p] // 4 + (at(p, 1) * 4 + at(p, 2)) * size, 16), size)
        total = acc1[mine, :]
        for n in range(15):
            total = total + in2[n, q, :].astype(F32)
        unit[q, :] = total.astype(BF16)
        for j, k in others:
            push(unit.at[q], place(p, 3), s4.at[p], r4.at[p], in_plane(p, j, k)).start()
        own[p] = pltpu.make_async_copy(unit.at[q], place(p, 3), local.at[p])
        own[p].start()

    def shared(p):
        where = pl.ds(pl.multiple_of(start_of(p) + at(p, 0) * (PARTS[p][1] * 16), 16), PARTS[p][1] * 15)
        return push(full.at[where], full.at[where], s4.at[p], r4.at[p], in_plane(p, 1, 1))

    def to_other_core(p, n, block):
        side[p, n] = push(block, block, sib_s.at[p * 7 + n], sib_r.at[p * 7 + n], sibling)
        side[p, n].start()

    def share_first(p):
        own[p].wait()
        shared(p).wait_recv()
        for n, (to, half) in enumerate(((1, 0), (3, 1), (1, 1), (3, 0))):
            block = half_of(p, 0, half)
            copy = push(block, block, s6.at[p * 6 + n], r6.at[p * 6 + n], along(p, 0, to))
            copy.start()
            step6[p, n] = copy
        to_other_core(p, 0, place(p, 1))

    def forward(p):
        for n, (to, half) in enumerate(((1, 0), (3, 1))):
            step6[p, n].wait_recv()
            block = half_of(p, -to, half)
            copy = push(block, block, s6.at[p * 6 + 4 + n], r6.at[p * 6 + 4 + n], along(p, 0, to))
            copy.start()
            step6[p, 4 + n] = copy
            to_other_core(p, 1 + n, block)

    def finish(p):
        for n, (to, half) in enumerate(((1, 1), (3, 0))):
            step6[p, 2 + n].wait_recv()
            to_other_core(p, 3 + n, half_of(p, -to, half))
        for half in range(2):
            step6[p, 4 + half].wait_recv()
            to_other_core(p, 5 + half, half_of(p, 2, half))

    def put(first, value):
        here = value.shape[0] // 16 * chunks
        for half in range(2):
            begin = max(first, half * SECOND_HALF_TILES)
            end = min(first + here, (half + 1) * SECOND_HALF_TILES)
            if begin >= end:
                continue

            def store(ref, base, half=half, begin=begin, end=end):
                for t in range(begin, end):
                    row = base + (t - half * SECOND_HALF_TILES) * 16
                    b, c = (t - first) // chunks, (t - first) % chunks
                    ref[row : row + 16, :] = value[b * 16 : b * 16 + 16, c * 128 : c * 128 + 128].astype(ref.dtype)

            @pl.when(core == half)
            def _(store=store):
                store(keep, WAVE_HALF[0])

            @pl.when(core != half)
            def _(store=store):
                store(given, 0)

    def make_wsum(d):
        rows = slice(d * trows, (d + 1) * trows)
        for k in range(width // 256):
            cols = slice(k * 256, (k + 1) * 256)
            w = lax.dot_general(
                hi[rows, cols], c_all[...], (((0,), (0,)), ((), ())), preferred_element_type=F32
            ) + lax.dot_general(
                lo[rows, cols], c_all[...], (((0,), (0,)), ((), ())), preferred_element_type=F32
            )
            put((d * 48 + k * 16) * chunks, w)

    def make_wself():
        self_comp = (own_h[...].astype(F32) * loop_ref[...].astype(F32).reshape(1, width)).astype(BF16)
        for k in range(width // 256):
            w = lax.dot_general(
                self_comp[:, k * 256 : (k + 1) * 256], own_c[...], (((0,), (0,)), ((), ())),
                preferred_element_type=F32,
            )
            put((96 + k * 16) * chunks, w)
        low = (W_TILES - SECOND_HALF_TILES) * 16
        n = rest.shape[0]

        def store(ref, base):
            ref[base + low : base + low + n, :] = rest[...].astype(ref.dtype)
            ref[base + low + n : base + WAVE_HALF[1], :] = jnp.zeros((WAVE_HALF[1] - low - n, 128), ref.dtype)

        @pl.when(core == 1)
        def _():
            store(keep, WAVE_HALF[0])

        @pl.when(core != 1)
        def _():
            store(given, 0)

    send_pair((0, 1))
    gz = []
    for k in (1, 3, 2):
        copy = push(g_ref.at[:, (z + k) % 4], g_in.at[k - 1], gz_s.at[k - 1], gz_r.at[k - 1], me.along("z", k))
        copy.start()
        gz.append(copy)
    loads[0].wait()
    for load in loads[1:]:
        load.wait()
    make_wsum(0)
    make_wsum(1)
    make_wself()
    send_pair((2, 3, 4))
    send_first((0, 1))
    send_first((2, 3, 4))
    send_second(0)
    send_second(1)
    send_second(2)
    send_second(3)
    send_second(4)
    share_second(0)
    share_second(1)
    for copy in gz:
        copy.wait_recv()
    for half in range(2):
        g_acc[half] = (
            g_own[half].astype(F32)
            + g_in[0, half].astype(F32)
            + g_in[1, half].astype(F32)
            + g_in[2, half].astype(F32)
        )
    gx = push(g_acc.at[1 - x_hi], g_side, gx_s, gx_r, me.along("x", 2))
    gx.start()
    share_second(2)
    share_second(3)
    share_second(4)
    share_first(0)
    share_first(1)
    share_first(2)
    share_first(3)
    share_first(4)
    forward(0)
    forward(1)
    forward(2)
    forward(3)
    forward(4)
    finish(0)
    finish(1)
    gx.wait_recv()
    g_out[...] = g_acc[x_hi] + g_side[...]
    finish(2)
    finish(3)
    finish(4)
    for copy in side.values():
        copy.wait_recv()
    gx.wait_send()
    for copy in gz:
        copy.wait_send()
    for group in (pairs, step1, step6, side):
        for copy in group.values():
            copy.wait_send()
    for p in parts:
        second(p).wait_send()
        shared(p).wait_send()


def reduce_all(keep, give, g, hi, lo, c_all, rest, own_c, own_h, loop):
    rows, width = g.shape
    g = g.reshape(2, 4, rows // 8, width)
    n = len(PARTS)
    return pl.pallas_call(
        reduce_kernel,
        out_shape=(
            jax.ShapeDtypeStruct((2 * HALF_ROWS, 128), BF16),
            jax.ShapeDtypeStruct((rows // 8, width), F32),
        ),
        in_specs=[ANY] * 6 + [VMEM] * 4,
        out_specs=[ANY, VMEM],
        scratch_shapes=[
            pltpu.VMEM((HALF_ROWS, 128), F32),
            pltpu.VMEM((WAVE_HALF[1], 128), F32),
            pltpu.VMEM(hi.shape, BF16),
            pltpu.VMEM(lo.shape, BF16),
            pltpu.VMEM(c_all.shape, BF16),
            pltpu.VMEM((2, rows // 8, width), BF16),
            pltpu.VMEM((HALF_ROWS, 128), F32),
            pltpu.VMEM((HALF_ROWS, 128), BF16),
            pltpu.VMEM((3, HALF_ROWS // 4, 128), BF16),
            pltpu.VMEM((HALF_ROWS // 4, 128), F32),
            pltpu.VMEM((HALF_ROWS // 4, 128), BF16),
            pltpu.VMEM((15, HALF_ROWS // 64, 128), BF16),
            pltpu.VMEM((HALF_ROWS // 64, 128), BF16),
            pltpu.VMEM((3, 2, rows // 8, width), BF16),
            pltpu.VMEM((2, rows // 8, width), F32),
            pltpu.VMEM((rows // 8, width), F32),
            *[DMA((4 * n,))] * 2, *[DMA((3 * n,))] * 2, *[DMA((n,))] * 4, *[DMA((6 * n,))] * 2, *[DMA((7 * n,))] * 2,
            DMA((3,)), DMA((3,)), DMA, DMA, DMA((n,)), DMA((5,)),
        ],
        compiler_params=pltpu.CompilerParams(
            collective_id=1, has_side_effects=True, vmem_limit_bytes=VMEM_BYTES
        ),
        name="reduce_all",
    )(keep, give, g, hi, lo, c_all, rest, own_c, own_h, loop)


REL_BLOCK = 18


def unpack_kernel(
    full_hbm, gs_in, gt_in, w_hbm, r_out, l_out, gs_out, gt_out, full, w_out, in_sem, out_sem,
    *, rels, edge_scale, self_scale, rel_scale,
):
    step = pl.program_id(0)
    last_step = -(-(rels + 1) // (REL_BLOCK * 16)) - 1
    width = r_out.shape[1]
    chunks = width // 128
    per = width // 16
    group = per // 3
    pieces = in_sem.shape[0]
    size = full.shape[0] // pieces

    def load(i):
        where = pl.ds(i * size, size)
        return pltpu.make_async_copy(full_hbm.at[where], full.at[where], in_sem.at[i])

    def store(n):
        if n < 9:
            where = pl.ds(n % 3 * group * 16, group * 16)
            return pltpu.make_async_copy(w_out.at[n // 3, where], w_hbm.at[n // 3, where], out_sem.at[n])
        source, target = ((gs_in, gs_out), (gt_in, gt_out))[n - 9]
        return pltpu.make_async_copy(source, target, out_sem.at[n])

    def tile(first, index):
        return full[pl.ds(pl.multiple_of(first + index * 16, 16), 16), :].astype(F32)

    w_first = 2 * WAVE_HALF[0]
    rest_first = w_first + W_TILES * 16

    @pl.when(step == 0)
    def _():
        order = [*range(w_first // size, pieces), *range(w_first // size)]
        for i in order:
            load(i).start()
        store(9).start()
        store(10).start()
        waited = 0
        for n in range(9):
            end = w_first + (n + 1) * group * chunks * 16
            while order[waited] * size < end and waited < pieces - w_first // size:
                load(order[waited]).wait()
                waited += 1
            d, scale = n // 3, (edge_scale, edge_scale, self_scale)[n // 3]

            @pl.loop(n % 3 * group, (n % 3 + 1) * group)
            def _(i, d=d, scale=scale):
                for c in range(chunks):
                    w_out[d, pl.ds(pl.multiple_of(i * 16, 16), 16), c * 128 : (c + 1) * 128] = (
                        tile(w_first, (d * per + i) * chunks + c) * scale
                    )

            store(n).start()
        for i in order[waited:]:
            load(i).wait()

    @pl.when(step != last_step)
    def _():
        @pl.loop(0, REL_BLOCK)
        def _(i):
            for c in range(chunks):
                r_out[pl.ds(pl.multiple_of(i * 16, 16), 16), c * 128 : (c + 1) * 128] = (
                    tile(0, (step * REL_BLOCK + i) * chunks + c) * rel_scale
                )

    @pl.when(step == last_step)
    def _():
        first = last_step * REL_BLOCK
        for t in range(first * chunks, -(-(rels + 1) // 16) * chunks):
            b, cols = t // chunks, slice(t % chunks * 128, t % chunks * 128 + 128)
            value = tile(0, t) if t < FIRST_TILES else tile(rest_first, t - FIRST_TILES)
            r_out[(b - first) * 16 : (b - first) * 16 + 16, cols] = value * rel_scale
            n = rels - b * 16
            if n < 16:
                l_out[cols] = (value[n : n + 1] * self_scale).reshape(128)
        for n in range(11):
            store(n).wait()


def unpack(full, grad_src, grad_tgt, rels, width, **scales):
    rows = REL_BLOCK * 16
    return pl.pallas_call(
        functools.partial(unpack_kernel, rels=rels, **scales),
        grid=(-(-(rels + 1) // rows),),
        out_shape=(
            jax.ShapeDtypeStruct((3, width, width), F32),
            jax.ShapeDtypeStruct((rels, width), F32),
            jax.ShapeDtypeStruct((width,), F32),
            jax.ShapeDtypeStruct(grad_src.shape, F32),
            jax.ShapeDtypeStruct(grad_tgt.shape, F32),
        ),
        in_specs=[ANY] * 3,
        out_specs=[
            ANY,
            pl.BlockSpec((rows, width), lambda i: (i, 0)),
            pl.BlockSpec((width,), lambda i: (0,)),
            ANY,
            ANY,
        ],
        scratch_shapes=[
            pltpu.VMEM(full.shape, BF16),
            pltpu.VMEM((3, width, width), F32),
            DMA((11,)),
            DMA((11,)),
        ],
        compiler_params=pltpu.CompilerParams(vmem_limit_bytes=VMEM_BYTES),
        name="unpack",
    )(full, grad_src, grad_tgt)


def body(
    h_src, rel_table, cotangent, h_tgt, loop_rel, weights, src_index, tgt_index, rel_ids, direction, counts
):
    width = weights.shape[1]
    tiles, edge = src_index.shape[2:]
    rels = rel_table.shape[0]
    h_all, c_all, s8, t8, r8, back, lsum = gather(
        h_src, cotangent, weights, h_tgt, loop_rel, *[a.reshape(tiles, edge) for a in (src_index, tgt_index, rel_ids, direction)]
    )
    g, hi, lo, rest, keep, give = edges(
        counts.reshape(1), s8, t8, r8, h_all, c_all, weights, rel_table, lsum
    )
    full, mine = reduce_all(
        keep, give, g, hi, lo, c_all, rest, cotangent, h_tgt, loop_rel
    )
    devices = lax.axis_size("src") * lax.axis_size("tgt")
    edges_all = float(devices * tiles * edge)
    targets_all = float(devices * cotangent.shape[0])
    grad_weights, grad_rel, grad_loop, grad_src, grad_tgt = unpack(
        full,
        mine,
        back,
        rels,
        width,
        edge_scale=edges_all**-0.5,
        self_scale=targets_all**-0.5,
        rel_scale=(float(rels) / edges_all) ** 0.5,
    )
    return grad_src, grad_tgt, grad_weights, grad_rel, grad_loop


def solution(mesh):
    return jax.shard_map(
        body,
        mesh=mesh,
        in_specs=(
            P(("src", "tgt"), None),
            P(),
            P(("tgt", "src"), None),
            P(("tgt", "src"), None),
            P(),
            P(),
            P("src", "tgt", None, None),
            P("src", "tgt", None, None),
            P("src", "tgt", None, None),
            P("src", "tgt", None, None),
            P("src", "tgt"),
        ),
        out_specs=(P(("src", "tgt"), None), P(("tgt", "src"), None), P(), P(), P()),
        check_vma=False,
    )
```

```python
import functools

import jax
import jax.numpy as jnp
from jax import lax
from jax.experimental import pallas as pl
from jax.experimental.pallas import tpu as pltpu
from jax.sharding import PartitionSpec as P

F32 = jnp.float32
BF16 = jnp.bfloat16
MESH = pl.DeviceIdType.MESH
ANY = pl.BlockSpec(memory_space=pl.ANY)
VMEM = pl.BlockSpec(memory_space=pltpu.VMEM)
SMEM = pl.BlockSpec(memory_space=pltpu.SMEM)
DMA = pltpu.SemaphoreType.DMA

WAVE_HALF = (4096, 7168)
HALF_ROWS = sum(WAVE_HALF)
FIRST_TILES = 2 * WAVE_HALF[0] // 16
SECOND_HALF_TILES = WAVE_HALF[1] // 16
W_TILES = 864
PARTS = (
    (("x", "y", "z"), 32),
    (("y", "z", "x"), 32),
    (("z", "x", "y"), 48),
    (("x", "y", "z"), 32),
    (("y", "z", "x"), 32),
)
BASES = (0, 2048, 4096, 7168, 9216)
UNROLL = 32
EDGE = 128
VMEM_BYTES = 63 * 2**20


class Place:
    def __init__(self):
        s, t = lax.axis_index("src"), lax.axis_index("tgt")
        self.x_lo, self.core = s // 8, s % 2
        self.x_hi = t // 4
        self.at = {"x": self.x_hi * 2 + self.x_lo, "y": (s // 2) % 4, "z": t % 4}

    def device(self, at, core):
        return ((at["x"] % 2) * 8 + at["y"] * 2 + core, (at["x"] // 2) * 4 + at["z"])

    def along(self, axis, offset):
        at = dict(self.at)
        at[axis] = (at[axis] + offset) % 4
        return self.device(at, self.core)

    def sibling(self):
        return self.device(self.at, 1 - self.core)

    def x_lo_partner(self):
        at = dict(self.at)
        at["x"] = self.x_hi * 2 + (1 - self.x_lo)
        return self.device(at, self.core)


def greet(partners):
    barrier = pltpu.get_barrier_semaphore()
    for partner in partners:
        pl.semaphore_signal(barrier, inc=1, device_id=partner, device_id_type=MESH)
    pl.semaphore_wait(barrier, len(partners))


def push(src, dst, send, recv, device):
    return pltpu.make_async_remote_copy(
        src_ref=src, dst_ref=dst, send_sem=send, recv_sem=recv, device_id=device, device_id_type=MESH
    )


def gather_kernel(
    h_ref, c_ref, w_hbm, src_ref, tgt_ref, rel_ref, dir_ref, own_c, own_h, loop_ref,
    h_all, c_all, s8, t8, r8, t_out, l_out, w_ref, local, hx_s, hx_r, hz_s, hz_r, cy_s, cy_r, cx_s, cx_r, cs_s, cs_r
):
    me = Place()
    x_lo, x_hi, core, y, z = me.x_lo, me.x_hi, me.core, me.at["y"], me.at["z"]
    sibling, across = me.sibling(), me.x_lo_partner()
    own_h_copy = pltpu.make_async_copy(h_ref, h_all.at[x_hi, z], local.at[0])
    own_c_copy = pltpu.make_async_copy(c_ref, c_all.at[x_lo, y, core], local.at[1])
    w_self = pltpu.make_async_copy(w_hbm.at[2], w_ref, local.at[2])
    w_self.start()
    own_h_copy.start()
    own_c_copy.start()
    s8[...] = src_ref[...] * 8
    t8[...] = (tgt_ref[...] + dir_ref[...] * (16 * c_ref.shape[0])) * 8
    r8[...] = rel_ref[...] * 8
    greet(
        [me.along("x", 2), across, sibling]
        + [me.along("y", k) for k in (1, 2, 3)]
        + [me.along("z", k) for k in (1, 2, 3)]
    )
    mine, theirs = h_all.at[x_hi, z], h_all.at[1 - x_hi, z]
    hx = push(h_ref, mine, hx_s, hx_r, me.along("x", 2))
    hx.start()
    cy, hz = [], []
    for k in (1, 3, 2):
        copy = push(h_ref, mine, hz_s.at[k - 1], hz_r.at[k - 1], me.along("z", k))
        copy.start()
        hz.append(copy)
        copy = push(c_ref, c_all.at[x_lo, y, core], cy_s.at[k - 1], cy_r.at[k - 1], me.along("y", k))
        copy.start()
        cy.append(copy)
    hx.wait()
    for k in (1, 3, 2):
        copy = push(theirs, theirs, hz_s.at[k + 2], hz_r.at[k + 2], me.along("z", k))
        copy.start()
        hz.append(copy)
    own_c_copy.wait()
    for copy in cy:
        copy.wait_recv()
    near = c_all.at[x_lo, :, core]
    far = c_all.at[1 - x_lo, :, core]
    cx = push(near, near, cx_s, cx_r, across)
    cx.start()
    first = push(near, near, cs_s.at[0], cs_r.at[0], sibling)
    first.start()
    w_self.wait()
    back = lax.dot_general(own_c[...], w_ref[...], (((1,), (1,)), ((), ())), preferred_element_type=F32)
    t_out[...] = back * loop_ref[...].astype(F32).reshape(1, back.shape[1])
    l_out[...] = jnp.sum(back * own_h[...].astype(F32), axis=0, keepdims=True)
    cx.wait()
    second = push(far, far, cs_s.at[1], cs_r.at[1], sibling)
    second.start()
    first.wait()
    second.wait()
    own_h_copy.wait()
    for copy in hz:
        copy.wait()
    for copy in cy:
        copy.wait_send()


def gather(h_src, cotangent, weights, h_tgt, loop, *indices):
    rows, width = h_src.shape
    trows = cotangent.shape[0]
    h_all, c_all, s8, t8, r8, grad_tgt, lsum = pl.pallas_call(
        gather_kernel,
        out_shape=(
            jax.ShapeDtypeStruct((2, 4, rows, width), BF16),
            jax.ShapeDtypeStruct((2, 4, 2, trows, width), BF16),
            *[jax.ShapeDtypeStruct(indices[0].shape, jnp.int32)] * 3,
            jax.ShapeDtypeStruct((trows, width), F32),
            jax.ShapeDtypeStruct((1, width), F32),
        ),
        in_specs=[ANY] * 3 + [VMEM] * 7,
        out_specs=[ANY] * 2 + [VMEM] * 5,
        scratch_shapes=[
            pltpu.VMEM((width, width), BF16),
            DMA((3,)), DMA, DMA, DMA((6,)), DMA((6,)), DMA((3,)), DMA((3,)), DMA, DMA, DMA((2,)), DMA((2,)),
        ],
        compiler_params=pltpu.CompilerParams(collective_id=0, has_side_effects=True, vmem_limit_bytes=VMEM_BYTES),
        name="gather_panels",
    )(h_src, cotangent, weights, *indices, cotangent, h_tgt, loop)
    flat = [a.reshape(-1) for a in (s8, t8, r8)]
    return h_all.reshape(8 * rows, width), c_all.reshape(16 * trows, width), *flat, grad_tgt, lsum


def edge_kernel(
    live_ref, src_ref, tgt_ref, rel_ref, h_hbm, c_hbm, w_hbm, z_hbm, lsum,
    g_out, hi_out, lo_out, rest_out, keep_out, give_out,
    h_ref, c_ref, w_ref, z_ref, g_ref, keep, give, hx, px, zx, gs, aa, rr, hi, lo, in_sem, out_sem,
):
    loads = [
        pltpu.make_async_copy(a, b, in_sem.at[i])
        for i, (a, b) in enumerate(((h_hbm, h_ref), (z_hbm, z_ref), (c_hbm, c_ref), (w_hbm.at[pl.ds(0, 2)], w_ref)))
    ]
    for load in loads:
        load.start()
    core = lax.axis_index("src") % 2
    rows = h_ref.shape[0]
    trows = c_ref.shape[0]
    rels, width = z_ref.shape
    chunks = width // 128

    def spread(dst, row, value):
        for c in range(chunks):
            dst[pl.ds(row * 8 + c, value.shape[0], stride=8), :] = value[:, c * 128 : (c + 1) * 128]

    zero = jnp.zeros((64, 128), F32)
    for ref in (gs, aa, rr):

        @pl.loop(0, ref.shape[0] // 64)
        def _(i, ref=ref):
            ref[pl.ds(pl.multiple_of(i * 64, 64), 64), :] = zero

    loads[0].wait()

    @pl.loop(0, rows // 16)
    def _(i):
        r = pl.multiple_of(i * 16, 16)
        spread(hx, r, h_ref[pl.ds(r, 16), :].astype(F32))

    loads[1].wait()

    @pl.loop(0, rels // 16)
    def _(i):
        r = pl.multiple_of(i * 16, 16)
        spread(zx, r, z_ref[pl.ds(r, 16), :].astype(F32))

    tail = rels // 16 * 16
    if tail < rels:
        spread(zx, tail, z_ref[tail:rels, :].astype(F32))
    loads[2].wait()
    loads[3].wait()
    for d in range(2):
        for k in range(width // 256):
            p = lax.dot_general(
                c_ref[...], w_ref[d, k * 256 : (k + 1) * 256, :], (((1,), (1,)), ((), ())),
                preferred_element_type=F32,
            )
            for h in range(2):
                px[pl.ds(d * trows * 8 + 2 * k + h, trows, stride=8), :] = p[:, h * 128 : (h + 1) * 128]
    def row(at):
        return pl.ds(pl.multiple_of(at, 8), 8)

    @pl.loop(0, live_ref[0] * (EDGE // UNROLL))
    def _(i):
        start = i * UNROLL
        for u in range(0, UNROLL, 2):
            s0, s1 = src_ref[start + u], src_ref[start + u + 1]
            t0, t1 = tgt_ref[start + u], tgt_ref[start + u + 1]
            r0, r1 = rel_ref[start + u], rel_ref[start + u + 1]
            h0, h1 = hx[row(s0), :], hx[row(s1), :]
            p0, p1 = px[row(t0), :], px[row(t1), :]
            z0, z1 = zx[row(r0), :], zx[row(r1), :]
            for ref, at0, at1, v0, v1 in (
                (gs, s0, s1, p0 * z0, p1 * z1),
                (aa, t0, t1, (h0 * z0).astype(BF16).astype(F32), (h1 * z1).astype(BF16).astype(F32)),
                (rr, r0, r1, p0 * h0, p1 * h1),
            ):
                sum0 = ref[row(at0), :] + v0
                sum1 = ref[row(at1), :] + v1 + jnp.where(at0 == at1, v0, jnp.zeros_like(v0))
                ref[row(at0), :] = sum0
                ref[row(at1), :] = sum1

    for c in range(chunks):
        rr[rels * 8 + c : rels * 8 + c + 1, :] = lsum[:, c * 128 : (c + 1) * 128]
    blocks = rr.shape[0] // 128

    def rel_tile(block, c):
        return rr[pl.ds(block * 128 + c, 16, stride=8), :]

    def collect(half, ref):
        first = half * (FIRST_TILES // 2)
        last = first + FIRST_TILES // 2

        @pl.loop(-(-first // chunks), last // chunks)
        def _(i):
            for c in range(chunks):
                row = pl.multiple_of((i * chunks + c - first) * 16, 16)
                ref[pl.ds(row, 16), :] = rel_tile(i, c).astype(ref.dtype)

        edge_tiles = [*range(first, -(-first // chunks) * chunks), *range(last // chunks * chunks, last)]
        for t in edge_tiles:
            row = (t - first) * 16
            ref[row : row + 16, :] = rel_tile(t // chunks, t % chunks).astype(ref.dtype)

    @pl.when(core == 0)
    def _():
        collect(0, keep)
        collect(1, give)

    @pl.when(core != 0)
    def _():
        collect(1, keep)
        collect(0, give)

    stores = [
        pltpu.make_async_copy(keep, keep_out, out_sem.at[0]),
        pltpu.make_async_copy(give, give_out, out_sem.at[1]),
    ]
    for store in stores:
        store.start()
    for t in range(FIRST_TILES, blocks * chunks):
        row = (t - FIRST_TILES) * 16
        rest_out[row : row + 16, :] = rel_tile(t // chunks, t % chunks)

    @pl.loop(0, 2 * trows // 16)
    def _(i):
        r = pl.multiple_of(i * 16, 16)
        for c in range(chunks):
            a = aa[pl.ds(r * 8 + c, 16, stride=8), :]
            top = a.astype(BF16)
            hi[pl.ds(r, 16), c * 128 : (c + 1) * 128] = top
            lo[pl.ds(r, 16), c * 128 : (c + 1) * 128] = (a - top.astype(F32)).astype(BF16)

    stores.append(pltpu.make_async_copy(hi, hi_out, out_sem.at[2]))
    stores.append(pltpu.make_async_copy(lo, lo_out, out_sem.at[3]))
    stores[2].start()
    stores[3].start()

    @pl.loop(0, rows // 16)
    def _(i):
        r = pl.multiple_of(i * 16, 16)
        for c in range(chunks):
            g_ref[pl.ds(r, 16), c * 128 : (c + 1) * 128] = gs[pl.ds(r * 8 + c, 16, stride=8), :].astype(BF16)

    stores.append(pltpu.make_async_copy(g_ref, g_out, out_sem.at[4]))
    stores[4].start()
    for store in stores:
        store.wait()


def edges(live, s8, t8, r8, h, c, w, z, lsum):
    rows, width = h.shape
    trows = c.shape[0]
    rpad = (z.shape[0] + 16) // 16 * 16
    return pl.pallas_call(
        edge_kernel,
        out_shape=(
            jax.ShapeDtypeStruct((rows, width), BF16),
            jax.ShapeDtypeStruct((2 * trows, width), BF16),
            jax.ShapeDtypeStruct((2 * trows, width), BF16),
            jax.ShapeDtypeStruct((rpad // 16 * (width // 128) * 16 - FIRST_TILES * 16, 128), F32),
            jax.ShapeDtypeStruct((WAVE_HALF[0], 128), F32),
            jax.ShapeDtypeStruct((WAVE_HALF[0], 128), F32),
        ),
        in_specs=[SMEM] * 4 + [ANY] * 4 + [VMEM],
        out_specs=[ANY, ANY, ANY, VMEM, ANY, ANY],
        scratch_shapes=[
            pltpu.VMEM(h.shape, BF16),
            pltpu.VMEM(c.shape, BF16),
            pltpu.VMEM((2, width, width), BF16),
            pltpu.VMEM(z.shape, BF16),
            pltpu.VMEM((rows, width), BF16),
            pltpu.VMEM((WAVE_HALF[0], 128), F32),
            pltpu.VMEM((WAVE_HALF[0], 128), F32),
            pltpu.VMEM((rows * 8, 128), F32),
            pltpu.VMEM((2 * trows * 8, 128), F32),
            pltpu.VMEM((rpad * 8, 128), F32),
            pltpu.VMEM((rows * 8, 128), F32),
            pltpu.VMEM((2 * trows * 8, 128), F32),
            pltpu.VMEM((rpad * 8, 128), F32),
            pltpu.VMEM((2 * trows, width), BF16),
            pltpu.VMEM((2 * trows, width), BF16),
            DMA((4,)),
            DMA((5,)),
        ],
        compiler_params=pltpu.CompilerParams(vmem_limit_bytes=VMEM_BYTES),
        name="edges",
    )(live, s8, t8, r8, h, c, w, z, lsum)


def reduce_kernel(
    keep_hbm, give, g_ref, hi_hbm, lo_hbm, c_hbm, rest, own_c, own_h, loop_ref, full, g_out,
    keep, given, hi, lo, c_all, g_own, pair, out1, in1, acc1, out2, in2, unit, g_in, g_acc, g_send, g_side,
    pair_s, pair_r, s1, r1, s2, r2, s4, r4, s6, r6, sib_s, sib_r, gz_s, gz_r, gx_s, gx_r,
    local, kept,
):
    me = Place()
    core = me.core
    sibling = me.sibling()
    x_hi, z = me.x_hi, me.at["z"]
    width = c_all.shape[1]
    trows = c_all.shape[0]
    chunks = width // 128
    parts = range(len(PARTS))

    def at(p, depth):
        return me.at[PARTS[p][0][depth]]

    def along(p, depth, j):
        return me.along(PARTS[p][0][depth], j)

    def in_plane(p, j, k):
        where = dict(me.at)
        where[PARTS[p][0][1]] = (at(p, 1) + j) % 4
        where[PARTS[p][0][2]] = (at(p, 2) + k) % 4
        return me.device(where, core)

    others = [(2, 2), (2, 1), (2, 3), (1, 2), (3, 2), (1, 1), (1, 3), (3, 1), (3, 3)]
    others += [(2, 0), (0, 2), (1, 0), (3, 0), (0, 1), (0, 3)]

    def rows_of(p, a):
        size = PARTS[p][1] * 16
        return pl.ds(pl.multiple_of(BASES[p] + a * size, 16), size)

    first_rows = pl.ds(0, WAVE_HALF[0])
    loads = [
        pltpu.make_async_copy(a, b, kept.at[n])
        for n, (a, b) in enumerate(
            (
                (keep_hbm, keep.at[first_rows]),
                (hi_hbm, hi),
                (c_hbm, c_all),
                (lo_hbm, lo),
                (g_ref.at[:, z], g_own),
            )
        )
    ]
    for load in loads:
        load.start()
    plane = [me.along(axis, k) for axis in ("x", "y", "z") for k in (1, 2, 3)]
    for p in (0, 1, 2):
        plane += [in_plane(p, j, k) for j, k in others[:9]]
    greet(plane + [sibling])

    pairs, step1, step6, side, own = {}, {}, {}, {}, {}

    def send_pair(some):
        for j in (1, 2, 3, 0):
            for p in some:
                where = rows_of(p, (at(p, 0) + j) % 4)
                if BASES[p] < WAVE_HALF[0]:
                    source = give.at[where]
                else:
                    row = BASES[p] - WAVE_HALF[0] + ((at(p, 0) + j) % 4) * (PARTS[p][1] * 16)
                    source = given.at[pl.ds(pl.multiple_of(row, 16), PARTS[p][1] * 16)]
                copy = push(source, pair.at[where], pair_s.at[p * 4 + j], pair_r.at[p * 4 + j], sibling)
                copy.start()
                pairs[p, j] = copy

    def send_first(some):
        for j in (1, 2, 3):
            for p in some:
                size = PARTS[p][1] * 16
                base = BASES[p] + ((at(p, 0) + j) % 4) * size
                pairs[p, j].wait_recv()

                @pl.loop(0, size // 128)
                def _(i, base=base):
                    r = pl.ds(pl.multiple_of(base + i * 128, 16), 128)
                    out1[r, :] = (keep[r, :] + pair[r, :]).astype(BF16)

                copy = push(
                    out1.at[rows_of(p, (at(p, 0) + j) % 4)],
                    in1.at[j - 1, pl.ds(BASES[p] // 4, size)],
                    s1.at[p * 3 + j - 1],
                    r1.at[p * 3 + j - 1],
                    along(p, 0, j),
                )
                copy.start()
                step1[p, j] = copy

    def send_second(p):
        size = PARTS[p][1]
        base = BASES[p] + at(p, 0) * (size * 16)
        low = BASES[p] // 4
        pairs[p, 0].wait_recv()
        for j in (1, 2, 3):
            step1[p, j].wait_recv()

        @pl.loop(0, size * 16 // 128)
        def _(i):
            r = pl.ds(pl.multiple_of(base + i * 128, 16), 128)
            q = pl.ds(pl.multiple_of(low + i * 128, 16), 128)
            total = (
                keep[r, :]
                + pair[r, :]
                + in1[0, q, :].astype(F32)
                + in1[1, q, :].astype(F32)
                + in1[2, q, :].astype(F32)
            )
            acc1[q, :] = total
            out2[q, :] = total.astype(BF16)

        for j, k in others:
            row = low + (((at(p, 1) + j) % 4) * 4 + (at(p, 2) + k) % 4) * size
            push(
                out2.at[pl.ds(pl.multiple_of(row, 16), size)],
                in2.at[j * 4 + k - 1, pl.ds(BASES[p] // 64, size)],
                s2.at[p],
                r2.at[p],
                in_plane(p, j, k),
            ).start()

    def second(p):
        mine = out2.at[pl.ds(BASES[p] // 4, PARTS[p][1] * 15)]
        return push(mine, in2.at[:, pl.ds(BASES[p] // 64, PARTS[p][1])], s2.at[p], r2.at[p], in_plane(p, 1, 1))

    def start_of(p):
        if BASES[p] < WAVE_HALF[0]:
            return core * WAVE_HALF[0] + BASES[p]
        return 2 * WAVE_HALF[0] + core * WAVE_HALF[1] + (BASES[p] - WAVE_HALF[0])

    def place(p, depth):
        size = PARTS[p][1]
        row = start_of(p) + at(p, 0) * (size * 16)
        if depth > 1:
            row = row + at(p, 1) * (size * 4)
        if depth > 2:
            row = row + at(p, 2) * size
        return full.at[pl.ds(pl.multiple_of(row, 16), (size * 16, size * 4, size)[depth - 1])]

    def half_of(p, offset, half):
        size = PARTS[p][1] * 8
        row = start_of(p) + ((at(p, 0) + 4 + offset) % 4) * (2 * size) + half * size
        return full.at[pl.ds(pl.multiple_of(row, 16), size)]

    def share_second(p):
        size = PARTS[p][1]
        second(p).wait_recv()
        q = pl.ds(BASES[p] // 64, size)
        mine = pl.ds(pl.multiple_of(BASES[p] // 4 + (at(p, 1) * 4 + at(p, 2)) * size, 16), size)
        total = acc1[mine, :]
        for n in range(15):
            total = total + in2[n, q, :].astype(F32)
        unit[q, :] = total.astype(BF16)
        for j, k in others:
            push(unit.at[q], place(p, 3), s4.at[p], r4.at[p], in_plane(p, j, k)).start()
        own[p] = pltpu.make_async_copy(unit.at[q], place(p, 3), local.at[p])
        own[p].start()

    def shared(p):
        where = pl.ds(pl.multiple_of(start_of(p) + at(p, 0) * (PARTS[p][1] * 16), 16), PARTS[p][1] * 15)
        return push(full.at[where], full.at[where], s4.at[p], r4.at[p], in_plane(p, 1, 1))

    def to_other_core(p, n, block):
        side[p, n] = push(block, block, sib_s.at[p * 7 + n], sib_r.at[p * 7 + n], sibling)
        side[p, n].start()

    def share_first(p):
        own[p].wait()
        shared(p).wait_recv()
        for n, (to, half) in enumerate(((1, 0), (3, 1), (1, 1), (3, 0))):
            block = half_of(p, 0, half)
            copy = push(block, block, s6.at[p * 6 + n], r6.at[p * 6 + n], along(p, 0, to))
            copy.start()
            step6[p, n] = copy
        to_other_core(p, 0, place(p, 1))

    def forward(p):
        for n, (to, half) in enumerate(((1, 0), (3, 1))):
            step6[p, n].wait_recv()
            block = half_of(p, -to, half)
            copy = push(block, block, s6.at[p * 6 + 4 + n], r6.at[p * 6 + 4 + n], along(p, 0, to))
            copy.start()
            step6[p, 4 + n] = copy
            to_other_core(p, 1 + n, block)

    def finish(p):
        for n, (to, half) in enumerate(((1, 1), (3, 0))):
            step6[p, 2 + n].wait_recv()
            to_other_core(p, 3 + n, half_of(p, -to, half))
        for half in range(2):
            step6[p, 4 + half].wait_recv()
            to_other_core(p, 5 + half, half_of(p, 2, half))

    def put(first, value):
        here = value.shape[0] // 16 * chunks
        for half in range(2):
            begin = max(first, half * SECOND_HALF_TILES)
            end = min(first + here, (half + 1) * SECOND_HALF_TILES)
            if begin >= end:
                continue

            def store(ref, base, half=half, begin=begin, end=end):
                for t in range(begin, end):
                    row = base + (t - half * SECOND_HALF_TILES) * 16
                    b, c = (t - first) // chunks, (t - first) % chunks
                    ref[row : row + 16, :] = value[b * 16 : b * 16 + 16, c * 128 : c * 128 + 128].astype(ref.dtype)

            @pl.when(core == half)
            def _(store=store):
                store(keep, WAVE_HALF[0])

            @pl.when(core != half)
            def _(store=store):
                store(given, 0)

    def make_wsum(d):
        rows = slice(d * trows, (d + 1) * trows)
        for k in range(width // 256):
            cols = slice(k * 256, (k + 1) * 256)
            w = lax.dot_general(
                hi[rows, cols], c_all[...], (((0,), (0,)), ((), ())), preferred_element_type=F32
            ) + lax.dot_general(
                lo[rows, cols], c_all[...], (((0,), (0,)), ((), ())), preferred_element_type=F32
            )
            put((d * 48 + k * 16) * chunks, w)

    def make_wself():
        self_comp = (own_h[...].astype(F32) * loop_ref[...].astype(F32).reshape(1, width)).astype(BF16)
        for k in range(width // 256):
            w = lax.dot_general(
                self_comp[:, k * 256 : (k + 1) * 256], own_c[...], (((0,), (0,)), ((), ())),
                preferred_element_type=F32,
            )
            put((96 + k * 16) * chunks, w)
        low = (W_TILES - SECOND_HALF_TILES) * 16
        n = rest.shape[0]

        def store(ref, base):
            ref[base + low : base + low + n, :] = rest[...].astype(ref.dtype)
            ref[base + low + n : base + WAVE_HALF[1], :] = jnp.zeros((WAVE_HALF[1] - low - n, 128), ref.dtype)

        @pl.when(core == 1)
        def _():
            store(keep, WAVE_HALF[0])

        @pl.when(core != 1)
        def _():
            store(given, 0)

    send_pair((0, 1))
    gz = []
    for k in (1, 3, 2):
        copy = push(g_ref.at[:, (z + k) % 4], g_in.at[k - 1], gz_s.at[k - 1], gz_r.at[k - 1], me.along("z", k))
        copy.start()
        gz.append(copy)
    loads[0].wait()
    for load in loads[1:]:
        load.wait()
    make_wsum(0)
    make_wsum(1)
    make_wself()
    send_pair((2, 3, 4))
    send_first((0, 1))
    send_first((2, 3, 4))
    send_second(0)
    send_second(1)
    send_second(2)
    send_second(3)
    send_second(4)
    share_second(0)
    share_second(1)
    share_second(2)
    share_second(3)
    share_second(4)
    for copy in gz:
        copy.wait_recv()
    for half in range(2):
        g_acc[half] = (
            g_own[half].astype(F32)
            + g_in[0, half].astype(F32)
            + g_in[1, half].astype(F32)
            + g_in[2, half].astype(F32)
        )
    g_send[...] = g_acc[1 - x_hi].astype(BF16)
    gx = push(g_send, g_side, gx_s, gx_r, me.along("x", 2))
    gx.start()
    share_first(0)
    share_first(1)
    share_first(2)
    share_first(3)
    share_first(4)
    forward(0)
    forward(1)
    forward(2)
    forward(3)
    forward(4)
    finish(0)
    finish(1)
    gx.wait_recv()
    g_out[...] = g_acc[x_hi] + g_side[...].astype(F32)
    finish(2)
    finish(3)
    finish(4)
    for copy in side.values():
        copy.wait_recv()
    gx.wait_send()
    for copy in gz:
        copy.wait_send()
    for group in (pairs, step1, step6, side):
        for copy in group.values():
            copy.wait_send()
    for p in parts:
        second(p).wait_send()
        shared(p).wait_send()


def reduce_all(keep, give, g, hi, lo, c_all, rest, own_c, own_h, loop):
    rows, width = g.shape
    g = g.reshape(2, 4, rows // 8, width)
    n = len(PARTS)
    return pl.pallas_call(
        reduce_kernel,
        out_shape=(
            jax.ShapeDtypeStruct((2 * HALF_ROWS, 128), BF16),
            jax.ShapeDtypeStruct((rows // 8, width), F32),
        ),
        in_specs=[ANY] * 6 + [VMEM] * 4,
        out_specs=[ANY, VMEM],
        scratch_shapes=[
            pltpu.VMEM((HALF_ROWS, 128), F32),
            pltpu.VMEM((WAVE_HALF[1], 128), F32),
            pltpu.VMEM(hi.shape, BF16),
            pltpu.VMEM(lo.shape, BF16),
            pltpu.VMEM(c_all.shape, BF16),
            pltpu.VMEM((2, rows // 8, width), BF16),
            pltpu.VMEM((HALF_ROWS, 128), F32),
            pltpu.VMEM((HALF_ROWS, 128), BF16),
            pltpu.VMEM((3, HALF_ROWS // 4, 128), BF16),
            pltpu.VMEM((HALF_ROWS // 4, 128), F32),
            pltpu.VMEM((HALF_ROWS // 4, 128), BF16),
            pltpu.VMEM((15, HALF_ROWS // 64, 128), BF16),
            pltpu.VMEM((HALF_ROWS // 64, 128), BF16),
            pltpu.VMEM((3, 2, rows // 8, width), BF16),
            pltpu.VMEM((2, rows // 8, width), F32),
            pltpu.VMEM((rows // 8, width), BF16),
            pltpu.VMEM((rows // 8, width), BF16),
            *[DMA((4 * n,))] * 2, *[DMA((3 * n,))] * 2, *[DMA((n,))] * 4, *[DMA((6 * n,))] * 2, *[DMA((7 * n,))] * 2,
            DMA((3,)), DMA((3,)), DMA, DMA, DMA((n,)), DMA((5,)),
        ],
        compiler_params=pltpu.CompilerParams(
            collective_id=1, has_side_effects=True, vmem_limit_bytes=VMEM_BYTES
        ),
        name="reduce_all",
    )(keep, give, g, hi, lo, c_all, rest, own_c, own_h, loop)


REL_BLOCK = 18


def unpack_kernel(
    full_hbm, gs_in, gt_in, w_hbm, r_out, l_out, gs_out, gt_out, full, w_out, gs, gt, in_sem, out_sem,
    *, rels, edge_scale, self_scale, rel_scale,
):
    step = pl.program_id(0)
    last_step = -(-(rels + 1) // (REL_BLOCK * 16)) - 1
    width = r_out.shape[1]
    chunks = width // 128
    per = width // 16
    group = per // 3
    pieces = in_sem.shape[0] - 2
    size = full.shape[0] // pieces

    def load(i):
        if i >= pieces:
            source, target = ((gs_in, gs), (gt_in, gt))[i - pieces]
            return pltpu.make_async_copy(source, target, in_sem.at[i])
        where = pl.ds(i * size, size)
        return pltpu.make_async_copy(full_hbm.at[where], full.at[where], in_sem.at[i])

    def store(n):
        if n < 9:
            where = pl.ds(n % 3 * group * 16, group * 16)
            return pltpu.make_async_copy(w_out.at[n // 3, where], w_hbm.at[n // 3, where], out_sem.at[n])
        source, target = ((gs, gs_out), (gt, gt_out))[n - 9]
        return pltpu.make_async_copy(source, target, out_sem.at[n])

    def tile(first, index):
        return full[pl.ds(pl.multiple_of(first + index * 16, 16), 16), :].astype(F32)

    w_first = 2 * WAVE_HALF[0]
    rest_first = w_first + W_TILES * 16

    @pl.when(step == 0)
    def _():
        order = [*range(w_first // size, pieces), *range(w_first // size), pieces, pieces + 1]
        for i in order:
            load(i).start()
        waited = 0
        for n in range(9):
            end = w_first + (n + 1) * group * chunks * 16
            while order[waited] * size < end and waited < pieces - w_first // size:
                load(order[waited]).wait()
                waited += 1
            d, scale = n // 3, (edge_scale, edge_scale, self_scale)[n // 3]

            @pl.loop(n % 3 * group, (n % 3 + 1) * group)
            def _(i, d=d, scale=scale):
                for c in range(chunks):
                    w_out[d, pl.ds(pl.multiple_of(i * 16, 16), 16), c * 128 : (c + 1) * 128] = (
                        tile(w_first, (d * per + i) * chunks + c) * scale
                    )

            store(n).start()
        for i in order[waited:]:
            load(i).wait()
        store(9).start()
        store(10).start()

    @pl.when(step != last_step)
    def _():
        @pl.loop(0, REL_BLOCK)
        def _(i):
            for c in range(chunks):
                r_out[pl.ds(pl.multiple_of(i * 16, 16), 16), c * 128 : (c + 1) * 128] = (
                    tile(0, (step * REL_BLOCK + i) * chunks + c) * rel_scale
                )

    @pl.when(step == last_step)
    def _():
        first = last_step * REL_BLOCK
        for t in range(first * chunks, -(-(rels + 1) // 16) * chunks):
            b, cols = t // chunks, slice(t % chunks * 128, t % chunks * 128 + 128)
            value = tile(0, t) if t < FIRST_TILES else tile(rest_first, t - FIRST_TILES)
            r_out[(b - first) * 16 : (b - first) * 16 + 16, cols] = value * rel_scale
            n = rels - b * 16
            if n < 16:
                l_out[cols] = (value[n : n + 1] * self_scale).reshape(128)
        for n in range(11):
            store(n).wait()


def unpack(full, grad_src, grad_tgt, rels, width, **scales):
    rows = REL_BLOCK * 16
    return pl.pallas_call(
        functools.partial(unpack_kernel, rels=rels, **scales),
        grid=(-(-(rels + 1) // rows),),
        out_shape=(
            jax.ShapeDtypeStruct((3, width, width), F32),
            jax.ShapeDtypeStruct((rels, width), F32),
            jax.ShapeDtypeStruct((width,), F32),
            jax.ShapeDtypeStruct(grad_src.shape, F32),
            jax.ShapeDtypeStruct(grad_tgt.shape, F32),
        ),
        in_specs=[ANY] * 3,
        out_specs=[
            ANY,
            pl.BlockSpec((rows, width), lambda i: (i, 0)),
            pl.BlockSpec((width,), lambda i: (0,)),
            ANY,
            ANY,
        ],
        scratch_shapes=[
            pltpu.VMEM(full.shape, BF16),
            pltpu.VMEM((3, width, width), F32),
            pltpu.VMEM(grad_src.shape, F32),
            pltpu.VMEM(grad_tgt.shape, F32),
            DMA((13,)),
            DMA((11,)),
        ],
        compiler_params=pltpu.CompilerParams(vmem_limit_bytes=VMEM_BYTES),
        name="unpack",
    )(full, grad_src, grad_tgt)


def body(
    h_src, rel_table, cotangent, h_tgt, loop_rel, weights, src_index, tgt_index, rel_ids, direction, counts
):
    width = weights.shape[1]
    tiles, edge = src_index.shape[2:]
    rels = rel_table.shape[0]
    h_all, c_all, s8, t8, r8, back, lsum = gather(
        h_src, cotangent, weights, h_tgt, loop_rel, *[a.reshape(tiles, edge) for a in (src_index, tgt_index, rel_ids, direction)]
    )
    g, hi, lo, rest, keep, give = edges(
        counts.reshape(1), s8, t8, r8, h_all, c_all, weights, rel_table, lsum
    )
    full, mine = reduce_all(
        keep, give, g, hi, lo, c_all, rest, cotangent, h_tgt, loop_rel
    )
    devices = lax.axis_size("src") * lax.axis_size("tgt")
    edges_all = float(devices * tiles * edge)
    targets_all = float(devices * cotangent.shape[0])
    grad_weights, grad_rel, grad_loop, grad_src, grad_tgt = unpack(
        full,
        mine,
        back,
        rels,
        width,
        edge_scale=edges_all**-0.5,
        self_scale=targets_all**-0.5,
        rel_scale=(float(rels) / edges_all) ** 0.5,
    )
    return grad_src, grad_tgt, grad_weights, grad_rel, grad_loop


def solution(mesh):
    return jax.shard_map(
        body,
        mesh=mesh,
        in_specs=(
            P(("src", "tgt"), None),
            P(),
            P(("tgt", "src"), None),
            P(("tgt", "src"), None),
            P(),
            P(),
            P("src", "tgt", None, None),
            P("src", "tgt", None, None),
            P("src", "tgt", None, None),
            P("src", "tgt", None, None),
            P("src", "tgt"),
        ),
        out_specs=(P(("src", "tgt"), None), P(("tgt", "src"), None), P(), P(), P()),
        check_vma=False,
    )
```

```python
import functools

import jax
import jax.numpy as jnp
from jax import lax
from jax.experimental import pallas as pl
from jax.experimental.pallas import tpu as pltpu
from jax.sharding import PartitionSpec as P

F32 = jnp.float32
BF16 = jnp.bfloat16
MESH = pl.DeviceIdType.MESH
ANY = pl.BlockSpec(memory_space=pl.ANY)
VMEM = pl.BlockSpec(memory_space=pltpu.VMEM)
SMEM = pl.BlockSpec(memory_space=pltpu.SMEM)
DMA = pltpu.SemaphoreType.DMA

WAVE_HALF = (4096, 7168)
HALF_ROWS = sum(WAVE_HALF)
FIRST_TILES = 2 * WAVE_HALF[0] // 16
SECOND_HALF_TILES = WAVE_HALF[1] // 16
W_TILES = 864
PARTS = (
    (("x", "y", "z"), 32),
    (("y", "z", "x"), 32),
    (("z", "x", "y"), 48),
    (("x", "y", "z"), 32),
    (("y", "z", "x"), 32),
)
BASES = (0, 2048, 4096, 7168, 9216)
UNROLL = 32
EDGE = 128
VMEM_BYTES = 63 * 2**20


class Place:
    def __init__(self):
        s, t = lax.axis_index("src"), lax.axis_index("tgt")
        self.x_lo, self.core = s // 8, s % 2
        self.x_hi = t // 4
        self.at = {"x": self.x_hi * 2 + self.x_lo, "y": (s // 2) % 4, "z": t % 4}

    def device(self, at, core):
        return ((at["x"] % 2) * 8 + at["y"] * 2 + core, (at["x"] // 2) * 4 + at["z"])

    def along(self, axis, offset):
        at = dict(self.at)
        at[axis] = (at[axis] + offset) % 4
        return self.device(at, self.core)

    def sibling(self):
        return self.device(self.at, 1 - self.core)

    def x_lo_partner(self):
        at = dict(self.at)
        at["x"] = self.x_hi * 2 + (1 - self.x_lo)
        return self.device(at, self.core)


def greet(partners):
    barrier = pltpu.get_barrier_semaphore()
    for partner in partners:
        pl.semaphore_signal(barrier, inc=1, device_id=partner, device_id_type=MESH)
    pl.semaphore_wait(barrier, len(partners))


def push(src, dst, send, recv, device):
    return pltpu.make_async_remote_copy(
        src_ref=src, dst_ref=dst, send_sem=send, recv_sem=recv, device_id=device, device_id_type=MESH
    )


def gather_kernel(
    h_ref, c_ref, w_hbm, src_ref, tgt_ref, rel_ref, dir_ref, own_c, own_h, loop_ref,
    h_all, c_all, s8, t8, r8, t_out, l_out, w_ref, local, hx_s, hx_r, hz_s, hz_r, cy_s, cy_r, cx_s, cx_r, cs_s, cs_r
):
    me = Place()
    x_lo, x_hi, core, y, z = me.x_lo, me.x_hi, me.core, me.at["y"], me.at["z"]
    sibling, across = me.sibling(), me.x_lo_partner()
    own_h_copy = pltpu.make_async_copy(h_ref, h_all.at[x_hi, z], local.at[0])
    own_c_copy = pltpu.make_async_copy(c_ref, c_all.at[x_lo, y, core], local.at[1])
    w_self = pltpu.make_async_copy(w_hbm.at[2], w_ref, local.at[2])
    w_self.start()
    own_h_copy.start()
    own_c_copy.start()
    s8[...] = src_ref[...] * 8
    t8[...] = (tgt_ref[...] + dir_ref[...] * (16 * c_ref.shape[0])) * 8
    r8[...] = rel_ref[...] * 8
    greet(
        [me.along("x", 2), across, sibling]
        + [me.along("y", k) for k in (1, 2, 3)]
        + [me.along("z", k) for k in (1, 2, 3)]
    )
    mine, theirs = h_all.at[x_hi, z], h_all.at[1 - x_hi, z]
    hx = push(h_ref, mine, hx_s, hx_r, me.along("x", 2))
    hx.start()
    cy, hz = [], []
    for k in (1, 3, 2):
        copy = push(h_ref, mine, hz_s.at[k - 1], hz_r.at[k - 1], me.along("z", k))
        copy.start()
        hz.append(copy)
        copy = push(c_ref, c_all.at[x_lo, y, core], cy_s.at[k - 1], cy_r.at[k - 1], me.along("y", k))
        copy.start()
        cy.append(copy)
    hx.wait()
    for k in (1, 3, 2):
        copy = push(theirs, theirs, hz_s.at[k + 2], hz_r.at[k + 2], me.along("z", k))
        copy.start()
        hz.append(copy)
    own_c_copy.wait()
    for copy in cy:
        copy.wait_recv()
    near = c_all.at[x_lo, :, core]
    far = c_all.at[1 - x_lo, :, core]
    cx = push(near, near, cx_s, cx_r, across)
    cx.start()
    first = push(near, near, cs_s.at[0], cs_r.at[0], sibling)
    first.start()
    w_self.wait()
    back = lax.dot_general(own_c[...], w_ref[...], (((1,), (1,)), ((), ())), preferred_element_type=F32)
    t_out[...] = back * loop_ref[...].astype(F32).reshape(1, back.shape[1])
    l_out[...] = jnp.sum(back * own_h[...].astype(F32), axis=0, keepdims=True)
    cx.wait()
    second = push(far, far, cs_s.at[1], cs_r.at[1], sibling)
    second.start()
    first.wait()
    second.wait()
    own_h_copy.wait()
    for copy in hz:
        copy.wait()
    for copy in cy:
        copy.wait_send()


def gather(h_src, cotangent, weights, h_tgt, loop, *indices):
    rows, width = h_src.shape
    trows = cotangent.shape[0]
    h_all, c_all, s8, t8, r8, grad_tgt, lsum = pl.pallas_call(
        gather_kernel,
        out_shape=(
            jax.ShapeDtypeStruct((2, 4, rows, width), BF16),
            jax.ShapeDtypeStruct((2, 4, 2, trows, width), BF16),
            *[jax.ShapeDtypeStruct(indices[0].shape, jnp.int32)] * 3,
            jax.ShapeDtypeStruct((trows, width), F32),
            jax.ShapeDtypeStruct((1, width), F32),
        ),
        in_specs=[ANY] * 3 + [VMEM] * 7,
        out_specs=[ANY] * 2 + [VMEM] * 5,
        scratch_shapes=[
            pltpu.VMEM((width, width), BF16),
            DMA((3,)), DMA, DMA, DMA((6,)), DMA((6,)), DMA((3,)), DMA((3,)), DMA, DMA, DMA((2,)), DMA((2,)),
        ],
        compiler_params=pltpu.CompilerParams(collective_id=0, has_side_effects=True, vmem_limit_bytes=VMEM_BYTES),
        name="gather_panels",
    )(h_src, cotangent, weights, *indices, cotangent, h_tgt, loop)
    flat = [a.reshape(-1) for a in (s8, t8, r8)]
    return h_all.reshape(8 * rows, width), c_all.reshape(16 * trows, width), *flat, grad_tgt, lsum


def edge_kernel(
    live_ref, src_ref, tgt_ref, rel_ref, h_hbm, c_hbm, w_hbm, z_hbm, lsum,
    g_out, hi_out, lo_out, rest_out, keep_out, give_out,
    h_ref, c_ref, w_ref, z_ref, g_ref, keep, give, hx, px, zx, gs, aa, rr, hi, lo, in_sem, out_sem,
):
    loads = [
        pltpu.make_async_copy(a, b, in_sem.at[i])
        for i, (a, b) in enumerate(((h_hbm, h_ref), (z_hbm, z_ref), (c_hbm, c_ref), (w_hbm.at[pl.ds(0, 2)], w_ref)))
    ]
    for load in loads:
        load.start()
    core = lax.axis_index("src") % 2
    rows = h_ref.shape[0]
    trows = c_ref.shape[0]
    rels, width = z_ref.shape
    chunks = width // 128

    def spread(dst, row, value):
        for c in range(chunks):
            dst[pl.ds(row * 8 + c, value.shape[0], stride=8), :] = value[:, c * 128 : (c + 1) * 128]

    zero = jnp.zeros((64, 128), F32)
    for ref in (gs, aa, rr):

        @pl.loop(0, ref.shape[0] // 64)
        def _(i, ref=ref):
            ref[pl.ds(pl.multiple_of(i * 64, 64), 64), :] = zero

    loads[0].wait()

    @pl.loop(0, rows // 16)
    def _(i):
        r = pl.multiple_of(i * 16, 16)
        spread(hx, r, h_ref[pl.ds(r, 16), :].astype(F32))

    loads[1].wait()

    @pl.loop(0, rels // 16)
    def _(i):
        r = pl.multiple_of(i * 16, 16)
        spread(zx, r, z_ref[pl.ds(r, 16), :].astype(F32))

    tail = rels // 16 * 16
    if tail < rels:
        spread(zx, tail, z_ref[tail:rels, :].astype(F32))
    loads[2].wait()
    loads[3].wait()
    for d in range(2):
        for k in range(width // 256):
            p = lax.dot_general(
                c_ref[...], w_ref[d, k * 256 : (k + 1) * 256, :], (((1,), (1,)), ((), ())),
                preferred_element_type=F32,
            )
            for h in range(2):
                px[pl.ds(d * trows * 8 + 2 * k + h, trows, stride=8), :] = p[:, h * 128 : (h + 1) * 128]
    def row(at):
        return pl.ds(pl.multiple_of(at, 8), 8)

    @pl.loop(0, live_ref[0] * (EDGE // UNROLL))
    def _(i):
        start = i * UNROLL
        for u in range(0, UNROLL, 2):
            s0, s1 = src_ref[start + u], src_ref[start + u + 1]
            t0, t1 = tgt_ref[start + u], tgt_ref[start + u + 1]
            r0, r1 = rel_ref[start + u], rel_ref[start + u + 1]
            h0, h1 = hx[row(s0), :], hx[row(s1), :]
            p0, p1 = px[row(t0), :], px[row(t1), :]
            z0, z1 = zx[row(r0), :], zx[row(r1), :]
            for ref, at0, at1, v0, v1 in (
                (gs, s0, s1, p0 * z0, p1 * z1),
                (aa, t0, t1, (h0 * z0).astype(BF16).astype(F32), (h1 * z1).astype(BF16).astype(F32)),
                (rr, r0, r1, p0 * h0, p1 * h1),
            ):
                sum0 = ref[row(at0), :] + v0
                sum1 = ref[row(at1), :] + v1 + jnp.where(at0 == at1, v0, jnp.zeros_like(v0))
                ref[row(at0), :] = sum0
                ref[row(at1), :] = sum1

    for c in range(chunks):
        rr[rels * 8 + c : rels * 8 + c + 1, :] = lsum[:, c * 128 : (c + 1) * 128]
    blocks = rr.shape[0] // 128

    def rel_tile(block, c):
        return rr[pl.ds(block * 128 + c, 16, stride=8), :]

    def collect(half, ref):
        first = half * (FIRST_TILES // 2)
        last = first + FIRST_TILES // 2

        @pl.loop(-(-first // chunks), last // chunks)
        def _(i):
            for c in range(chunks):
                row = pl.multiple_of((i * chunks + c - first) * 16, 16)
                ref[pl.ds(row, 16), :] = rel_tile(i, c).astype(ref.dtype)

        edge_tiles = [*range(first, -(-first // chunks) * chunks), *range(last // chunks * chunks, last)]
        for t in edge_tiles:
            row = (t - first) * 16
            ref[row : row + 16, :] = rel_tile(t // chunks, t % chunks).astype(ref.dtype)

    @pl.when(core == 0)
    def _():
        collect(0, keep)
        collect(1, give)

    @pl.when(core != 0)
    def _():
        collect(1, keep)
        collect(0, give)

    stores = [
        pltpu.make_async_copy(keep, keep_out, out_sem.at[0]),
        pltpu.make_async_copy(give, give_out, out_sem.at[1]),
    ]
    for store in stores:
        store.start()
    for t in range(FIRST_TILES, blocks * chunks):
        row = (t - FIRST_TILES) * 16
        rest_out[row : row + 16, :] = rel_tile(t // chunks, t % chunks)

    @pl.loop(0, 2 * trows // 16)
    def _(i):
        r = pl.multiple_of(i * 16, 16)
        for c in range(chunks):
            a = aa[pl.ds(r * 8 + c, 16, stride=8), :]
            top = a.astype(BF16)
            hi[pl.ds(r, 16), c * 128 : (c + 1) * 128] = top
            lo[pl.ds(r, 16), c * 128 : (c + 1) * 128] = (a - top.astype(F32)).astype(BF16)

    stores.append(pltpu.make_async_copy(hi, hi_out, out_sem.at[2]))
    stores.append(pltpu.make_async_copy(lo, lo_out, out_sem.at[3]))
    stores[2].start()
    stores[3].start()

    @pl.loop(0, rows // 16)
    def _(i):
        r = pl.multiple_of(i * 16, 16)
        for c in range(chunks):
            g_ref[pl.ds(r, 16), c * 128 : (c + 1) * 128] = gs[pl.ds(r * 8 + c, 16, stride=8), :].astype(BF16)

    stores.append(pltpu.make_async_copy(g_ref, g_out, out_sem.at[4]))
    stores[4].start()
    for store in stores:
        store.wait()


def edges(live, s8, t8, r8, h, c, w, z, lsum):
    rows, width = h.shape
    trows = c.shape[0]
    rpad = (z.shape[0] + 16) // 16 * 16
    return pl.pallas_call(
        edge_kernel,
        out_shape=(
            jax.ShapeDtypeStruct((rows, width), BF16),
            jax.ShapeDtypeStruct((2 * trows, width), BF16),
            jax.ShapeDtypeStruct((2 * trows, width), BF16),
            jax.ShapeDtypeStruct((rpad // 16 * (width // 128) * 16 - FIRST_TILES * 16, 128), F32),
            jax.ShapeDtypeStruct((WAVE_HALF[0], 128), F32),
            jax.ShapeDtypeStruct((WAVE_HALF[0], 128), F32),
        ),
        in_specs=[SMEM] * 4 + [ANY] * 4 + [VMEM],
        out_specs=[ANY, ANY, ANY, VMEM, ANY, ANY],
        scratch_shapes=[
            pltpu.VMEM(h.shape, BF16),
            pltpu.VMEM(c.shape, BF16),
            pltpu.VMEM((2, width, width), BF16),
            pltpu.VMEM(z.shape, BF16),
            pltpu.VMEM((rows, width), BF16),
            pltpu.VMEM((WAVE_HALF[0], 128), F32),
            pltpu.VMEM((WAVE_HALF[0], 128), F32),
            pltpu.VMEM((rows * 8, 128), F32),
            pltpu.VMEM((2 * trows * 8, 128), F32),
            pltpu.VMEM((rpad * 8, 128), F32),
            pltpu.VMEM((rows * 8, 128), F32),
            pltpu.VMEM((2 * trows * 8, 128), F32),
            pltpu.VMEM((rpad * 8, 128), F32),
            pltpu.VMEM((2 * trows, width), BF16),
            pltpu.VMEM((2 * trows, width), BF16),
            DMA((4,)),
            DMA((5,)),
        ],
        compiler_params=pltpu.CompilerParams(vmem_limit_bytes=VMEM_BYTES),
        name="edges",
    )(live, s8, t8, r8, h, c, w, z, lsum)


def reduce_kernel(
    keep_hbm, give, g_ref, hi_hbm, lo_hbm, c_hbm, rest, own_c, own_h, loop_ref, full, g_out,
    keep, given, hi, lo, c_all, g_own, pair, out1, in1, acc1, out2, in2, unit, g_in, g_acc, g_send, g_side,
    pair_s, pair_r, s1, r1, s2, r2, s4, r4, s6, r6, sib_s, sib_r, gz_s, gz_r, gx_s, gx_r,
    local, kept,
):
    me = Place()
    core = me.core
    sibling = me.sibling()
    x_hi, z = me.x_hi, me.at["z"]
    width = c_all.shape[1]
    trows = c_all.shape[0]
    chunks = width // 128
    parts = range(len(PARTS))

    def at(p, depth):
        return me.at[PARTS[p][0][depth]]

    def along(p, depth, j):
        return me.along(PARTS[p][0][depth], j)

    def in_plane(p, j, k):
        where = dict(me.at)
        where[PARTS[p][0][1]] = (at(p, 1) + j) % 4
        where[PARTS[p][0][2]] = (at(p, 2) + k) % 4
        return me.device(where, core)

    others = [(2, 2), (2, 1), (2, 3), (1, 2), (3, 2), (1, 1), (1, 3), (3, 1), (3, 3)]
    others += [(2, 0), (0, 2), (1, 0), (3, 0), (0, 1), (0, 3)]

    def rows_of(p, a):
        size = PARTS[p][1] * 16
        return pl.ds(pl.multiple_of(BASES[p] + a * size, 16), size)

    first_rows = pl.ds(0, WAVE_HALF[0])
    loads = [
        pltpu.make_async_copy(a, b, kept.at[n])
        for n, (a, b) in enumerate(
            (
                (keep_hbm, keep.at[first_rows]),
                (hi_hbm, hi),
                (c_hbm, c_all),
                (lo_hbm, lo),
                (g_ref.at[:, z], g_own),
            )
        )
    ]
    for load in loads:
        load.start()
    plane = [me.along(axis, k) for axis in ("x", "y", "z") for k in (1, 2, 3)]
    for p in (0, 1, 2):
        plane += [in_plane(p, j, k) for j, k in others[:9]]
    greet(plane + [sibling])

    pairs, step1, step6, side, own = {}, {}, {}, {}, {}

    def send_pair(some):
        for j in (1, 2, 3, 0):
            for p in some:
                where = rows_of(p, (at(p, 0) + j) % 4)
                if BASES[p] < WAVE_HALF[0]:
                    source = give.at[where]
                else:
                    row = BASES[p] - WAVE_HALF[0] + ((at(p, 0) + j) % 4) * (PARTS[p][1] * 16)
                    source = given.at[pl.ds(pl.multiple_of(row, 16), PARTS[p][1] * 16)]
                copy = push(source, pair.at[where], pair_s.at[p * 4 + j], pair_r.at[p * 4 + j], sibling)
                copy.start()
                pairs[p, j] = copy

    def send_first(some):
        for j in (1, 2, 3):
            for p in some:
                size = PARTS[p][1] * 16
                base = BASES[p] + ((at(p, 0) + j) % 4) * size
                pairs[p, j].wait_recv()

                @pl.loop(0, size // 128)
                def _(i, base=base):
                    r = pl.ds(pl.multiple_of(base + i * 128, 16), 128)
                    out1[r, :] = (keep[r, :] + pair[r, :]).astype(BF16)

                copy = push(
                    out1.at[rows_of(p, (at(p, 0) + j) % 4)],
                    in1.at[j - 1, pl.ds(BASES[p] // 4, size)],
                    s1.at[p * 3 + j - 1],
                    r1.at[p * 3 + j - 1],
                    along(p, 0, j),
                )
                copy.start()
                step1[p, j] = copy

    def send_second(p):
        size = PARTS[p][1]
        base = BASES[p] + at(p, 0) * (size * 16)
        low = BASES[p] // 4
        pairs[p, 0].wait_recv()
        for j in (1, 2, 3):
            step1[p, j].wait_recv()

        @pl.loop(0, size * 16 // 128)
        def _(i):
            r = pl.ds(pl.multiple_of(base + i * 128, 16), 128)
            q = pl.ds(pl.multiple_of(low + i * 128, 16), 128)
            total = (
                keep[r, :]
                + pair[r, :]
                + in1[0, q, :].astype(F32)
                + in1[1, q, :].astype(F32)
                + in1[2, q, :].astype(F32)
            )
            acc1[q, :] = total
            out2[q, :] = total.astype(BF16)

        for j, k in others:
            row = low + (((at(p, 1) + j) % 4) * 4 + (at(p, 2) + k) % 4) * size
            push(
                out2.at[pl.ds(pl.multiple_of(row, 16), size)],
                in2.at[j * 4 + k - 1, pl.ds(BASES[p] // 64, size)],
                s2.at[p],
                r2.at[p],
                in_plane(p, j, k),
            ).start()

    def second(p):
        mine = out2.at[pl.ds(BASES[p] // 4, PARTS[p][1] * 15)]
        return push(mine, in2.at[:, pl.ds(BASES[p] // 64, PARTS[p][1])], s2.at[p], r2.at[p], in_plane(p, 1, 1))

    def start_of(p):
        if BASES[p] < WAVE_HALF[0]:
            return core * WAVE_HALF[0] + BASES[p]
        return 2 * WAVE_HALF[0] + core * WAVE_HALF[1] + (BASES[p] - WAVE_HALF[0])

    def place(p, depth):
        size = PARTS[p][1]
        row = start_of(p) + at(p, 0) * (size * 16)
        if depth > 1:
            row = row + at(p, 1) * (size * 4)
        if depth > 2:
            row = row + at(p, 2) * size
        return full.at[pl.ds(pl.multiple_of(row, 16), (size * 16, size * 4, size)[depth - 1])]

    def half_of(p, offset, half):
        size = PARTS[p][1] * 8
        row = start_of(p) + ((at(p, 0) + 4 + offset) % 4) * (2 * size) + half * size
        return full.at[pl.ds(pl.multiple_of(row, 16), size)]

    def share_second(p):
        size = PARTS[p][1]
        second(p).wait_recv()
        q = pl.ds(BASES[p] // 64, size)
        mine = pl.ds(pl.multiple_of(BASES[p] // 4 + (at(p, 1) * 4 + at(p, 2)) * size, 16), size)
        total = acc1[mine, :]
        for n in range(15):
            total = total + in2[n, q, :].astype(F32)
        unit[q, :] = total.astype(BF16)
        for j, k in others:
            push(unit.at[q], place(p, 3), s4.at[p], r4.at[p], in_plane(p, j, k)).start()
        own[p] = pltpu.make_async_copy(unit.at[q], place(p, 3), local.at[p])
        own[p].start()

    def shared(p):
        where = pl.ds(pl.multiple_of(start_of(p) + at(p, 0) * (PARTS[p][1] * 16), 16), PARTS[p][1] * 15)
        return push(full.at[where], full.at[where], s4.at[p], r4.at[p], in_plane(p, 1, 1))

    def to_other_core(p, n, block):
        side[p, n] = push(block, block, sib_s.at[p * 7 + n], sib_r.at[p * 7 + n], sibling)
        side[p, n].start()

    def share_first(p):
        own[p].wait()
        shared(p).wait_recv()
        for n, (to, half) in enumerate(((1, 0), (3, 1), (1, 1), (3, 0))):
            block = half_of(p, 0, half)
            copy = push(block, block, s6.at[p * 6 + n], r6.at[p * 6 + n], along(p, 0, to))
            copy.start()
            step6[p, n] = copy
        to_other_core(p, 0, place(p, 1))

    def forward(p):
        for n, (to, half) in enumerate(((1, 0), (3, 1))):
            step6[p, n].wait_recv()
            block = half_of(p, -to, half)
            copy = push(block, block, s6.at[p * 6 + 4 + n], r6.at[p * 6 + 4 + n], along(p, 0, to))
            copy.start()
            step6[p, 4 + n] = copy
            to_other_core(p, 1 + n, block)

    def finish(p):
        for n, (to, half) in enumerate(((1, 1), (3, 0))):
            step6[p, 2 + n].wait_recv()
            to_other_core(p, 3 + n, half_of(p, -to, half))
        for half in range(2):
            step6[p, 4 + half].wait_recv()
            to_other_core(p, 5 + half, half_of(p, 2, half))

    def put(first, value):
        here = value.shape[0] // 16 * chunks
        for half in range(2):
            begin = max(first, half * SECOND_HALF_TILES)
            end = min(first + here, (half + 1) * SECOND_HALF_TILES)
            if begin >= end:
                continue

            def store(ref, base, half=half, begin=begin, end=end):
                for t in range(begin, end):
                    row = base + (t - half * SECOND_HALF_TILES) * 16
                    b, c = (t - first) // chunks, (t - first) % chunks
                    ref[row : row + 16, :] = value[b * 16 : b * 16 + 16, c * 128 : c * 128 + 128].astype(ref.dtype)

            @pl.when(core == half)
            def _(store=store):
                store(keep, WAVE_HALF[0])

            @pl.when(core != half)
            def _(store=store):
                store(given, 0)

    def make_wsum(d):
        rows = slice(d * trows, (d + 1) * trows)
        for k in range(width // 256):
            cols = slice(k * 256, (k + 1) * 256)
            w = lax.dot_general(
                hi[rows, cols], c_all[...], (((0,), (0,)), ((), ())), preferred_element_type=F32
            ) + lax.dot_general(
                lo[rows, cols], c_all[...], (((0,), (0,)), ((), ())), preferred_element_type=F32
            )
            put((d * 48 + k * 16) * chunks, w)

    def make_wself():
        self_comp = (own_h[...].astype(F32) * loop_ref[...].astype(F32).reshape(1, width)).astype(BF16)
        for k in range(width // 256):
            w = lax.dot_general(
                self_comp[:, k * 256 : (k + 1) * 256], own_c[...], (((0,), (0,)), ((), ())),
                preferred_element_type=F32,
            )
            put((96 + k * 16) * chunks, w)
        low = (W_TILES - SECOND_HALF_TILES) * 16
        n = rest.shape[0]

        def store(ref, base):
            ref[base + low : base + low + n, :] = rest[...].astype(ref.dtype)
            ref[base + low + n : base + WAVE_HALF[1], :] = jnp.zeros((WAVE_HALF[1] - low - n, 128), ref.dtype)

        @pl.when(core == 1)
        def _():
            store(keep, WAVE_HALF[0])

        @pl.when(core != 1)
        def _():
            store(given, 0)

    send_pair((0, 1))
    gz = []
    for k in (1, 3, 2):
        copy = push(g_ref.at[:, (z + k) % 4], g_in.at[k - 1], gz_s.at[k - 1], gz_r.at[k - 1], me.along("z", k))
        copy.start()
        gz.append(copy)
    loads[0].wait()
    for load in loads[1:]:
        load.wait()
    make_wsum(0)
    make_wsum(1)
    make_wself()
    send_pair((2, 3, 4))
    send_first((0, 1, 2, 3, 4))
    send_second(0)
    send_second(1)
    send_second(2)
    send_second(3)
    send_second(4)
    share_second(0)
    share_second(1)
    share_second(2)
    share_second(3)
    share_second(4)
    for copy in gz:
        copy.wait_recv()
    for half in range(2):
        g_acc[half] = (
            g_own[half].astype(F32)
            + g_in[0, half].astype(F32)
            + g_in[1, half].astype(F32)
            + g_in[2, half].astype(F32)
        )
    g_send[...] = g_acc[1 - x_hi].astype(BF16)
    gx = push(g_send, g_side, gx_s, gx_r, me.along("x", 2))
    gx.start()
    share_first(0)
    share_first(1)
    share_first(2)
    share_first(3)
    share_first(4)
    forward(0)
    forward(1)
    forward(2)
    forward(3)
    forward(4)
    finish(0)
    finish(1)
    gx.wait_recv()
    g_out[...] = g_acc[x_hi] + g_side[...].astype(F32)
    finish(2)
    finish(3)
    finish(4)
    for copy in side.values():
        copy.wait_recv()
    gx.wait_send()
    for copy in gz:
        copy.wait_send()
    for group in (pairs, step1, step6, side):
        for copy in group.values():
            copy.wait_send()
    for p in parts:
        second(p).wait_send()
        shared(p).wait_send()


def reduce_all(keep, give, g, hi, lo, c_all, rest, own_c, own_h, loop):
    rows, width = g.shape
    g = g.reshape(2, 4, rows // 8, width)
    n = len(PARTS)
    return pl.pallas_call(
        reduce_kernel,
        out_shape=(
            jax.ShapeDtypeStruct((2 * HALF_ROWS, 128), BF16),
            jax.ShapeDtypeStruct((rows // 8, width), F32),
        ),
        in_specs=[ANY] * 6 + [VMEM] * 4,
        out_specs=[ANY, VMEM],
        scratch_shapes=[
            pltpu.VMEM((HALF_ROWS, 128), F32),
            pltpu.VMEM((WAVE_HALF[1], 128), F32),
            pltpu.VMEM(hi.shape, BF16),
            pltpu.VMEM(lo.shape, BF16),
            pltpu.VMEM(c_all.shape, BF16),
            pltpu.VMEM((2, rows // 8, width), BF16),
            pltpu.VMEM((HALF_ROWS, 128), F32),
            pltpu.VMEM((HALF_ROWS, 128), BF16),
            pltpu.VMEM((3, HALF_ROWS // 4, 128), BF16),
            pltpu.VMEM((HALF_ROWS // 4, 128), F32),
            pltpu.VMEM((HALF_ROWS // 4, 128), BF16),
            pltpu.VMEM((15, HALF_ROWS // 64, 128), BF16),
            pltpu.VMEM((HALF_ROWS // 64, 128), BF16),
            pltpu.VMEM((3, 2, rows // 8, width), BF16),
            pltpu.VMEM((2, rows // 8, width), F32),
            pltpu.VMEM((rows // 8, width), BF16),
            pltpu.VMEM((rows // 8, width), BF16),
            *[DMA((4 * n,))] * 2, *[DMA((3 * n,))] * 2, *[DMA((n,))] * 4, *[DMA((6 * n,))] * 2, *[DMA((7 * n,))] * 2,
            DMA((3,)), DMA((3,)), DMA, DMA, DMA((n,)), DMA((5,)),
        ],
        compiler_params=pltpu.CompilerParams(
            collective_id=1, has_side_effects=True, vmem_limit_bytes=VMEM_BYTES
        ),
        name="reduce_all",
    )(keep, give, g, hi, lo, c_all, rest, own_c, own_h, loop)


REL_BLOCK = 18


def unpack_kernel(
    full_hbm, gs_in, gt_in, w_hbm, r_out, l_out, gs_out, gt_out, full, w_out, gs, gt, in_sem, out_sem,
    *, rels, edge_scale, self_scale, rel_scale,
):
    step = pl.program_id(0)
    last_step = -(-(rels + 1) // (REL_BLOCK * 16)) - 1
    width = r_out.shape[1]
    chunks = width // 128
    per = width // 16
    group = per // 3
    pieces = in_sem.shape[0] - 2
    size = full.shape[0] // pieces

    def load(i):
        if i >= pieces:
            source, target = ((gs_in, gs), (gt_in, gt))[i - pieces]
            return pltpu.make_async_copy(source, target, in_sem.at[i])
        where = pl.ds(i * size, size)
        return pltpu.make_async_copy(full_hbm.at[where], full.at[where], in_sem.at[i])

    def store(n):
        if n < 9:
            where = pl.ds(n % 3 * group * 16, group * 16)
            return pltpu.make_async_copy(w_out.at[n // 3, where], w_hbm.at[n // 3, where], out_sem.at[n])
        source, target = ((gs, gs_out), (gt, gt_out))[n - 9]
        return pltpu.make_async_copy(source, target, out_sem.at[n])

    def tile(first, index):
        return full[pl.ds(pl.multiple_of(first + index * 16, 16), 16), :].astype(F32)

    w_first = 2 * WAVE_HALF[0]
    rest_first = w_first + W_TILES * 16

    @pl.when(step == 0)
    def _():
        order = [*range(w_first // size, pieces), *range(w_first // size), pieces, pieces + 1]
        for i in order:
            load(i).start()
        waited = 0
        for n in range(9):
            end = w_first + (n + 1) * group * chunks * 16
            while order[waited] * size < end and waited < pieces - w_first // size:
                load(order[waited]).wait()
                waited += 1
            d, scale = n // 3, (edge_scale, edge_scale, self_scale)[n // 3]

            @pl.loop(n % 3 * group, (n % 3 + 1) * group)
            def _(i, d=d, scale=scale):
                for c in range(chunks):
                    w_out[d, pl.ds(pl.multiple_of(i * 16, 16), 16), c * 128 : (c + 1) * 128] = (
                        tile(w_first, (d * per + i) * chunks + c) * scale
                    )

            store(n).start()
        for i in order[waited:]:
            load(i).wait()
        store(9).start()
        store(10).start()

    @pl.when(step != last_step)
    def _():
        @pl.loop(0, REL_BLOCK)
        def _(i):
            for c in range(chunks):
                r_out[pl.ds(pl.multiple_of(i * 16, 16), 16), c * 128 : (c + 1) * 128] = (
                    tile(0, (step * REL_BLOCK + i) * chunks + c) * rel_scale
                )

    @pl.when(step == last_step)
    def _():
        first = last_step * REL_BLOCK
        for t in range(first * chunks, -(-(rels + 1) // 16) * chunks):
            b, cols = t // chunks, slice(t % chunks * 128, t % chunks * 128 + 128)
            value = tile(0, t) if t < FIRST_TILES else tile(rest_first, t - FIRST_TILES)
            r_out[(b - first) * 16 : (b - first) * 16 + 16, cols] = value * rel_scale
            n = rels - b * 16
            if n < 16:
                l_out[cols] = (value[n : n + 1] * self_scale).reshape(128)
        for n in range(11):
            store(n).wait()


def unpack(full, grad_src, grad_tgt, rels, width, **scales):
    rows = REL_BLOCK * 16
    return pl.pallas_call(
        functools.partial(unpack_kernel, rels=rels, **scales),
        grid=(-(-(rels + 1) // rows),),
        out_shape=(
            jax.ShapeDtypeStruct((3, width, width), F32),
            jax.ShapeDtypeStruct((rels, width), F32),
            jax.ShapeDtypeStruct((width,), F32),
            jax.ShapeDtypeStruct(grad_src.shape, F32),
            jax.ShapeDtypeStruct(grad_tgt.shape, F32),
        ),
        in_specs=[ANY] * 3,
        out_specs=[
            ANY,
            pl.BlockSpec((rows, width), lambda i: (i, 0)),
            pl.BlockSpec((width,), lambda i: (0,)),
            ANY,
            ANY,
        ],
        scratch_shapes=[
            pltpu.VMEM(full.shape, BF16),
            pltpu.VMEM((3, width, width), F32),
            pltpu.VMEM(grad_src.shape, F32),
            pltpu.VMEM(grad_tgt.shape, F32),
            DMA((13,)),
            DMA((11,)),
        ],
        compiler_params=pltpu.CompilerParams(vmem_limit_bytes=VMEM_BYTES),
        name="unpack",
    )(full, grad_src, grad_tgt)


def body(
    h_src, rel_table, cotangent, h_tgt, loop_rel, weights, src_index, tgt_index, rel_ids, direction, counts
):
    width = weights.shape[1]
    tiles, edge = src_index.shape[2:]
    rels = rel_table.shape[0]
    h_all, c_all, s8, t8, r8, back, lsum = gather(
        h_src, cotangent, weights, h_tgt, loop_rel, *[a.reshape(tiles, edge) for a in (src_index, tgt_index, rel_ids, direction)]
    )
    g, hi, lo, rest, keep, give = edges(
        counts.reshape(1), s8, t8, r8, h_all, c_all, weights, rel_table, lsum
    )
    full, mine = reduce_all(
        keep, give, g, hi, lo, c_all, rest, cotangent, h_tgt, loop_rel
    )
    devices = lax.axis_size("src") * lax.axis_size("tgt")
    edges_all = float(devices * tiles * edge)
    targets_all = float(devices * cotangent.shape[0])
    grad_weights, grad_rel, grad_loop, grad_src, grad_tgt = unpack(
        full,
        mine,
        back,
        rels,
        width,
        edge_scale=edges_all**-0.5,
        self_scale=targets_all**-0.5,
        rel_scale=(float(rels) / edges_all) ** 0.5,
    )
    return grad_src, grad_tgt, grad_weights, grad_rel, grad_loop


def solution(mesh):
    return jax.shard_map(
        body,
        mesh=mesh,
        in_specs=(
            P(("src", "tgt"), None),
            P(),
            P(("tgt", "src"), None),
            P(("tgt", "src"), None),
            P(),
            P(),
            P("src", "tgt", None, None),
            P("src", "tgt", None, None),
            P("src", "tgt", None, None),
            P("src", "tgt", None, None),
            P("src", "tgt"),
        ),
        out_specs=(P(("src", "tgt"), None), P(("tgt", "src"), None), P(), P(), P()),
        check_vma=False,
    )
```

```python
import functools

import jax
import jax.numpy as jnp
from jax import lax
from jax.experimental import pallas as pl
from jax.experimental.pallas import tpu as pltpu
from jax.sharding import PartitionSpec as P

F32 = jnp.float32
BF16 = jnp.bfloat16
MESH = pl.DeviceIdType.MESH
ANY = pl.BlockSpec(memory_space=pl.ANY)
VMEM = pl.BlockSpec(memory_space=pltpu.VMEM)
SMEM = pl.BlockSpec(memory_space=pltpu.SMEM)
DMA = pltpu.SemaphoreType.DMA

WAVE_HALF = (4096, 7168)
HALF_ROWS = sum(WAVE_HALF)
FIRST_TILES = 2 * WAVE_HALF[0] // 16
SECOND_HALF_TILES = WAVE_HALF[1] // 16
W_TILES = 864
PARTS = (
    (("x", "y", "z"), 32),
    (("y", "z", "x"), 32),
    (("z", "x", "y"), 48),
    (("x", "y", "z"), 32),
    (("y", "z", "x"), 32),
)
BASES = (0, 2048, 4096, 7168, 9216)
UNROLL = 32
EDGE = 128
VMEM_BYTES = 63 * 2**20


class Place:
    def __init__(self):
        s, t = lax.axis_index("src"), lax.axis_index("tgt")
        self.x_lo, self.core = s // 8, s % 2
        self.x_hi = t // 4
        self.at = {"x": self.x_hi * 2 + self.x_lo, "y": (s // 2) % 4, "z": t % 4}

    def device(self, at, core):
        return ((at["x"] % 2) * 8 + at["y"] * 2 + core, (at["x"] // 2) * 4 + at["z"])

    def along(self, axis, offset):
        at = dict(self.at)
        at[axis] = (at[axis] + offset) % 4
        return self.device(at, self.core)

    def sibling(self):
        return self.device(self.at, 1 - self.core)

    def x_lo_partner(self):
        at = dict(self.at)
        at["x"] = self.x_hi * 2 + (1 - self.x_lo)
        return self.device(at, self.core)


def greet(partners):
    barrier = pltpu.get_barrier_semaphore()
    for partner in partners:
        pl.semaphore_signal(barrier, inc=1, device_id=partner, device_id_type=MESH)
    pl.semaphore_wait(barrier, len(partners))


def push(src, dst, send, recv, device):
    return pltpu.make_async_remote_copy(
        src_ref=src, dst_ref=dst, send_sem=send, recv_sem=recv, device_id=device, device_id_type=MESH
    )


def gather_kernel(
    h_ref, c_ref, w_hbm, src_ref, tgt_ref, rel_ref, dir_ref, own_c, own_h, loop_ref,
    h_all, c_all, s8, t8, r8, t_out, l_out, w_ref, local, hx_s, hx_r, hz_s, hz_r, cy_s, cy_r, cx_s, cx_r, cs_s, cs_r
):
    me = Place()
    x_lo, x_hi, core, y, z = me.x_lo, me.x_hi, me.core, me.at["y"], me.at["z"]
    sibling, across = me.sibling(), me.x_lo_partner()
    own_h_copy = pltpu.make_async_copy(h_ref, h_all.at[x_hi, z], local.at[0])
    own_c_copy = pltpu.make_async_copy(c_ref, c_all.at[x_lo, y, core], local.at[1])
    w_self = pltpu.make_async_copy(w_hbm.at[2], w_ref, local.at[2])
    w_self.start()
    own_h_copy.start()
    own_c_copy.start()
    s8[...] = src_ref[...] * 8
    t8[...] = (tgt_ref[...] + dir_ref[...] * (16 * c_ref.shape[0])) * 8
    r8[...] = rel_ref[...] * 8
    greet(
        [me.along("x", 2), across, sibling]
        + [me.along("y", k) for k in (1, 2, 3)]
        + [me.along("z", k) for k in (1, 2, 3)]
    )
    mine, theirs = h_all.at[x_hi, z], h_all.at[1 - x_hi, z]
    hx = push(h_ref, mine, hx_s, hx_r, me.along("x", 2))
    hx.start()
    cy, hz = [], []
    for k in (1, 3, 2):
        copy = push(h_ref, mine, hz_s.at[k - 1], hz_r.at[k - 1], me.along("z", k))
        copy.start()
        hz.append(copy)
        copy = push(c_ref, c_all.at[x_lo, y, core], cy_s.at[k - 1], cy_r.at[k - 1], me.along("y", k))
        copy.start()
        cy.append(copy)
    hx.wait()
    for k in (1, 3, 2):
        copy = push(theirs, theirs, hz_s.at[k + 2], hz_r.at[k + 2], me.along("z", k))
        copy.start()
        hz.append(copy)
    own_c_copy.wait()
    for copy in cy:
        copy.wait_recv()
    near = c_all.at[x_lo, :, core]
    far = c_all.at[1 - x_lo, :, core]
    cx = push(near, near, cx_s, cx_r, across)
    cx.start()
    first = push(near, near, cs_s.at[0], cs_r.at[0], sibling)
    first.start()
    w_self.wait()
    back = lax.dot_general(own_c[...], w_ref[...], (((1,), (1,)), ((), ())), preferred_element_type=F32)
    t_out[...] = back * loop_ref[...].astype(F32).reshape(1, back.shape[1])
    l_out[...] = jnp.sum(back * own_h[...].astype(F32), axis=0, keepdims=True)
    cx.wait()
    second = push(far, far, cs_s.at[1], cs_r.at[1], sibling)
    second.start()
    first.wait()
    second.wait()
    own_h_copy.wait()
    for copy in hz:
        copy.wait()
    for copy in cy:
        copy.wait_send()


def gather(h_src, cotangent, weights, h_tgt, loop, *indices):
    rows, width = h_src.shape
    trows = cotangent.shape[0]
    h_all, c_all, s8, t8, r8, grad_tgt, lsum = pl.pallas_call(
        gather_kernel,
        out_shape=(
            jax.ShapeDtypeStruct((2, 4, rows, width), BF16),
            jax.ShapeDtypeStruct((2, 4, 2, trows, width), BF16),
            *[jax.ShapeDtypeStruct(indices[0].shape, jnp.int32)] * 3,
            jax.ShapeDtypeStruct((trows, width), F32),
            jax.ShapeDtypeStruct((1, width), F32),
        ),
        in_specs=[ANY] * 3 + [VMEM] * 7,
        out_specs=[ANY] * 2 + [VMEM] * 5,
        scratch_shapes=[
            pltpu.VMEM((width, width), BF16),
            DMA((3,)), DMA, DMA, DMA((6,)), DMA((6,)), DMA((3,)), DMA((3,)), DMA, DMA, DMA((2,)), DMA((2,)),
        ],
        compiler_params=pltpu.CompilerParams(collective_id=0, has_side_effects=True, vmem_limit_bytes=VMEM_BYTES),
        name="gather_panels",
    )(h_src, cotangent, weights, *indices, cotangent, h_tgt, loop)
    flat = [a.reshape(-1) for a in (s8, t8, r8)]
    return h_all.reshape(8 * rows, width), c_all.reshape(16 * trows, width), *flat, grad_tgt, lsum


def edge_kernel(
    live_ref, src_ref, tgt_ref, rel_ref, h_hbm, c_hbm, w_hbm, z_hbm, lsum,
    g_out, hi_out, lo_out, rest_out, keep_out, give_out,
    h_ref, c_ref, w_ref, z_ref, g_ref, keep, give, hx, px, zx, gs, aa, rr, hi, lo, in_sem, out_sem,
):
    loads = [
        pltpu.make_async_copy(a, b, in_sem.at[i])
        for i, (a, b) in enumerate(((h_hbm, h_ref), (z_hbm, z_ref), (c_hbm, c_ref), (w_hbm.at[pl.ds(0, 2)], w_ref)))
    ]
    for load in loads:
        load.start()
    core = lax.axis_index("src") % 2
    rows = h_ref.shape[0]
    trows = c_ref.shape[0]
    rels, width = z_ref.shape
    chunks = width // 128

    def spread(dst, row, value):
        for c in range(chunks):
            dst[pl.ds(row * 8 + c, value.shape[0], stride=8), :] = value[:, c * 128 : (c + 1) * 128]

    zero = jnp.zeros((64, 128), F32)
    for ref in (gs, aa, rr):

        @pl.loop(0, ref.shape[0] // 64)
        def _(i, ref=ref):
            ref[pl.ds(pl.multiple_of(i * 64, 64), 64), :] = zero

    loads[0].wait()

    @pl.loop(0, rows // 16)
    def _(i):
        r = pl.multiple_of(i * 16, 16)
        spread(hx, r, h_ref[pl.ds(r, 16), :].astype(F32))

    loads[1].wait()

    @pl.loop(0, rels // 16)
    def _(i):
        r = pl.multiple_of(i * 16, 16)
        spread(zx, r, z_ref[pl.ds(r, 16), :].astype(F32))

    tail = rels // 16 * 16
    if tail < rels:
        spread(zx, tail, z_ref[tail:rels, :].astype(F32))
    loads[2].wait()
    loads[3].wait()
    for d in range(2):
        for k in range(width // 256):
            p = lax.dot_general(
                c_ref[...], w_ref[d, k * 256 : (k + 1) * 256, :], (((1,), (1,)), ((), ())),
                preferred_element_type=F32,
            )
            for h in range(2):
                px[pl.ds(d * trows * 8 + 2 * k + h, trows, stride=8), :] = p[:, h * 128 : (h + 1) * 128]
    def row(at):
        return pl.ds(pl.multiple_of(at, 8), 8)

    @pl.loop(0, live_ref[0] * (EDGE // UNROLL))
    def _(i):
        start = i * UNROLL
        for u in range(0, UNROLL, 2):
            s0, s1 = src_ref[start + u], src_ref[start + u + 1]
            t0, t1 = tgt_ref[start + u], tgt_ref[start + u + 1]
            r0, r1 = rel_ref[start + u], rel_ref[start + u + 1]
            h0, h1 = hx[row(s0), :], hx[row(s1), :]
            p0, p1 = px[row(t0), :], px[row(t1), :]
            z0, z1 = zx[row(r0), :], zx[row(r1), :]
            for ref, at0, at1, v0, v1 in (
                (gs, s0, s1, p0 * z0, p1 * z1),
                (aa, t0, t1, (h0 * z0).astype(BF16).astype(F32), (h1 * z1).astype(BF16).astype(F32)),
                (rr, r0, r1, p0 * h0, p1 * h1),
            ):
                sum0 = ref[row(at0), :] + v0
                sum1 = ref[row(at1), :] + v1 + jnp.where(at0 == at1, v0, jnp.zeros_like(v0))
                ref[row(at0), :] = sum0
                ref[row(at1), :] = sum1

    for c in range(chunks):
        rr[rels * 8 + c : rels * 8 + c + 1, :] = lsum[:, c * 128 : (c + 1) * 128]
    blocks = rr.shape[0] // 128

    def rel_tile(block, c):
        return rr[pl.ds(block * 128 + c, 16, stride=8), :]

    def collect(half, ref):
        first = half * (FIRST_TILES // 2)
        last = first + FIRST_TILES // 2

        @pl.loop(-(-first // chunks), last // chunks)
        def _(i):
            for c in range(chunks):
                row = pl.multiple_of((i * chunks + c - first) * 16, 16)
                ref[pl.ds(row, 16), :] = rel_tile(i, c).astype(ref.dtype)

        edge_tiles = [*range(first, -(-first // chunks) * chunks), *range(last // chunks * chunks, last)]
        for t in edge_tiles:
            row = (t - first) * 16
            ref[row : row + 16, :] = rel_tile(t // chunks, t % chunks).astype(ref.dtype)

    @pl.when(core == 0)
    def _():
        collect(0, keep)
        collect(1, give)

    @pl.when(core != 0)
    def _():
        collect(1, keep)
        collect(0, give)

    stores = [
        pltpu.make_async_copy(keep, keep_out, out_sem.at[0]),
        pltpu.make_async_copy(give, give_out, out_sem.at[1]),
    ]
    for store in stores:
        store.start()
    for t in range(FIRST_TILES, blocks * chunks):
        row = (t - FIRST_TILES) * 16
        rest_out[row : row + 16, :] = rel_tile(t // chunks, t % chunks)

    @pl.loop(0, 2 * trows // 16)
    def _(i):
        r = pl.multiple_of(i * 16, 16)
        for c in range(chunks):
            a = aa[pl.ds(r * 8 + c, 16, stride=8), :]
            top = a.astype(BF16)
            hi[pl.ds(r, 16), c * 128 : (c + 1) * 128] = top
            lo[pl.ds(r, 16), c * 128 : (c + 1) * 128] = (a - top.astype(F32)).astype(BF16)

    stores.append(pltpu.make_async_copy(hi, hi_out, out_sem.at[2]))
    stores.append(pltpu.make_async_copy(lo, lo_out, out_sem.at[3]))
    stores[2].start()
    stores[3].start()

    @pl.loop(0, rows // 16)
    def _(i):
        r = pl.multiple_of(i * 16, 16)
        for c in range(chunks):
            g_ref[pl.ds(r, 16), c * 128 : (c + 1) * 128] = gs[pl.ds(r * 8 + c, 16, stride=8), :].astype(BF16)

    stores.append(pltpu.make_async_copy(g_ref, g_out, out_sem.at[4]))
    stores[4].start()
    for store in stores:
        store.wait()


def edges(live, s8, t8, r8, h, c, w, z, lsum):
    rows, width = h.shape
    trows = c.shape[0]
    rpad = (z.shape[0] + 16) // 16 * 16
    return pl.pallas_call(
        edge_kernel,
        out_shape=(
            jax.ShapeDtypeStruct((rows, width), BF16),
            jax.ShapeDtypeStruct((2 * trows, width), BF16),
            jax.ShapeDtypeStruct((2 * trows, width), BF16),
            jax.ShapeDtypeStruct((rpad // 16 * (width // 128) * 16 - FIRST_TILES * 16, 128), F32),
            jax.ShapeDtypeStruct((WAVE_HALF[0], 128), F32),
            jax.ShapeDtypeStruct((WAVE_HALF[0], 128), F32),
        ),
        in_specs=[SMEM] * 4 + [ANY] * 4 + [VMEM],
        out_specs=[ANY, ANY, ANY, VMEM, ANY, ANY],
        scratch_shapes=[
            pltpu.VMEM(h.shape, BF16),
            pltpu.VMEM(c.shape, BF16),
            pltpu.VMEM((2, width, width), BF16),
            pltpu.VMEM(z.shape, BF16),
            pltpu.VMEM((rows, width), BF16),
            pltpu.VMEM((WAVE_HALF[0], 128), F32),
            pltpu.VMEM((WAVE_HALF[0], 128), F32),
            pltpu.VMEM((rows * 8, 128), F32),
            pltpu.VMEM((2 * trows * 8, 128), F32),
            pltpu.VMEM((rpad * 8, 128), F32),
            pltpu.VMEM((rows * 8, 128), F32),
            pltpu.VMEM((2 * trows * 8, 128), F32),
            pltpu.VMEM((rpad * 8, 128), F32),
            pltpu.VMEM((2 * trows, width), BF16),
            pltpu.VMEM((2 * trows, width), BF16),
            DMA((4,)),
            DMA((5,)),
        ],
        compiler_params=pltpu.CompilerParams(vmem_limit_bytes=VMEM_BYTES),
        name="edges",
    )(live, s8, t8, r8, h, c, w, z, lsum)


def reduce_kernel(
    keep_hbm, give, g_ref, hi_hbm, lo_hbm, c_hbm, rest, own_c, own_h, loop_ref, full, g_out,
    keep, given, hi, lo, c_all, g_own, pair, out1, in1, acc1, out2, in2, unit, g_in, g_acc, g_send, g_side,
    pair_s, pair_r, s1, r1, s2, r2, s4, r4, s6, r6, sib_s, sib_r, gz_s, gz_r, gx_s, gx_r,
    local, kept,
):
    me = Place()
    core = me.core
    sibling = me.sibling()
    x_hi, z = me.x_hi, me.at["z"]
    width = c_all.shape[1]
    trows = c_all.shape[0]
    chunks = width // 128
    parts = range(len(PARTS))

    def at(p, depth):
        return me.at[PARTS[p][0][depth]]

    def along(p, depth, j):
        return me.along(PARTS[p][0][depth], j)

    def in_plane(p, j, k):
        where = dict(me.at)
        where[PARTS[p][0][1]] = (at(p, 1) + j) % 4
        where[PARTS[p][0][2]] = (at(p, 2) + k) % 4
        return me.device(where, core)

    others = [(2, 2), (2, 1), (2, 3), (1, 2), (3, 2), (1, 1), (1, 3), (3, 1), (3, 3)]
    others += [(2, 0), (0, 2), (1, 0), (3, 0), (0, 1), (0, 3)]

    def rows_of(p, a):
        size = PARTS[p][1] * 16
        return pl.ds(pl.multiple_of(BASES[p] + a * size, 16), size)

    first_rows = pl.ds(0, WAVE_HALF[0])
    loads = [
        pltpu.make_async_copy(a, b, kept.at[n])
        for n, (a, b) in enumerate(
            (
                (keep_hbm, keep.at[first_rows]),
                (hi_hbm, hi),
                (c_hbm, c_all),
                (lo_hbm, lo),
                (g_ref.at[:, z], g_own),
            )
        )
    ]
    for load in loads:
        load.start()
    plane = [me.along(axis, k) for axis in ("x", "y", "z") for k in (1, 2, 3)]
    for p in (0, 1, 2):
        plane += [in_plane(p, j, k) for j, k in others[:9]]
    greet(plane[::-1] + [sibling])

    pairs, step1, step6, side, own = {}, {}, {}, {}, {}

    def send_pair(some):
        for j in (1, 2, 3, 0):
            for p in some:
                where = rows_of(p, (at(p, 0) + j) % 4)
                if BASES[p] < WAVE_HALF[0]:
                    source = give.at[where]
                else:
                    row = BASES[p] - WAVE_HALF[0] + ((at(p, 0) + j) % 4) * (PARTS[p][1] * 16)
                    source = given.at[pl.ds(pl.multiple_of(row, 16), PARTS[p][1] * 16)]
                copy = push(source, pair.at[where], pair_s.at[p * 4 + j], pair_r.at[p * 4 + j], sibling)
                copy.start()
                pairs[p, j] = copy

    def send_first(some):
        for j in (1, 2, 3):
            for p in some:
                size = PARTS[p][1] * 16
                base = BASES[p] + ((at(p, 0) + j) % 4) * size
                pairs[p, j].wait_recv()

                @pl.loop(0, size // 128)
                def _(i, base=base):
                    r = pl.ds(pl.multiple_of(base + i * 128, 16), 128)
                    out1[r, :] = (keep[r, :] + pair[r, :]).astype(BF16)

                copy = push(
                    out1.at[rows_of(p, (at(p, 0) + j) % 4)],
                    in1.at[j - 1, pl.ds(BASES[p] // 4, size)],
                    s1.at[p * 3 + j - 1],
                    r1.at[p * 3 + j - 1],
                    along(p, 0, j),
                )
                copy.start()
                step1[p, j] = copy

    def send_second(p):
        size = PARTS[p][1]
        base = BASES[p] + at(p, 0) * (size * 16)
        low = BASES[p] // 4
        pairs[p, 0].wait_recv()
        for j in (1, 2, 3):
            step1[p, j].wait_recv()

        @pl.loop(0, size * 16 // 128)
        def _(i):
            r = pl.ds(pl.multiple_of(base + i * 128, 16), 128)
            q = pl.ds(pl.multiple_of(low + i * 128, 16), 128)
            total = (
                keep[r, :]
                + pair[r, :]
                + in1[0, q, :].astype(F32)
                + in1[1, q, :].astype(F32)
                + in1[2, q, :].astype(F32)
            )
            acc1[q, :] = total
            out2[q, :] = total.astype(BF16)

        for j, k in others:
            row = low + (((at(p, 1) + j) % 4) * 4 + (at(p, 2) + k) % 4) * size
            push(
                out2.at[pl.ds(pl.multiple_of(row, 16), size)],
                in2.at[j * 4 + k - 1, pl.ds(BASES[p] // 64, size)],
                s2.at[p],
                r2.at[p],
                in_plane(p, j, k),
            ).start()

    def second(p):
        mine = out2.at[pl.ds(BASES[p] // 4, PARTS[p][1] * 15)]
        return push(mine, in2.at[:, pl.ds(BASES[p] // 64, PARTS[p][1])], s2.at[p], r2.at[p], in_plane(p, 1, 1))

    def start_of(p):
        if BASES[p] < WAVE_HALF[0]:
            return core * WAVE_HALF[0] + BASES[p]
        return 2 * WAVE_HALF[0] + core * WAVE_HALF[1] + (BASES[p] - WAVE_HALF[0])

    def place(p, depth):
        size = PARTS[p][1]
        row = start_of(p) + at(p, 0) * (size * 16)
        if depth > 1:
            row = row + at(p, 1) * (size * 4)
        if depth > 2:
            row = row + at(p, 2) * size
        return full.at[pl.ds(pl.multiple_of(row, 16), (size * 16, size * 4, size)[depth - 1])]

    def half_of(p, offset, half):
        size = PARTS[p][1] * 8
        row = start_of(p) + ((at(p, 0) + 4 + offset) % 4) * (2 * size) + half * size
        return full.at[pl.ds(pl.multiple_of(row, 16), size)]

    def share_second(p):
        size = PARTS[p][1]
        second(p).wait_recv()
        q = pl.ds(BASES[p] // 64, size)
        mine = pl.ds(pl.multiple_of(BASES[p] // 4 + (at(p, 1) * 4 + at(p, 2)) * size, 16), size)
        total = acc1[mine, :]
        for n in range(15):
            total = total + in2[n, q, :].astype(F32)
        unit[q, :] = total.astype(BF16)
        for j, k in others:
            push(unit.at[q], place(p, 3), s4.at[p], r4.at[p], in_plane(p, j, k)).start()
        own[p] = pltpu.make_async_copy(unit.at[q], place(p, 3), local.at[p])
        own[p].start()

    def shared(p):
        where = pl.ds(pl.multiple_of(start_of(p) + at(p, 0) * (PARTS[p][1] * 16), 16), PARTS[p][1] * 15)
        return push(full.at[where], full.at[where], s4.at[p], r4.at[p], in_plane(p, 1, 1))

    def to_other_core(p, n, block):
        side[p, n] = push(block, block, sib_s.at[p * 7 + n], sib_r.at[p * 7 + n], sibling)
        side[p, n].start()

    def share_first(p):
        own[p].wait()
        shared(p).wait_recv()
        for n, (to, half) in enumerate(((1, 0), (3, 1), (1, 1), (3, 0))):
            block = half_of(p, 0, half)
            copy = push(block, block, s6.at[p * 6 + n], r6.at[p * 6 + n], along(p, 0, to))
            copy.start()
            step6[p, n] = copy
        to_other_core(p, 0, place(p, 1))

    def forward(p):
        for n, (to, half) in enumerate(((1, 0), (3, 1))):
            step6[p, n].wait_recv()
            block = half_of(p, -to, half)
            copy = push(block, block, s6.at[p * 6 + 4 + n], r6.at[p * 6 + 4 + n], along(p, 0, to))
            copy.start()
            step6[p, 4 + n] = copy
            to_other_core(p, 1 + n, block)

    def finish(p):
        for n, (to, half) in enumerate(((1, 1), (3, 0))):
            step6[p, 2 + n].wait_recv()
            to_other_core(p, 3 + n, half_of(p, -to, half))
        for half in range(2):
            step6[p, 4 + half].wait_recv()
            to_other_core(p, 5 + half, half_of(p, 2, half))

    def put(first, value):
        here = value.shape[0] // 16 * chunks
        for half in range(2):
            begin = max(first, half * SECOND_HALF_TILES)
            end = min(first + here, (half + 1) * SECOND_HALF_TILES)
            if begin >= end:
                continue

            def store(ref, base, half=half, begin=begin, end=end):
                for t in range(begin, end):
                    row = base + (t - half * SECOND_HALF_TILES) * 16
                    b, c = (t - first) // chunks, (t - first) % chunks
                    ref[row : row + 16, :] = value[b * 16 : b * 16 + 16, c * 128 : c * 128 + 128].astype(ref.dtype)

            @pl.when(core == half)
            def _(store=store):
                store(keep, WAVE_HALF[0])

            @pl.when(core != half)
            def _(store=store):
                store(given, 0)

    def make_wsum(d):
        rows = slice(d * trows, (d + 1) * trows)
        for k in range(width // 256):
            cols = slice(k * 256, (k + 1) * 256)
            w = lax.dot_general(
                hi[rows, cols], c_all[...], (((0,), (0,)), ((), ())), preferred_element_type=F32
            ) + lax.dot_general(
                lo[rows, cols], c_all[...], (((0,), (0,)), ((), ())), preferred_element_type=F32
            )
            put((d * 48 + k * 16) * chunks, w)

    def make_wself():
        self_comp = (own_h[...].astype(F32) * loop_ref[...].astype(F32).reshape(1, width)).astype(BF16)
        for k in range(width // 256):
            w = lax.dot_general(
                self_comp[:, k * 256 : (k + 1) * 256], own_c[...], (((0,), (0,)), ((), ())),
                preferred_element_type=F32,
            )
            put((96 + k * 16) * chunks, w)
        low = (W_TILES - SECOND_HALF_TILES) * 16
        n = rest.shape[0]

        def store(ref, base):
            ref[base + low : base + low + n, :] = rest[...].astype(ref.dtype)
            ref[base + low + n : base + WAVE_HALF[1], :] = jnp.zeros((WAVE_HALF[1] - low - n, 128), ref.dtype)

        @pl.when(core == 1)
        def _():
            store(keep, WAVE_HALF[0])

        @pl.when(core != 1)
        def _():
            store(given, 0)

    gz = []
    for k in (1, 3, 2):
        copy = push(g_ref.at[:, (z + k) % 4], g_in.at[k - 1], gz_s.at[k - 1], gz_r.at[k - 1], me.along("z", k))
        copy.start()
        gz.append(copy)
    send_pair((0, 1))
    loads[0].wait()
    for load in loads[1:]:
        load.wait()
    make_wsum(0)
    make_wsum(1)
    make_wself()
    send_pair((2, 3, 4))
    send_first((0, 1, 2, 3, 4))
    send_second(0)
    send_second(1)
    send_second(2)
    send_second(3)
    send_second(4)
    share_second(0)
    share_second(1)
    share_second(2)
    share_second(3)
    share_second(4)
    for copy in gz:
        copy.wait_recv()
    for half in range(2):
        g_acc[half] = (
            g_own[half].astype(F32)
            + g_in[0, half].astype(F32)
            + g_in[1, half].astype(F32)
            + g_in[2, half].astype(F32)
        )
    g_send[...] = g_acc[1 - x_hi].astype(BF16)
    gx = push(g_send, g_side, gx_s, gx_r, me.along("x", 2))
    gx.start()
    share_first(0)
    share_first(1)
    share_first(2)
    share_first(3)
    share_first(4)
    forward(0)
    forward(1)
    forward(2)
    forward(3)
    forward(4)
    finish(0)
    finish(1)
    gx.wait_recv()
    g_out[...] = g_acc[x_hi] + g_side[...].astype(F32)
    finish(2)
    finish(3)
    finish(4)
    for copy in side.values():
        copy.wait_recv()
    gx.wait_send()
    for copy in gz:
        copy.wait_send()
    for group in (pairs, step1, step6, side):
        for copy in group.values():
            copy.wait_send()
    for p in parts:
        second(p).wait_send()
        shared(p).wait_send()


def reduce_all(keep, give, g, hi, lo, c_all, rest, own_c, own_h, loop):
    rows, width = g.shape
    g = g.reshape(2, 4, rows // 8, width)
    n = len(PARTS)
    return pl.pallas_call(
        reduce_kernel,
        out_shape=(
            jax.ShapeDtypeStruct((2 * HALF_ROWS, 128), BF16),
            jax.ShapeDtypeStruct((rows // 8, width), F32),
        ),
        in_specs=[ANY] * 6 + [VMEM] * 4,
        out_specs=[ANY, VMEM],
        scratch_shapes=[
            pltpu.VMEM((HALF_ROWS, 128), F32),
            pltpu.VMEM((WAVE_HALF[1], 128), F32),
            pltpu.VMEM(hi.shape, BF16),
            pltpu.VMEM(lo.shape, BF16),
            pltpu.VMEM(c_all.shape, BF16),
            pltpu.VMEM((2, rows // 8, width), BF16),
            pltpu.VMEM((HALF_ROWS, 128), F32),
            pltpu.VMEM((HALF_ROWS, 128), BF16),
            pltpu.VMEM((3, HALF_ROWS // 4, 128), BF16),
            pltpu.VMEM((HALF_ROWS // 4, 128), F32),
            pltpu.VMEM((HALF_ROWS // 4, 128), BF16),
            pltpu.VMEM((15, HALF_ROWS // 64, 128), BF16),
            pltpu.VMEM((HALF_ROWS // 64, 128), BF16),
            pltpu.VMEM((3, 2, rows // 8, width), BF16),
            pltpu.VMEM((2, rows // 8, width), F32),
            pltpu.VMEM((rows // 8, width), BF16),
            pltpu.VMEM((rows // 8, width), BF16),
            *[DMA((4 * n,))] * 2, *[DMA((3 * n,))] * 2, *[DMA((n,))] * 4, *[DMA((6 * n,))] * 2, *[DMA((7 * n,))] * 2,
            DMA((3,)), DMA((3,)), DMA, DMA, DMA((n,)), DMA((5,)),
        ],
        compiler_params=pltpu.CompilerParams(
            collective_id=1, has_side_effects=True, vmem_limit_bytes=VMEM_BYTES
        ),
        name="reduce_all",
    )(keep, give, g, hi, lo, c_all, rest, own_c, own_h, loop)


REL_BLOCK = 18


def unpack_kernel(
    full_hbm, gs_in, gt_in, w_hbm, r_out, l_out, gs_out, gt_out, full, w_out, gs, gt, in_sem, out_sem,
    *, rels, edge_scale, self_scale, rel_scale,
):
    step = pl.program_id(0)
    last_step = -(-(rels + 1) // (REL_BLOCK * 16)) - 1
    width = r_out.shape[1]
    chunks = width // 128
    per = width // 16
    group = per // 3
    pieces = in_sem.shape[0] - 2
    size = full.shape[0] // pieces

    def load(i):
        if i >= pieces:
            source, target = ((gs_in, gs), (gt_in, gt))[i - pieces]
            return pltpu.make_async_copy(source, target, in_sem.at[i])
        where = pl.ds(i * size, size)
        return pltpu.make_async_copy(full_hbm.at[where], full.at[where], in_sem.at[i])

    def store(n):
        if n < 9:
            where = pl.ds(n % 3 * group * 16, group * 16)
            return pltpu.make_async_copy(w_out.at[n // 3, where], w_hbm.at[n // 3, where], out_sem.at[n])
        source, target = ((gs, gs_out), (gt, gt_out))[n - 9]
        return pltpu.make_async_copy(source, target, out_sem.at[n])

    def tile(first, index):
        return full[pl.ds(pl.multiple_of(first + index * 16, 16), 16), :].astype(F32)

    w_first = 2 * WAVE_HALF[0]
    rest_first = w_first + W_TILES * 16

    @pl.when(step == 0)
    def _():
        order = [*range(w_first // size, pieces), *range(w_first // size), pieces, pieces + 1]
        for i in order:
            load(i).start()
        waited = 0
        for n in range(9):
            end = w_first + (n + 1) * group * chunks * 16
            while order[waited] * size < end and waited < pieces - w_first // size:
                load(order[waited]).wait()
                waited += 1
            d, scale = n // 3, (edge_scale, edge_scale, self_scale)[n // 3]

            @pl.loop(n % 3 * group, (n % 3 + 1) * group)
            def _(i, d=d, scale=scale):
                for c in range(chunks):
                    w_out[d, pl.ds(pl.multiple_of(i * 16, 16), 16), c * 128 : (c + 1) * 128] = (
                        tile(w_first, (d * per + i) * chunks + c) * scale
                    )

            store(n).start()
        for i in order[waited:]:
            load(i).wait()
        store(9).start()
        store(10).start()

    @pl.when(step != last_step)
    def _():
        @pl.loop(0, REL_BLOCK)
        def _(i):
            for c in range(chunks):
                r_out[pl.ds(pl.multiple_of(i * 16, 16), 16), c * 128 : (c + 1) * 128] = (
                    tile(0, (step * REL_BLOCK + i) * chunks + c) * rel_scale
                )

    @pl.when(step == last_step)
    def _():
        first = last_step * REL_BLOCK
        for t in range(first * chunks, -(-(rels + 1) // 16) * chunks):
            b, cols = t // chunks, slice(t % chunks * 128, t % chunks * 128 + 128)
            value = tile(0, t) if t < FIRST_TILES else tile(rest_first, t - FIRST_TILES)
            r_out[(b - first) * 16 : (b - first) * 16 + 16, cols] = value * rel_scale
            n = rels - b * 16
            if n < 16:
                l_out[cols] = (value[n : n + 1] * self_scale).reshape(128)
        for n in range(11):
            store(n).wait()


def unpack(full, grad_src, grad_tgt, rels, width, **scales):
    rows = REL_BLOCK * 16
    return pl.pallas_call(
        functools.partial(unpack_kernel, rels=rels, **scales),
        grid=(-(-(rels + 1) // rows),),
        out_shape=(
            jax.ShapeDtypeStruct((3, width, width), F32),
            jax.ShapeDtypeStruct((rels, width), F32),
            jax.ShapeDtypeStruct((width,), F32),
            jax.ShapeDtypeStruct(grad_src.shape, F32),
            jax.ShapeDtypeStruct(grad_tgt.shape, F32),
        ),
        in_specs=[ANY] * 3,
        out_specs=[
            ANY,
            pl.BlockSpec((rows, width), lambda i: (i, 0)),
            pl.BlockSpec((width,), lambda i: (0,)),
            ANY,
            ANY,
        ],
        scratch_shapes=[
            pltpu.VMEM(full.shape, BF16),
            pltpu.VMEM((3, width, width), F32),
            pltpu.VMEM(grad_src.shape, F32),
            pltpu.VMEM(grad_tgt.shape, F32),
            DMA((13,)),
            DMA((11,)),
        ],
        compiler_params=pltpu.CompilerParams(vmem_limit_bytes=VMEM_BYTES),
        name="unpack",
    )(full, grad_src, grad_tgt)


def body(
    h_src, rel_table, cotangent, h_tgt, loop_rel, weights, src_index, tgt_index, rel_ids, direction, counts
):
    width = weights.shape[1]
    tiles, edge = src_index.shape[2:]
    rels = rel_table.shape[0]
    h_all, c_all, s8, t8, r8, back, lsum = gather(
        h_src, cotangent, weights, h_tgt, loop_rel, *[a.reshape(tiles, edge) for a in (src_index, tgt_index, rel_ids, direction)]
    )
    g, hi, lo, rest, keep, give = edges(
        counts.reshape(1), s8, t8, r8, h_all, c_all, weights, rel_table, lsum
    )
    full, mine = reduce_all(
        keep, give, g, hi, lo, c_all, rest, cotangent, h_tgt, loop_rel
    )
    devices = lax.axis_size("src") * lax.axis_size("tgt")
    edges_all = float(devices * tiles * edge)
    targets_all = float(devices * cotangent.shape[0])
    grad_weights, grad_rel, grad_loop, grad_src, grad_tgt = unpack(
        full,
        mine,
        back,
        rels,
        width,
        edge_scale=edges_all**-0.5,
        self_scale=targets_all**-0.5,
        rel_scale=(float(rels) / edges_all) ** 0.5,
    )
    return grad_src, grad_tgt, grad_weights, grad_rel, grad_loop


def solution(mesh):
    return jax.shard_map(
        body,
        mesh=mesh,
        in_specs=(
            P(("src", "tgt"), None),
            P(),
            P(("tgt", "src"), None),
            P(("tgt", "src"), None),
            P(),
            P(),
            P("src", "tgt", None, None),
            P("src", "tgt", None, None),
            P("src", "tgt", None, None),
            P("src", "tgt", None, None),
            P("src", "tgt"),
        ),
        out_specs=(P(("src", "tgt"), None), P(("tgt", "src"), None), P(), P(), P()),
        check_vma=False,
    )
```
